32 devices in a mesh: grp: 4 (over y, x), dp: 2 (over core), mp: 4 (over z).
Axes of the slice: x: 2, y: 2, z: 4, core: 2. Of those that a mesh axis runs over, the one named last changes fastest.
Arguments:
- tokens: bfloat16 [4, 2048, 768], P('grp', ('dp', 'mp')), may hold values from -6 to 6
- cotangent: bfloat16 [4, 2048, 768], P('grp', ('dp', 'mp')), may hold values from -6 to 6
- modulation: float32 [4, 8, 9216], P('grp', 'dp'), may hold values from -3 to 3
- clip_frames: int32 [4, 8], P('grp', 'dp'), may hold values from 1 to 64, as said below
- clip_patches: int32 [4, 8], P('grp', 'dp'), may hold values from 1 to 21, as said below
- params: float32 [2, 768, 9216], P(None, 'dp', 'mp')
- first_moment: float32 [4, 2, 768, 9216], P('grp', None, 'dp', 'mp'), may hold values from -5 to 5
- second_moment: float32 [4, 2, 768, 9216], P('grp', None, 'dp', 'mp'), may hold values from 0.02048 to 0.2048
- outer_momentum: float32 [2, 768, 9216], P(None, 'dp', 'mp'), may hold values from -0.21875 to 0.21875
Outputs:
- mixed: bfloat16 [4, 2048, 768], P('grp', ('dp', 'mp'))
- input_grad: float32 [4, 2048, 768], P('grp', ('dp', 'mp'))
- first_moment_new: float32 [4, 2, 768, 9216], P('grp', None, 'dp', 'mp')
- second_moment_new: float32 [4, 2, 768, 9216], P('grp', None, 'dp', 'mp')
- outer_delta: float32 [2, 768, 9216], P(None, 'dp', 'mp')
- outer_momentum_new: float32 [2, 768, 9216], P(None, 'dp', 'mp')
- new_weights: float32 [2, 768, 9216], P(None, 'dp', 'mp')
- new_weights_low: bfloat16 [2, 768, 9216], P(None, 'dp', 'mp')
The draws below stay inside these ranges and needn't reach their ends.
Inputs may be any that keep to these rules, and one draw needn't show every extreme that they name: `clip_frames`: in each segment exactly one clip has 64 frames, the others at most 8; the clips of a segment fill at most 1024 rows. `clip_patches`: the clip with 64 frames has 4 to 8 patches a frame, the others 21 // 2 to 21.
All inputs are finite; a program needn't handle non-finite values.
Results may differ from the reference program's by a relative error of at most 0.02.
Values may be sent and summed in bfloat16 or wider, within the bound.
A program may use at most 192 MiB of HBM per device.

```python
import math
from functools import partial
import jax
import jax.numpy as jnp
from jax import lax

D = 768
HEADS = 12
HD = 64
FF = 3072
L = 2
STEP = 5
CAP = 1024
SLOTS = 4
LONGF = 64
SHORTF = 8
GROUPS = 4
HEADS_DEV = 3
FF_DEV = 768
COLS = 9216
WB = 2304
LONGP = 8
SHORTP = 21
N_DP = 2
N_MP = 4


def clip_plan(key):
    key_long, key_frames, key_patches, key_place = jax.random.split(key, 4)
    long_patches = jax.random.randint(key_long, (GROUPS, N_DP, 1), max(LONGP // 2, 1), LONGP + 1)
    short_frames = jax.random.randint(key_frames, (GROUPS, N_DP, SLOTS - 1), 1, SHORTF + 1)
    short_patches = jax.random.randint(key_patches, (GROUPS, N_DP, SLOTS - 1), max(SHORTP // 2, 1), SHORTP + 1)
    long_place = jax.random.randint(key_place, (GROUPS, N_DP, 1), 0, SLOTS)
    slot_index = jnp.arange(SLOTS, dtype=jnp.int32)[None, None, :]
    pick_index = jnp.clip(slot_index - (slot_index > long_place).astype(jnp.int32), 0, SLOTS - 2)
    pick_index = jnp.broadcast_to(pick_index, (GROUPS, N_DP, SLOTS))
    frames = jnp.where(slot_index == long_place, LONGF, jnp.take_along_axis(short_frames, pick_index, axis=2))
    patches = jnp.where(slot_index == long_place, long_patches, jnp.take_along_axis(short_patches, pick_index, axis=2))
    return (frames.reshape(GROUPS, N_DP * SLOTS).astype(jnp.int32), patches.reshape(GROUPS, N_DP * SLOTS).astype(jnp.int32))


def draw_clip_frames(key, part):
    frames, patches = clip_plan(key)
    return frames


def draw_clip_patches(key, part):
    frames, patches = clip_plan(key)
    return patches


def draw_params(key, part):
    key = jax.random.fold_in(key, 7)
    head_width = HEADS_DEV * HD
    column = jnp.arange(COLS, dtype=jnp.int32) % WB
    column_scale = jnp.where(column < 3 * head_width, D ** (-0.5), jnp.where(column < 4 * head_width, 4.0 * D ** (-0.5), jnp.where(column < 4 * head_width + FF_DEV, D ** (-0.5), 1.5 * FF ** (-0.5))))
    base = jax.random.normal(key, (L, D, COLS), jnp.float32)
    return (base * column_scale[None, None, :]).astype(jnp.float32)


def shard_levels(stream_key, dims, cuts, low, top_value):
    gain, own = 1.0, jax.random.fold_in(stream_key, 6)
    for dim, parts in cuts:
        steps = jnp.exp(jax.random.uniform(jax.random.fold_in(own, dim), (parts,), jnp.float32, low / len(cuts), top_value / len(cuts)))
        gain = gain * jnp.repeat(steps, dims[dim] // parts).reshape([-1 if axis == dim else 1 for axis in range(len(dims))])
    return gain


def normal_values(own_key, extent, width, reach, cuts=(), held_as=jnp.bfloat16):
    array = width * jax.random.normal(own_key, extent, jnp.float32)
    if cuts:
        array = array * shard_levels(own_key, extent, cuts, -0.22, 0.18)
    return jnp.clip(array, -reach, reach).astype(held_as)


def setup_inputs(seed: int = 0) -> dict:
    streams_of = jax.random.split(jax.random.key(seed), 10)
    return {
        "tokens": normal_values(streams_of[0], (GROUPS, N_DP * CAP, D), 1.0, 6.0, ((0, 4), (1, 8))),
        "cotangent": normal_values(streams_of[1], (GROUPS, N_DP * CAP, D), 1.0, 6.0, ((0, 4), (1, 8))),
        "modulation": normal_values(streams_of[2], (GROUPS, N_DP * SLOTS, L * 6 * D), 0.5, 3.0, ((0, 4), (1, 2)), jnp.float32),
        "clip_frames": draw_clip_frames(jax.random.fold_in(streams_of[9], 71), 0),
        "clip_patches": draw_clip_patches(jax.random.fold_in(streams_of[9], 71), 0),
        "params": draw_params(jax.random.fold_in(streams_of[9], 71), 0),
        "first_moment": normal_values(streams_of[6], (GROUPS, L, D, COLS), (0.012 * (N_DP * CAP) ** 0.5), 5.0, ((0, 4), (2, 2), (3, 4)), jnp.float32),
        "second_moment": jnp.clip(jnp.exp(math.log(0.2048) - 2.3025851 * jax.random.uniform(streams_of[7], (GROUPS, L, D, COLS), jnp.float32) ** shard_levels(streams_of[7], (GROUPS, L, D, COLS), ((0, 4), (2, 2), (3, 4)), -0.2, 0.2)), 0.02048, 0.2048),
        "outer_momentum": normal_values(streams_of[8], (L, D, COLS), 0.015, 0.21875, ((1, 2), (2, 4)), jnp.float32),
    }


@jax.custom_vjp
def low(v):
    return lax.optimization_barrier(v.astype(jnp.bfloat16)).astype(jnp.float32)

@jax.custom_vjp
def low_back(v):
    return v

def low_keep(v):
    return (low(v), None)

def low_pass(kept, grad):
    return (grad,)

def back_keep(v):
    return (v, None)

def back_low(kept, grad):
    return (low(grad),)
low.defvjp(low_keep, low_pass)
low_back.defvjp(back_keep, back_low)
highest = lax.Precision.HIGHEST
ln_eps = 1e-06
neg_fill = -1e+30
beta_one = 0.9
beta_two = 0.999
adam_eps = 1e-08
inner_rate = 0.04
decay_rate = 0.1
outer_rate = 0.7
outer_mu = 0.5

def clip_meta(frames, patches):
    clip_sizes = (frames * patches).astype(jnp.int32)
    clip_ends = jnp.cumsum(clip_sizes).astype(jnp.int32)
    clip_starts = (clip_ends - clip_sizes).astype(jnp.int32)
    position = jnp.arange(CAP, dtype=jnp.int32)
    clip_index = lax.optimization_barrier(jnp.sum((position[:, None] >= clip_ends[None, :]).astype(jnp.int32), axis=1)).astype(jnp.int32)
    onehot_int = (clip_index[:, None] == jnp.arange(SLOTS, dtype=jnp.int32)[None, :]).astype(jnp.int32)
    live_mask = clip_index < SLOTS
    clip_begin = lax.optimization_barrier(jnp.sum(onehot_int * clip_starts[None, :], axis=1)).astype(jnp.int32)
    frame_width = jnp.maximum(lax.optimization_barrier(jnp.sum(onehot_int * patches[None, :], axis=1)).astype(jnp.int32), 1)
    offset_in = (position - clip_begin).astype(jnp.int32)
    frame_index = (offset_in // frame_width).astype(jnp.int32)
    patch_index = (offset_in - frame_index * frame_width).astype(jnp.int32)
    space_id = jnp.where(live_mask, clip_index * CAP + frame_index, -1 - position).astype(jnp.int32)
    time_id = jnp.where(live_mask, clip_index * CAP + patch_index, -1 - position).astype(jnp.int32)
    return (live_mask, onehot_int.astype(jnp.float32), space_id, time_id)

def normalize(values):
    centered = values - lax.optimization_barrier(jnp.mean(values, axis=-1, keepdims=True))
    return centered * lax.rsqrt(lax.optimization_barrier(jnp.mean(centered * centered, axis=-1, keepdims=True)) + ln_eps)

def layer_apply(stream, modulate, weights, group_ids):
    allowed = group_ids[:, None] == group_ids[None, :]
    head_width = HEADS_DEV * HD
    blocks = weights.reshape(D, N_MP, WB)
    w_qkv = blocks[:, :, :3 * head_width]
    w_out = blocks[:, :, 3 * head_width:4 * head_width]
    w_up = blocks[:, :, 4 * head_width:4 * head_width + FF_DEV]
    w_down = blocks[:, :, 4 * head_width + FF_DEV:]
    lifted = low(normalize(stream) * (1.0 + modulate[:, 1]) + modulate[:, 0])
    qkv = jnp.einsum('td,dbc->tbc', lifted, w_qkv, precision=highest)
    qkv = low(low_back(qkv)).reshape(CAP, N_MP, 3, HEADS_DEV, HD)
    query = jnp.transpose(qkv[:, :, 0].reshape(CAP, HEADS, HD), (1, 0, 2))
    keys = jnp.transpose(qkv[:, :, 1].reshape(CAP, HEADS, HD), (1, 0, 2))
    values = jnp.transpose(qkv[:, :, 2].reshape(CAP, HEADS, HD), (1, 0, 2))

    def head_step(pieces):
        head_q, head_k, head_v = pieces
        scores = jnp.dot(head_q, head_k.T, precision=highest) * HD ** (-0.5)
        scores = jnp.where(allowed, low_back(scores), neg_fill)
        probs = jax.nn.softmax(scores, axis=-1)
        return jnp.dot(low(probs), head_v, precision=highest)
    attended = lax.map(jax.checkpoint(head_step), (query, keys, values))
    attended = low(low_back(attended))
    attended = jnp.transpose(attended, (1, 0, 2)).reshape(CAP, N_MP, head_width)
    branch = low_back(jnp.einsum('tbc,ebc->te', attended, w_out, precision=highest))
    middle = stream + modulate[:, 2] * branch
    lifted_two = low(normalize(middle) * (1.0 + modulate[:, 4]) + modulate[:, 3])
    hidden = low_back(jnp.einsum('td,dbc->tbc', lifted_two, w_up, precision=highest))
    active = low(jax.nn.gelu(hidden, approximate=False))
    update = low_back(jnp.einsum('tbc,ebc->te', active, w_down, precision=highest))
    return middle + modulate[:, 5] * update

def segment_grads(rounded, carry, pieces):
    seg_tokens, seg_cot, seg_mod, seg_frames, seg_patches = pieces
    live_mask, onehot, space_id, time_id = clip_meta(seg_frames, seg_patches)
    modulate = jnp.dot(onehot, seg_mod, precision=highest).reshape(CAP, L, 6, D)

    def forward(stream, weights):
        for layer_index in range(L):
            group_ids = space_id if layer_index % 2 == 0 else time_id
            stream = layer_apply(stream, modulate[:, layer_index], weights[layer_index], group_ids)
        return stream
    result, pullback = jax.vjp(forward, seg_tokens.astype(jnp.float32), rounded)
    cot_rows = seg_cot.astype(jnp.float32) * live_mask[:, None].astype(jnp.float32)
    grad_in, grad_weights = pullback(cot_rows)
    return (carry + grad_weights, (result.astype(jnp.bfloat16), grad_in))

def reference(tokens, cotangent, modulation, clip_frames, clip_patches, params, first_moment, second_moment, outer_momentum):
    rounded = params.astype(jnp.bfloat16).astype(jnp.float32)
    step_fn = partial(segment_grads, rounded)
    mixed_list = []
    grad_list = []
    moment_ones = []
    moment_twos = []
    diff_total = jnp.zeros(params.shape, jnp.float32)
    for group_index in range(GROUPS):
        pieces = (tokens[group_index].reshape(N_DP, CAP, D), cotangent[group_index].reshape(N_DP, CAP, D), modulation[group_index].reshape(N_DP, SLOTS, L * 6 * D), clip_frames[group_index].reshape(N_DP, SLOTS), clip_patches[group_index].reshape(N_DP, SLOTS))
        gradient, (mixed, grad_in) = lax.scan(step_fn, jnp.zeros(params.shape, jnp.float32), pieces)
        moment_one = beta_one * first_moment[group_index] + (1 - beta_one) * gradient
        moment_two = beta_two * second_moment[group_index] + (1 - beta_two) * gradient * gradient
        step_size = moment_one / (1 - beta_one ** STEP) / (jnp.sqrt(moment_two / (1 - beta_two ** STEP)) + adam_eps)
        inner_new = params - inner_rate * (step_size + decay_rate * params)
        diff_total = diff_total + (params - inner_new)
        mixed_list.append(mixed.reshape(N_DP * CAP, D))
        grad_list.append(grad_in.reshape(N_DP * CAP, D))
        moment_ones.append(moment_one)
        moment_twos.append(moment_two)
    average = diff_total / GROUPS
    momentum = outer_mu * outer_momentum + average
    updated = params - outer_rate * (average + outer_mu * momentum)
    return (jnp.stack(mixed_list), jnp.stack(grad_list), jnp.stack(moment_ones), jnp.stack(moment_twos), average, momentum, updated, updated.astype(jnp.bfloat16))
```

```python
from functools import partial

import jax
import jax.numpy as jnp
from jax import lax
from jax.experimental import pallas as pl
from jax.experimental.pallas import tpu as pltpu
from jax.sharding import PartitionSpec as P

D = 768
HEADS = 12
HD = 64
FF = 3072
L = 2
STEP = 5
CAP = 1024
SLOTS = 4
LONGF = 64
ROWS = CAP // 2
CHUNK = 128

ln_eps = 1e-06
neg_fill = -1e30
beta_one = 0.9
beta_two = 0.999
adam_eps = 1e-08
inner_rate = 0.04
decay_rate = 0.1
outer_rate = 0.7
outer_mu = 0.5

f32 = jnp.float32
bf16 = jnp.bfloat16
VM = pltpu.VMEM
SMEM = pltpu.SMEM
MIB = 2**20


def mm(left, right, lc, rc):
    return lax.dot_general(left, right, (((lc,), (rc,)), ((), ())), preferred_element_type=f32)


def moments(values):
    centered = values - jnp.mean(values, axis=-1, keepdims=True)
    inv_std = lax.rsqrt(jnp.mean(centered * centered, axis=-1, keepdims=True) + ln_eps)
    return centered * inv_std, inv_std


def norm_back(grad_normed, normed, inv_std):
    inner = grad_normed - jnp.mean(grad_normed, axis=-1, keepdims=True)
    inner = inner - normed * jnp.mean(grad_normed * normed, axis=-1, keepdims=True)
    return inv_std * inner


def row_mod(clip_col, table):
    total = jnp.where(clip_col == 0, table[0:1, :], 0.0)
    for clip in range(1, SLOTS):
        total = total + jnp.where(clip_col == clip, table[clip : clip + 1, :], 0.0)
    return total


def chunks():
    return [slice(at, at + CHUNK) for at in range(0, ROWS, CHUNK)]


def fetch(w_hbm, buf, sems, layer, low, high):
    copies = []
    for slot in range(4):
        copies.append(
            pltpu.make_async_copy(w_hbm.at[layer, slot, :, low:high], buf.at[slot], sems.at[slot])
        )
        copies[-1].start()
    return copies


def attn_fwd(layer, flag, x, clip, idc, idr, mod, w_hbm, x1, qkv_t, o_t, lse, buf, u_s, acc, sems):
    @pl.when(flag[0] == 1)
    def _():
        width = buf.shape[2]
        heads = 3
        hw = heads * HD
        copies = fetch(w_hbm, buf, sems, layer, 0, width)
        for rows in chunks():
            normed, _ = moments(x[rows, :])
            shift = row_mod(clip[rows, :], mod[0])
            scale = row_mod(clip[rows, :], mod[1])
            u_s[rows, :] = (normed * (1.0 + scale) + shift).astype(bf16)
        acc[...] = jnp.zeros_like(acc)
        for slot in range(4):
            copies[slot].wait()
            part = mm(u_s[...], buf[slot, :, : 3 * hw], 1, 0)
            qkv_t[slot] = part.T.astype(bf16)

            def head_step(head, carry):
                base = pl.multiple_of(head * HD, HD)
                keys = qkv_t[slot, pl.ds(hw + base, HD), :].T
                value_t = qkv_t[slot, pl.ds(2 * hw + base, HD), :]
                for q0 in range(0, ROWS, 256):
                    query_t = qkv_t[slot, pl.ds(base, HD), q0 : q0 + 256]
                    scores = mm(keys, query_t * jnp.asarray(0.125, bf16), 1, 0)
                    allowed = idc[...] == idr[:, q0 : q0 + 256]
                    scores = jnp.where(allowed, scores, neg_fill)
                    top = jnp.max(scores, axis=0, keepdims=True)
                    raw = jnp.exp(scores - top)
                    total = jnp.sum(raw, axis=0, keepdims=True)
                    probs = (raw / total).astype(bf16)
                    o_t[slot, pl.ds(base, HD), q0 : q0 + 256] = mm(value_t, probs, 1, 0).astype(
                        bf16
                    )
                    lse[slot * heads + head, :, q0 : q0 + 256] = top + jnp.log(total)
                return carry

            lax.fori_loop(0, heads, head_step, 0)
            acc[...] += mm(buf[slot, :, 3 * hw :], o_t[slot], 1, 0)
        for rows in chunks():
            gate = row_mod(clip[rows, :], mod[2])
            x1[rows, :] = x[rows, :] + gate * acc[:, rows].T


def mlp_fwd(layer, flag, x, clip, mod, w_hbm, x2, act, dgelu, buf, u_s, acc, sems):
    @pl.when(flag[0] == 1)
    def _():
        half = buf.shape[2] // 2
        attn_width = w_hbm.shape[3] - 2 * half
        copies = fetch(w_hbm, buf, sems, layer, attn_width, w_hbm.shape[3])
        for rows in chunks():
            normed, _ = moments(x[rows, :])
            shift = row_mod(clip[rows, :], mod[3])
            scale = row_mod(clip[rows, :], mod[4])
            u_s[rows, :] = (normed * (1.0 + scale) + shift).astype(bf16)
        acc[...] = jnp.zeros_like(acc)
        for slot in range(4):
            copies[slot].wait()
            for rows in chunks():
                hid = mm(u_s[rows, :], buf[slot, :, :half], 1, 0)
                cdf = 0.5 * (1.0 + lax.erf(hid * 0.7071067811865476))
                pdf = jnp.exp(-0.5 * hid * hid) * 0.3989422804014327
                act[slot, rows, :] = (hid * cdf).astype(bf16)
                dgelu[slot, rows, :] = (cdf + hid * pdf).astype(bf16)
            acc[...] += mm(act[slot], buf[slot, :, half:], 1, 1)
        for rows in chunks():
            gate = row_mod(clip[rows, :], mod[5])
            x2[rows, :] = x[rows, :] + gate * acc[rows, :]


def mlp_bwd(
    layer, flag, g, x, act, dgelu, clip, mod, w_hbm, g1, gw, buf, u_t, d_s, d_t, dh, acc, out, sems, osem
):
    @pl.when(flag[0] == 1)
    def _():
        half = buf.shape[2] // 2
        attn_width = w_hbm.shape[3] - 2 * half
        copies = fetch(w_hbm, buf, sems, layer, attn_width, w_hbm.shape[3])
        for rows in chunks():
            normed, _ = moments(x[rows, :])
            shift = row_mod(clip[rows, :], mod[3])
            scale = row_mod(clip[rows, :], mod[4])
            u_t[:, rows] = (normed * (1.0 + scale) + shift).T.astype(bf16)
            gate = row_mod(clip[rows, :], mod[5])
            down = gate * g[rows, :]
            d_s[rows, :] = down.astype(bf16)
            d_t[:, rows] = down.T.astype(bf16)
        acc[...] = jnp.zeros_like(acc)
        sends = []
        for slot in range(4):
            copies[slot].wait()
            if slot >= 2:
                sends[slot - 2].wait()
            place = slot % 2
            for rows in chunks():
                dact = mm(d_s[rows, :], buf[slot, :, half:], 1, 0)
                dh[rows, :] = (dact * dgelu[slot, rows, :].astype(f32)).astype(bf16)
            out[place, :, :half] = mm(u_t[...], dh[...], 1, 0).astype(bf16)
            out[place, :, half:] = mm(d_t[...], act[slot], 1, 0).astype(bf16)
            sends.append(pltpu.make_async_copy(out.at[place], gw.at[slot], osem.at[place]))
            sends[-1].start()
            acc[...] += mm(dh[...], buf[slot, :, :half], 1, 1)
        for rows in chunks():
            normed, inv_std = moments(x[rows, :])
            scale = row_mod(clip[rows, :], mod[4])
            g1[rows, :] = g[rows, :] + norm_back(acc[rows, :] * (1.0 + scale), normed, inv_std)
        sends[2].wait()
        sends[3].wait()


def attn_bwd(
    layer, flag, g1, x, qkv_t, o_t, lse, clip, idc, idr, mod, w_hbm, g0, gw,
    buf, u_t, d_t, dq, do_s, acc, out, sems, osem
):
    @pl.when(flag[0] == 1)
    def _():
        width = buf.shape[2]
        heads = 3
        hw = heads * HD
        copies = fetch(w_hbm, buf, sems, layer, 0, width)
        for rows in chunks():
            normed, _ = moments(x[rows, :])
            shift = row_mod(clip[rows, :], mod[0])
            scale = row_mod(clip[rows, :], mod[1])
            u_t[:, rows] = (normed * (1.0 + scale) + shift).T.astype(bf16)
            gate = row_mod(clip[rows, :], mod[2])
            d_t[:, rows] = (gate * g1[rows, :]).T.astype(bf16)
        acc[...] = jnp.zeros_like(acc)
        sends = []
        for slot in range(4):
            copies[slot].wait()
            if slot >= 2:
                sends[slot - 2].wait()
            place = slot % 2
            out[place, :, 3 * hw :] = mm(d_t[...], o_t[slot], 1, 1).astype(bf16)
            do_s[...] = mm(buf[slot, :, 3 * hw :], d_t[...], 0, 0).astype(bf16)

            def head_step(head, carry):
                base = pl.multiple_of(head * HD, HD)
                keys_t = qkv_t[slot, pl.ds(hw + base, HD), :]
                keys = keys_t.T
                values = qkv_t[slot, pl.ds(2 * hw + base, HD), :].T
                dk = jnp.zeros((HD, ROWS), f32)
                dv = jnp.zeros((HD, ROWS), f32)
                for q0 in range(0, ROWS, 256):
                    query_t = qkv_t[slot, pl.ds(base, HD), q0 : q0 + 256]
                    grad_t = do_s[pl.ds(base, HD), q0 : q0 + 256]
                    scores = mm(keys, query_t * jnp.asarray(0.125, bf16), 1, 0)
                    allowed = idc[...] == idr[:, q0 : q0 + 256]
                    probs = jnp.where(
                        allowed, jnp.exp(scores - lse[slot * heads + head, :, q0 : q0 + 256]), 0.0
                    )
                    dv = dv + mm(grad_t, probs.astype(bf16), 1, 1)
                    dp = mm(values, grad_t, 1, 0)
                    weighted = probs * dp
                    delta = jnp.sum(weighted, axis=0, keepdims=True)
                    ds = (weighted - probs * delta).astype(bf16)
                    dq[pl.ds(base, HD), q0 : q0 + 256] = (mm(keys_t, ds, 1, 0) * 0.125).astype(bf16)
                    dk = dk + mm(query_t, ds, 1, 1)
                dq[pl.ds(hw + base, HD), :] = (dk * 0.125).astype(bf16)
                dq[pl.ds(2 * hw + base, HD), :] = dv.astype(bf16)
                return carry

            lax.fori_loop(0, heads, head_step, 0)
            out[place, :, : 3 * hw] = mm(u_t[...], dq[...], 1, 1).astype(bf16)
            sends.append(pltpu.make_async_copy(out.at[place], gw.at[slot], osem.at[place]))
            sends[-1].start()
            acc[...] += mm(buf[slot, :, : 3 * hw], dq[...], 1, 0)
        for rows in chunks():
            normed, inv_std = moments(x[rows, :])
            scale = row_mod(clip[rows, :], mod[1])
            g0[rows, :] = g1[rows, :] + norm_back(acc[:, rows].T * (1.0 + scale), normed, inv_std)
        sends[2].wait()
        sends[3].wait()


def any_spec():
    return pl.BlockSpec(memory_space=pl.ANY)


def vm_spec():
    return pl.BlockSpec(memory_space=VM)


def smem_spec():
    return pl.BlockSpec(memory_space=SMEM)


def local_call(kernel, ins, outs, out_spaces, scratch, flops, moved):
    spaces = [smem_spec()] + [
        any_spec() if getattr(a, "ndim", 0) == 4 and a.shape[0] == L and a.shape[1] == 4 else vm_spec()
        for a in ins[1:]
    ]
    return pl.pallas_call(
        kernel,
        out_shape=outs,
        in_specs=spaces,
        out_specs=out_spaces,
        scratch_shapes=scratch,
        compiler_params=pltpu.CompilerParams(vmem_limit_bytes=58 * MIB),
        cost_estimate=pl.CostEstimate(flops=flops, bytes_accessed=moved, transcendentals=0),
    )(*ins)


def run_attn_fwd(layer, flag, x, clip, idc, idr, mod, w):
    sds = jax.ShapeDtypeStruct
    return local_call(
        partial(attn_fwd, layer),
        (flag, x, clip, idc, idr, mod, w),
        (
            sds((ROWS, D), f32),
            sds((4, 9 * HD, ROWS), bf16),
            sds((4, 3 * HD, ROWS), bf16),
            sds((HEADS, 1, ROWS), f32),
        ),
        (vm_spec(),) * 4,
        [
            VM((4, D, 12 * HD), bf16),
            VM((ROWS, D), bf16),
            VM((D, ROWS), f32),
            pltpu.SemaphoreType.DMA((4,)),
        ],
        int(8e9), int(1e7),
    )


def run_mlp_fwd(layer, flag, x, clip, mod, w):
    sds = jax.ShapeDtypeStruct
    unit = FF // 4
    return local_call(
        partial(mlp_fwd, layer),
        (flag, x, clip, mod, w),
        (sds((ROWS, D), f32), sds((4, ROWS, unit), bf16), sds((4, ROWS, unit), bf16)),
        (vm_spec(),) * 3,
        [
            VM((4, D, 2 * unit), bf16),
            VM((ROWS, D), bf16),
            VM((ROWS, D), f32),
            pltpu.SemaphoreType.DMA((4,)),
        ],
        int(8e9), int(1e7),
    )


def run_mlp_bwd(layer, flag, g, x, act, dgelu, clip, mod, w):
    sds = jax.ShapeDtypeStruct
    unit = FF // 4
    return local_call(
        partial(mlp_bwd, layer),
        (flag, g, x, act, dgelu, clip, mod, w),
        (sds((ROWS, D), f32), sds((4, D, 2 * unit), bf16)),
        (vm_spec(), any_spec()),
        [
            VM((4, D, 2 * unit), bf16),
            VM((D, ROWS), bf16),
            VM((ROWS, D), bf16),
            VM((D, ROWS), bf16),
            VM((ROWS, unit), bf16),
            VM((ROWS, D), f32),
            VM((2, D, 2 * unit), bf16),
            pltpu.SemaphoreType.DMA((4,)),
            pltpu.SemaphoreType.DMA((2,)),
        ],
        int(16e9), int(2e7),
    )


def run_attn_bwd(layer, flag, g1, x, qkv_t, o_t, lse, clip, idc, idr, mod, w):
    sds = jax.ShapeDtypeStruct
    return local_call(
        partial(attn_bwd, layer),
        (flag, g1, x, qkv_t, o_t, lse, clip, idc, idr, mod, w),
        (sds((ROWS, D), f32), sds((4, D, 12 * HD), bf16)),
        (vm_spec(), any_spec()),
        [
            VM((4, D, 12 * HD), bf16),
            VM((D, ROWS), bf16),
            VM((D, ROWS), bf16),
            VM((9 * HD, ROWS), bf16),
            VM((3 * HD, ROWS), bf16),
            VM((D, ROWS), f32),
            VM((2, D, 12 * HD), bf16),
            pltpu.SemaphoreType.DMA((4,)),
            pltpu.SemaphoreType.DMA((2,)),
        ],
        int(16e9), int(2e7),
    )


def slot_meta(frames, patches, long_core):
    frames = frames.astype(jnp.int32)
    patches = patches.astype(jnp.int32)
    sizes = frames * patches
    order = jnp.arange(SLOTS, dtype=jnp.int32)
    ends = jnp.sum(jnp.where(order[None, :] <= order[:, None], sizes[None, :], 0), axis=1)
    starts = ends - sizes
    long_hot = frames == LONGF
    long_start = jnp.sum(jnp.where(long_hot, starts, 0))
    long_size = jnp.sum(jnp.where(long_hot, sizes, 0))
    index = jnp.arange(ROWS, dtype=jnp.int32)
    short_pos = jnp.where(index < long_start, index, index + long_size)
    pos = jnp.where(long_core, index + long_start, short_pos)
    clip = jnp.sum((pos[:, None] >= ends[None, :]).astype(jnp.int32), axis=1)
    live = jnp.where(long_core, index < long_size, clip < SLOTS)
    clip = jnp.where(live, clip, SLOTS)
    hot = (clip[:, None] == order[None, :]).astype(jnp.int32)
    begin = jnp.sum(hot * starts[None, :], axis=1)
    width = jnp.maximum(jnp.sum(hot * patches[None, :], axis=1), 1)
    offset = pos - begin
    frame = offset // width
    patch = offset - frame * width
    space_id = jnp.where(live, clip * CAP + frame, -1 - index)
    time_id = jnp.where(live, clip * CAP + patch, -1 - index)
    return pos, live, clip, space_id, time_id


MESH_ID = pl.DeviceIdType.MESH
PIECE = 768
DMA = pltpu.SemaphoreType.DMA


def flip(index, bit):
    return index + bit - 2 * bit * lax.rem(index // bit, 2)


def gather_kernel(
    n_dp, tok, cot, meta, wb, tok_o, cot_o, meta_o, w_o,
    zs, zr, gs, gr, ds, dr, own_l, own_s, own_r, ts, tr, tl, cs, cr, ms, mr, ml,
):
    grp, dp, mp = lax.axis_index("grp"), lax.axis_index("dp"), lax.axis_index("mp")
    rows = wb.shape[1]
    cols = wb.shape[2]
    quarter = tok.shape[0]
    side = PIECE // 2
    pieces = [(layer, at) for layer in range(L) for at in range(0, cols, PIECE)]
    star = 1 + lax.rem(dp, 2)
    is_mid = jnp.logical_or(mp == 1, mp == 2)
    is_main = mp == star
    is_second = jnp.logical_and(is_mid, mp != star)
    other_mid = 3 - mp
    near = jnp.where(mp == 0, 1, 2)
    far = 3 - near
    my_rows = pl.ds(pl.multiple_of(dp * rows, rows), rows)

    def at_mp(where):
        return (grp, dp, where)

    def at_grp(bit):
        return (flip(grp, bit), dp, mp)

    def at_dp(step):
        return (grp, lax.rem(dp + step, n_dp), mp)

    mate = (grp, flip(dp, 1), mp)

    def greet(devices):
        for device in devices:
            pl.semaphore_signal(barrier, inc=1, device_id=device, device_id_type=MESH_ID)
        pl.semaphore_wait(barrier, len(devices))

    barrier = pltpu.get_barrier_semaphore()

    @pl.when(is_mid)
    def _():
        greet(
            [at_mp(0), at_mp(3), at_mp(other_mid), at_grp(1), at_grp(2)]
            + [at_dp(step) for step in range(1, n_dp)]
        )

    @pl.when(jnp.logical_not(is_mid))
    def _():
        greet([at_mp(1), at_mp(2)])

    def remote(src, dst, send, recv, device):
        return pltpu.make_async_remote_copy(
            src_ref=src, dst_ref=dst, send_sem=send, recv_sem=recv,
            device_id=device, device_id_type=MESH_ID,
        )

    def bit_of(k, slot):
        return 1 + (k + slot) % 2

    def half_cols(k, bit, mine):
        index = lax.rem(grp // bit, 2)
        if not mine:
            index = 1 - index
        return pl.ds(pl.multiple_of(pieces[k][1] + index * side, 128), side)

    def z_copy(k, slot, device):
        layer = pieces[k][0]
        span = half_cols(k, bit_of(k, slot), True)
        return remote(
            wb.at[layer, :, span], w_o.at[layer, slot, my_rows, span],
            zs.at[k, slot - 1], zr.at[k, slot - 1], device,
        )

    def g_copy(k, slot):
        layer = pieces[k][0]
        bit = bit_of(k, slot)
        span = half_cols(k, bit, True)
        place = w_o.at[layer, slot, my_rows, span]
        return remote(place, place, gs.at[k, slot - 1], gr.at[k, slot - 1], at_grp(bit))

    def d_copies(k, slot, mine):
        layer = pieces[k][0]
        span = half_cols(k, bit_of(k, slot), mine)
        place = w_o.at[layer, slot, my_rows, span]
        turn = 0 if mine else 1
        return [
            remote(
                place, place, ds.at[k, slot - 1, turn, step - 1], dr.at[k, slot - 1, turn, step - 1],
                at_dp(step),
            )
            for step in range(1, n_dp)
        ]

    def d_arrivals(k, slot, mine):
        layer = pieces[k][0]
        span = half_cols(k, bit_of(k, slot), mine)
        turn = 0 if mine else 1
        result = []
        for step in range(1, n_dp):
            source = lax.rem(dp + n_dp - step, n_dp)
            place = w_o.at[layer, slot, pl.ds(pl.multiple_of(source * rows, rows), rows), span]
            result.append(
                remote(
                    place, place, ds.at[k, slot - 1, turn, step - 1],
                    dr.at[k, slot - 1, turn, step - 1], at_dp(step),
                )
            )
        return result

    def part(ref, index):
        return ref.at[pl.ds(pl.multiple_of(index * quarter, quarter), quarter)]

    def route(src, out, send, recv):
        return remote(src, part(out, mp), send.at[0], recv.at[mp], at_mp(star))

    def pass_on(out, send, recv, index):
        return remote(
            part(out, index), part(out, index), send.at[1 + index], recv.at[4 + index], mate
        )

    both = ((tok, tok_o, ts, tr), (cot, cot_o, cs, cr))

    @pl.when(jnp.logical_not(is_main))
    def _():
        route(tok, tok_o, ts, tr).start()

    @pl.when(is_main)
    def _():
        pltpu.make_async_copy(meta, meta_o, ml.at[0]).start()
        remote(meta, meta_o, ms.at[0], mr.at[0], mate).start()
        for i, (src, out, send, recv) in enumerate(both):
            pltpu.make_async_copy(src, part(out, mp), tl.at[i]).start()

    count = len(pieces)

    @pl.when(jnp.logical_not(is_mid))
    def _():
        for k in range(count):
            if k == 2:
                route(cot, cot_o, cs, cr).start()
            if k >= 2:
                z_copy(k - 2, 1, at_mp(near)).wait_send()
                z_copy(k - 2, 3, at_mp(far)).wait_send()
            z_copy(k, 1, at_mp(near)).start()
            z_copy(k, 3, at_mp(far)).start()
        for k in range(count - 2, count):
            z_copy(k, 1, at_mp(near)).wait_send()
            z_copy(k, 3, at_mp(far)).wait_send()
        route(tok, tok_o, ts, tr).wait_send()
        route(cot, cot_o, cs, cr).wait_send()

    def arrival(out, recv, index):
        return remote(part(out, index), part(out, index), ts.at[0], recv.at[index], mate)

    def second_arrival(out, recv, index):
        return remote(part(out, index), part(out, index), ts.at[0], recv.at[4 + index], mate)

    def spread(which):
        src, out, send, recv = both[which]

        @pl.when(is_main)
        def _():
            pltpu.make_async_copy(src, part(out, mp), tl.at[which]).wait()
            pass_on(out, send, recv, mp).start()
            for index in (other_mid, 0, 3):
                arrival(out, recv, index).wait_recv()
                pass_on(out, send, recv, index).start()

    @pl.when(is_mid)
    def _():
        own = [
            pltpu.make_async_copy(wb.at[layer], w_o.at[layer, 0, my_rows], own_l.at[layer])
            for layer in range(L)
        ]
        shares = [
            [
                remote(
                    wb.at[layer], w_o.at[layer, 0, my_rows],
                    own_s.at[layer, step - 1], own_r.at[layer, step - 1], at_dp(step),
                )
                for step in range(1, n_dp)
            ]
            for layer in range(L)
        ]
        own[0].start()
        for copy in shares[0]:
            copy.start()
        z_copy(0, 2, at_mp(other_mid)).start()
        z_copy(1, 2, at_mp(other_mid)).start()
        spread(0)
        for k in range(count):
            if k == 2:
                own[1].start()
                for copy in shares[1]:
                    copy.start()
                pl.when(is_second)(lambda: route(cot, cot_o, cs, cr).start())
            if k == 4:
                spread(1)
            for slot in (1, 2, 3):
                z_copy(k, slot, at_mp(other_mid)).wait_recv()
                g_copy(k, slot).start()
                for copy in d_copies(k, slot, True):
                    copy.start()
            if k + 2 < count:
                z_copy(k, 2, at_mp(other_mid)).wait_send()
                z_copy(k + 2, 2, at_mp(other_mid)).start()
            if k >= 1:
                for slot in (1, 2, 3):
                    g_copy(k - 1, slot).wait_recv()
                    for copy in d_copies(k - 1, slot, False):
                        copy.start()
        for slot in (1, 2, 3):
            g_copy(count - 1, slot).wait_recv()
            for copy in d_copies(count - 1, slot, False):
                copy.start()
        for k in range(count - 2, count):
            z_copy(k, 2, at_mp(other_mid)).wait_send()
        for k in range(count):
            for slot in (1, 2, 3):
                g_copy(k, slot).wait_send()
                for mine in (True, False):
                    for copy in d_copies(k, slot, mine):
                        copy.wait_send()
                    for copy in d_arrivals(k, slot, mine):
                        copy.wait_recv()
        for layer in range(L):
            own[layer].wait()
            for step in range(1, n_dp):
                shares[layer][step - 1].wait_send()
                source = lax.rem(dp + n_dp - step, n_dp)
                place = w_o.at[layer, 0, pl.ds(pl.multiple_of(source * rows, rows), rows)]
                remote(
                    place, place, own_s.at[layer, step - 1], own_r.at[layer, step - 1], at_dp(step)
                ).wait_recv()

    @pl.when(is_main)
    def _():
        pltpu.make_async_copy(meta, meta_o, ml.at[0]).wait()
        remote(meta, meta_o, ms.at[0], mr.at[0], mate).wait_send()
        for src, out, send, recv in both:
            for index in range(4):
                pass_on(out, send, recv, index).wait_send()

    @pl.when(is_second)
    def _():
        remote(meta, meta_o, ms.at[0], mr.at[0], mate).wait_recv()
        route(tok, tok_o, ts, tr).wait_send()
        route(cot, cot_o, cs, cr).wait_send()
        for src, out, send, recv in both:
            for index in range(4):
                second_arrival(out, recv, index).wait_recv()


def gather_all(tok, cot, meta, wb):
    sds = jax.ShapeDtypeStruct
    n_dp = lax.axis_size("dp")
    rows, cols = wb.shape[1], wb.shape[2]
    count = L * cols // PIECE
    far = n_dp - 1
    return pl.pallas_call(
        partial(gather_kernel, n_dp),
        out_shape=(
            sds((CAP, D), bf16), sds((CAP, D), bf16), sds(meta.shape, f32),
            sds((L, 4, rows * n_dp, cols), bf16),
        ),
        in_specs=[any_spec()] * 4,
        out_specs=(any_spec(),) * 4,
        scratch_shapes=[
            DMA((count, 3)), DMA((count, 3)), DMA((count, 3)), DMA((count, 3)),
            DMA((count, 3, 2, far)), DMA((count, 3, 2, far)),
            DMA((L,)), DMA((L, far)), DMA((L, far)),
            DMA((5,)), DMA((8,)), DMA((2,)), DMA((5,)), DMA((8,)), DMA((1,)), DMA((1,)), DMA((1,)),
        ],
        compiler_params=pltpu.CompilerParams(collective_id=1, has_side_effects=True),
    )(tok, cot, meta, wb)


def adam_kernel(flag, par, mom, var, own, ga, gb, gc, *rest):
    new_m, new_v, diff = rest[-3:]
    keep = jnp.where(flag[0] == 1, own[...].astype(f32), 0.0)
    grad = keep + ga[...].astype(f32) + gb[...].astype(f32) + gc[...].astype(f32)
    one = beta_one * mom[...] + (1 - beta_one) * grad
    two = beta_two * var[...] + (1 - beta_two) * grad * grad
    step = one / (1 - beta_one**STEP) / (jnp.sqrt(two / (1 - beta_two**STEP)) + adam_eps)
    new_m[...] = one
    new_v[...] = two
    diff[...] = (inner_rate * (step + decay_rate * par[...])).astype(bf16)


def row_block(rows):
    return 96 if rows % 96 == 0 else rows


def adam(flag, layer, first, width, par, mom, var, parts, prev):
    rows, cols = par.shape[1], par.shape[2]
    block = row_block(rows)
    sds = jax.ShapeDtypeStruct
    base = first // PIECE
    full = pl.BlockSpec((None, block, PIECE), lambda i, j: (layer, i, base + j))
    piece = pl.BlockSpec((block, PIECE), lambda i, j: (i, j))
    ins = [flag, par, mom, var, *parts]
    specs = [smem_spec(), full, full, full] + [piece] * 4
    aliases = {}
    if prev is not None:
        aliases = {len(ins): 0, len(ins) + 1: 1}
        ins += list(prev)
        specs += [any_spec(), any_spec()]
    return pl.pallas_call(
        adam_kernel,
        grid=(rows // block, width // PIECE),
        out_shape=(sds(par.shape, f32), sds(par.shape, f32), sds((rows, width), bf16)),
        in_specs=specs,
        out_specs=(full, full, piece),
        input_output_aliases=aliases,
        compiler_params=pltpu.CompilerParams(vmem_limit_bytes=48 * MIB),
        cost_estimate=pl.CostEstimate(
            flops=rows * width * 20, bytes_accessed=rows * width * 30, transcendentals=0
        ),
    )(*ins)


def outer_kernel(count, par, mom, *rest):
    total = rest[0][...].astype(f32)
    for other in rest[1:count]:
        total = total + other[...].astype(f32)
    average = total / count
    out_a, out_m, out_w, out_l = rest[-4:]
    momentum = outer_mu * mom[...] + average
    updated = par[...] - outer_rate * (average + outer_mu * momentum)
    out_a[...] = average
    out_m[...] = momentum
    out_w[...] = updated
    out_l[...] = updated.astype(bf16)


def outer(layer, first, width, par, mom, diffs, prev):
    rows, cols = par.shape[1], par.shape[2]
    block = row_block(rows)
    sds = jax.ShapeDtypeStruct
    base = first // PIECE
    full = pl.BlockSpec((None, block, PIECE), lambda i, j: (layer, i, base + j))
    piece = pl.BlockSpec((block, PIECE), lambda i, j: (i, j))
    ins = [par, mom, *diffs]
    specs = [full, full] + [piece] * len(diffs)
    aliases = {}
    if prev is not None:
        aliases = {len(ins) + i: i for i in range(4)}
        ins += list(prev)
        specs += [any_spec()] * 4
    return pl.pallas_call(
        partial(outer_kernel, len(diffs)),
        grid=(rows // block, width // PIECE),
        out_shape=(sds(par.shape, f32),) * 3 + (sds(par.shape, bf16),),
        in_specs=specs,
        out_specs=(full,) * 4,
        input_output_aliases=aliases,
        compiler_params=pltpu.CompilerParams(vmem_limit_bytes=48 * MIB),
        cost_estimate=pl.CostEstimate(
            flops=rows * width * 20, bytes_accessed=rows * width * 30, transcendentals=0
        ),
    )(*ins)


def send_mp(values, pairs):
    return lax.ppermute(values, "mp", pairs)


def body(
    tokens, cotangent, modulation, clip_frames, clip_patches, params, first_moment, second_moment,
    outer_momentum,
):
    n_dp = lax.axis_size("dp")
    n_grp = lax.axis_size("grp")
    dp, mp = lax.axis_index("dp"), lax.axis_index("mp")
    quarter = tokens.shape[1]
    rows, cols = params.shape[1], params.shape[2]
    star = 1 + lax.rem(dp, 2)
    is_mid = jnp.logical_or(mp == 1, mp == 2)
    flag = is_mid.astype(jnp.int32)[None]

    meta = jnp.concatenate(
        [
            modulation[0],
            clip_frames[0].astype(f32)[:, None],
            clip_patches[0].astype(f32)[:, None],
            jnp.zeros((SLOTS, 126), f32),
        ],
        axis=1,
    )
    tok_all, cot_all, meta_all, w = gather_all(tokens[0], cotangent[0], meta, params.astype(bf16))

    mods = meta_all[:, : modulation.shape[2]].reshape(SLOTS, L, 6, D).transpose(1, 2, 0, 3)
    frames = meta_all[:, modulation.shape[2]]
    patches = meta_all[:, modulation.shape[2] + 1]
    pos, live, clip, space_id, time_id = slot_meta(frames, patches, mp == star)
    pick = (pos[:, None] == jnp.arange(CAP, dtype=jnp.int32)[None, :]) & live[:, None]
    pick = pick.astype(bf16)
    clip = clip[:, None]

    x = jnp.dot(pick, tok_all, preferred_element_type=f32)
    gradient = jnp.dot(pick, cot_all, preferred_element_type=f32)
    ids = (space_id, time_id)
    kept = []
    for layer in range(L):
        idc, idr = ids[layer % 2][:, None], ids[layer % 2][None, :]
        x1, qkv_t, o_t, lse = run_attn_fwd(layer, flag, x, clip, idc, idr, mods[layer], w)
        x2, act, dgelu = run_mlp_fwd(layer, flag, x1, clip, mods[layer], w)
        kept.append((x, x1, qkv_t, o_t, lse, act, dgelu))
        x = x2

    back = [
        [((d, s), (d, o)) for d, s, o in ((d, 1 + d % 2, order(d)) for d in range(n_dp))]
        for order in (
            lambda d: 0 if d % 2 == 0 else 3,
            lambda d: 2 if d % 2 == 0 else 1,
            lambda d: 3 if d % 2 == 0 else 0,
        )
    ]
    quarters = [jnp.where(star == 1, a, b) for a, b in ((0, 3), (2, 1), (3, 0))]
    swap = [(d, d ^ 1) for d in range(n_dp)]

    def send_back(values):
        placed = lax.dot_general(
            pick, values.astype(bf16), (((0,), (0,)), ((), ())), preferred_element_type=f32
        ).astype(bf16)
        placed = jnp.where(is_mid, placed, jnp.zeros_like(placed))
        placed = placed + lax.ppermute(placed, "dp", swap)
        mine = lax.dynamic_slice_in_dim(placed, mp * quarter, quarter, 0)
        result = jnp.where(mp == star, mine, jnp.zeros_like(mine))
        for pairs, index in zip(back, quarters):
            piece = lax.dynamic_slice_in_dim(placed, index * quarter, quarter, 0)
            flat = [(a[0] * 4 + a[1], b[0] * 4 + b[1]) for a, b in pairs]
            result = result + lax.ppermute(piece, ("dp", "mp"), flat)
        return result

    total = jnp.sum(clip_frames[0] * clip_patches[0])
    own_live = (mp * quarter + jnp.arange(quarter, dtype=jnp.int32) < total)[:, None]
    mixed = jnp.where(own_live, send_back(x), tokens[0])

    mom, var = first_moment[0], second_moment[0]
    state, done = None, None

    def finish(layer, first, grads, state, done):
        width = grads.shape[2]
        share = lax.psum_scatter(grads, "dp", scatter_dimension=1, tiled=True)
        parts = (
            share[0],
            send_mp(share[1], [(1, 0), (2, 3)]),
            send_mp(share[2], [(1, 2), (2, 1)]),
            send_mp(share[3], [(1, 3), (2, 0)]),
        )
        new_m, new_v, diff = adam(flag, layer, first, width, params, mom, var, parts, state)
        diffs = [diff] + [
            lax.ppermute(diff, "grp", [(g, (g + step) % n_grp) for g in range(n_grp)])
            if n_grp != 4
            else lax.ppermute(diff, "grp", [(g, g ^ step) for g in range(n_grp)])
            for step in range(1, n_grp)
        ]
        done = outer(layer, first, width, params, outer_momentum, diffs, done)
        return (new_m, new_v), done

    for layer in reversed(range(L)):
        idc, idr = ids[layer % 2][:, None], ids[layer % 2][None, :]
        x0, x1, qkv_t, o_t, lse, act, dgelu = kept[layer]
        g1, g_mlp = run_mlp_bwd(layer, flag, gradient, x1, act, dgelu, clip, mods[layer], w)
        state, done = finish(layer, PIECE, g_mlp, state, done)
        gradient, g_attn = run_attn_bwd(
            layer, flag, g1, x0, qkv_t, o_t, lse, clip, idc, idr, mods[layer], w
        )
        state, done = finish(layer, 0, g_attn, state, done)
    input_grad = send_back(gradient).astype(f32)
    average, momentum, updated, low = done
    return (
        mixed[None], input_grad[None], state[0][None], state[1][None], average, momentum, updated, low,
    )


def solution(mesh):
    in_specs = (
        P("grp", ("dp", "mp"), None),
        P("grp", ("dp", "mp"), None),
        P("grp", "dp", None),
        P("grp", "dp"),
        P("grp", "dp"),
        P(None, "dp", "mp"),
        P("grp", None, "dp", "mp"),
        P("grp", None, "dp", "mp"),
        P(None, "dp", "mp"),
    )
    out_specs = (
        P("grp", ("dp", "mp"), None),
        P("grp", ("dp", "mp"), None),
        P("grp", None, "dp", "mp"),
        P("grp", None, "dp", "mp"),
        P(None, "dp", "mp"),
        P(None, "dp", "mp"),
        P(None, "dp", "mp"),
        P(None, "dp", "mp"),
    )
    return jax.shard_map(body, mesh=mesh, in_specs=in_specs, out_specs=out_specs, check_vma=False)
```

```python
from functools import partial

import jax
import jax.numpy as jnp
from jax import lax
from jax.experimental import pallas as pl
from jax.experimental.pallas import tpu as pltpu
from jax.sharding import PartitionSpec as P

D = 768
HEADS = 12
HD = 64
FF = 3072
L = 2
STEP = 5
CAP = 1024
SLOTS = 4
LONGF = 64
ROWS = CAP // 2
CHUNK = 128

ln_eps = 1e-06
neg_fill = -1e30
beta_one = 0.9
beta_two = 0.999
adam_eps = 1e-08
inner_rate = 0.04
decay_rate = 0.1
outer_rate = 0.7
outer_mu = 0.5

f32 = jnp.float32
bf16 = jnp.bfloat16
VM = pltpu.VMEM
SMEM = pltpu.SMEM
MIB = 2**20


def mm(left, right, lc, rc):
    return lax.dot_general(left, right, (((lc,), (rc,)), ((), ())), preferred_element_type=f32)


def moments(values):
    centered = values - jnp.mean(values, axis=-1, keepdims=True)
    inv_std = lax.rsqrt(jnp.mean(centered * centered, axis=-1, keepdims=True) + ln_eps)
    return centered * inv_std, inv_std


def norm_back(grad_normed, normed, inv_std):
    inner = grad_normed - jnp.mean(grad_normed, axis=-1, keepdims=True)
    inner = inner - normed * jnp.mean(grad_normed * normed, axis=-1, keepdims=True)
    return inv_std * inner


def row_mod(clip_col, table):
    total = jnp.where(clip_col == 0, table[0:1, :], 0.0)
    for clip in range(1, SLOTS):
        total = total + jnp.where(clip_col == clip, table[clip : clip + 1, :], 0.0)
    return total


def chunks():
    return [slice(at, at + CHUNK) for at in range(0, ROWS, CHUNK)]


def fetch(w_hbm, buf, sems, layer, low, high):
    copies = []
    for slot in range(4):
        copies.append(
            pltpu.make_async_copy(w_hbm.at[layer, slot, :, low:high], buf.at[slot], sems.at[slot])
        )
        copies[-1].start()
    return copies


def attn_fwd(layer, flag, x, clip, idc, idr, mod, w_hbm, x1, qo, lse, buf, u_s, acc, sems):
    @pl.when(flag[0] == 1)
    def _():
        width = buf.shape[2]
        heads = 3
        hw = heads * HD
        copies = fetch(w_hbm, buf, sems, layer, 0, width)
        for rows in chunks():
            normed, _ = moments(x[rows, :])
            shift = row_mod(clip[rows, :], mod[0])
            scale = row_mod(clip[rows, :], mod[1])
            u_s[rows, :] = (normed * (1.0 + scale) + shift).astype(bf16)
        acc[...] = jnp.zeros_like(acc)
        for slot in range(4):
            copies[slot].wait()
            part = mm(u_s[...], buf[slot, :, : 3 * hw], 1, 0)
            qo[slot, : 3 * hw] = part.T.astype(bf16)

            def head_step(head, carry):
                base = pl.multiple_of(head * HD, HD)
                keys = qo[slot, pl.ds(hw + base, HD), :].T
                value_t = qo[slot, pl.ds(2 * hw + base, HD), :]
                for q0 in range(0, ROWS, 256):
                    query_t = qo[slot, pl.ds(base, HD), q0 : q0 + 256]
                    scores = mm(keys, query_t * jnp.asarray(0.125, bf16), 1, 0)
                    allowed = idc[...] == idr[:, q0 : q0 + 256]
                    scores = jnp.where(allowed, scores, neg_fill)
                    top = jnp.max(scores, axis=0, keepdims=True)
                    raw = jnp.exp(scores - top)
                    total = jnp.sum(raw, axis=0, keepdims=True)
                    probs = (raw / total).astype(bf16)
                    qo[slot, pl.ds(3 * hw + base, HD), q0 : q0 + 256] = mm(value_t, probs, 1, 0).astype(
                        bf16
                    )
                    lse[slot * heads + head, :, q0 : q0 + 256] = top + jnp.log(total)
                return carry

            lax.fori_loop(0, heads, head_step, 0)
            acc[...] += mm(buf[slot, :, 3 * hw :], qo[slot, 3 * hw :], 1, 0)
        for rows in chunks():
            gate = row_mod(clip[rows, :], mod[2])
            x1[rows, :] = x[rows, :] + gate * acc[:, rows].T


def mlp_fwd(layer, flag, x, clip, mod, w_hbm, x2, ad, buf, u_s, acc, sems):
    @pl.when(flag[0] == 1)
    def _():
        half = buf.shape[2] // 2
        attn_width = w_hbm.shape[3] - 2 * half
        copies = fetch(w_hbm, buf, sems, layer, attn_width, w_hbm.shape[3])
        for rows in chunks():
            normed, _ = moments(x[rows, :])
            shift = row_mod(clip[rows, :], mod[3])
            scale = row_mod(clip[rows, :], mod[4])
            u_s[rows, :] = (normed * (1.0 + scale) + shift).astype(bf16)
        acc[...] = jnp.zeros_like(acc)
        for slot in range(4):
            copies[slot].wait()
            for rows in chunks():
                hid = mm(u_s[rows, :], buf[slot, :, :half], 1, 0)
                cdf = 0.5 * (1.0 + lax.erf(hid * 0.7071067811865476))
                pdf = jnp.exp(-0.5 * hid * hid) * 0.3989422804014327
                ad[slot, 0, rows, :] = (hid * cdf).astype(bf16)
                ad[slot, 1, rows, :] = (cdf + hid * pdf).astype(bf16)
            acc[...] += mm(ad[slot, 0], buf[slot, :, half:], 1, 1)
        for rows in chunks():
            gate = row_mod(clip[rows, :], mod[5])
            x2[rows, :] = x[rows, :] + gate * acc[rows, :]


def any_spec():
    return pl.BlockSpec(memory_space=pl.ANY)


def vm_spec():
    return pl.BlockSpec(memory_space=VM)


def smem_spec():
    return pl.BlockSpec(memory_space=SMEM)


def local_call(kernel, ins, outs, out_spaces, scratch, flops, moved):
    spaces = [smem_spec()] + [
        any_spec() if getattr(a, "ndim", 0) == 4 and a.shape[0] == L and a.shape[1] == 4 else vm_spec()
        for a in ins[1:]
    ]
    return pl.pallas_call(
        kernel,
        out_shape=outs,
        in_specs=spaces,
        out_specs=out_spaces,
        scratch_shapes=scratch,
        compiler_params=pltpu.CompilerParams(vmem_limit_bytes=58 * MIB),
        cost_estimate=pl.CostEstimate(flops=flops, bytes_accessed=moved, transcendentals=0),
    )(*ins)


def run_attn_fwd(layer, flag, x, clip, idc, idr, mod, w):
    sds = jax.ShapeDtypeStruct
    return local_call(
        partial(attn_fwd, layer),
        (flag, x, clip, idc, idr, mod, w),
        (
            sds((ROWS, D), f32),
            sds((4, 12 * HD, ROWS), bf16),
            sds((HEADS, 1, ROWS), f32),
        ),
        (vm_spec(),) * 3,
        [
            VM((4, D, 12 * HD), bf16),
            VM((ROWS, D), bf16),
            VM((D, ROWS), f32),
            pltpu.SemaphoreType.DMA((4,)),
        ],
        int(8e9), int(1e7),
    )


def run_mlp_fwd(layer, flag, x, clip, mod, w):
    sds = jax.ShapeDtypeStruct
    unit = FF // 4
    return local_call(
        partial(mlp_fwd, layer),
        (flag, x, clip, mod, w),
        (sds((ROWS, D), f32), sds((4, 2, ROWS, unit), bf16)),
        (vm_spec(),) * 2,
        [
            VM((4, D, 2 * unit), bf16),
            VM((ROWS, D), bf16),
            VM((ROWS, D), f32),
            pltpu.SemaphoreType.DMA((4,)),
        ],
        int(8e9), int(1e7),
    )


def slot_meta(frames, patches, long_core):
    frames = frames.astype(jnp.int32)
    patches = patches.astype(jnp.int32)
    sizes = frames * patches
    order = jnp.arange(SLOTS, dtype=jnp.int32)
    ends = jnp.sum(jnp.where(order[None, :] <= order[:, None], sizes[None, :], 0), axis=1)
    starts = ends - sizes
    long_hot = frames == LONGF
    long_start = jnp.sum(jnp.where(long_hot, starts, 0))
    long_size = jnp.sum(jnp.where(long_hot, sizes, 0))
    index = jnp.arange(ROWS, dtype=jnp.int32)
    short_pos = jnp.where(index < long_start, index, index + long_size)
    pos = jnp.where(long_core, index + long_start, short_pos)
    clip = jnp.sum((pos[:, None] >= ends[None, :]).astype(jnp.int32), axis=1)
    live = jnp.where(long_core, index < long_size, clip < SLOTS)
    clip = jnp.where(live, clip, SLOTS)
    hot = (clip[:, None] == order[None, :]).astype(jnp.int32)
    begin = jnp.sum(hot * starts[None, :], axis=1)
    width = jnp.maximum(jnp.sum(hot * patches[None, :], axis=1), 1)
    offset = pos - begin
    frame = offset // width
    patch = offset - frame * width
    space_id = jnp.where(live, clip * CAP + frame, -1 - index)
    time_id = jnp.where(live, clip * CAP + patch, -1 - index)
    return pos, live, clip, space_id, time_id


MESH_ID = pl.DeviceIdType.MESH
PIECE = 768
DMA = pltpu.SemaphoreType.DMA


def flip(index, bit):
    return index + bit - 2 * bit * lax.rem(index // bit, 2)


def gather_kernel(
    n_dp, tok, cot, meta, wb, tok_o, cot_o, meta_o, w_o,
    zs, zr, gs, gr, ds, dr, own_l, own_s, own_r, ts, tr, tl, cs, cr, ms, mr, ml,
):
    grp, dp, mp = lax.axis_index("grp"), lax.axis_index("dp"), lax.axis_index("mp")
    rows = wb.shape[1]
    cols = wb.shape[2]
    quarter = tok.shape[0]
    side = PIECE // 2
    pieces = [(layer, at) for layer in range(L) for at in range(0, cols, PIECE)]
    star = 1 + lax.rem(dp, 2)
    is_mid = jnp.logical_or(mp == 1, mp == 2)
    is_main = mp == star
    is_second = jnp.logical_and(is_mid, mp != star)
    other_mid = 3 - mp
    near = jnp.where(mp == 0, 1, 2)
    far = 3 - near
    my_rows = pl.ds(pl.multiple_of(dp * rows, rows), rows)

    def at_mp(where):
        return (grp, dp, where)

    def at_grp(bit):
        return (flip(grp, bit), dp, mp)

    def at_dp(step):
        return (grp, lax.rem(dp + step, n_dp), mp)

    mate = (grp, flip(dp, 1), mp)

    def greet(devices):
        for device in devices:
            pl.semaphore_signal(barrier, inc=1, device_id=device, device_id_type=MESH_ID)
        pl.semaphore_wait(barrier, len(devices))

    barrier = pltpu.get_barrier_semaphore()

    @pl.when(is_mid)
    def _():
        greet(
            [at_mp(0), at_mp(3), at_mp(other_mid), at_grp(1), at_grp(2)]
            + [at_dp(step) for step in range(1, n_dp)]
        )

    @pl.when(jnp.logical_not(is_mid))
    def _():
        greet([at_mp(1), at_mp(2)])

    def remote(src, dst, send, recv, device):
        return pltpu.make_async_remote_copy(
            src_ref=src, dst_ref=dst, send_sem=send, recv_sem=recv,
            device_id=device, device_id_type=MESH_ID,
        )

    def bit_of(k, slot):
        return 1 + (k + slot) % 2

    def half_cols(k, bit, mine):
        index = lax.rem(grp // bit, 2)
        if not mine:
            index = 1 - index
        return pl.ds(pl.multiple_of(pieces[k][1] + index * side, 128), side)

    def z_copy(k, slot, device):
        layer = pieces[k][0]
        span = half_cols(k, bit_of(k, slot), True)
        return remote(
            wb.at[layer, :, span], w_o.at[layer, slot, my_rows, span],
            zs.at[k, slot - 1], zr.at[k, slot - 1], device,
        )

    def g_copy(k, slot):
        layer = pieces[k][0]
        bit = bit_of(k, slot)
        span = half_cols(k, bit, True)
        place = w_o.at[layer, slot, my_rows, span]
        return remote(place, place, gs.at[k, slot - 1], gr.at[k, slot - 1], at_grp(bit))

    def d_copies(k, slot, mine):
        layer = pieces[k][0]
        span = half_cols(k, bit_of(k, slot), mine)
        place = w_o.at[layer, slot, my_rows, span]
        turn = 0 if mine else 1
        return [
            remote(
                place, place, ds.at[k, slot - 1, turn, step - 1], dr.at[k, slot - 1, turn, step - 1],
                at_dp(step),
            )
            for step in range(1, n_dp)
        ]

    def d_arrivals(k, slot, mine):
        layer = pieces[k][0]
        span = half_cols(k, bit_of(k, slot), mine)
        turn = 0 if mine else 1
        result = []
        for step in range(1, n_dp):
            source = lax.rem(dp + n_dp - step, n_dp)
            place = w_o.at[layer, slot, pl.ds(pl.multiple_of(source * rows, rows), rows), span]
            result.append(
                remote(
                    place, place, ds.at[k, slot - 1, turn, step - 1],
                    dr.at[k, slot - 1, turn, step - 1], at_dp(step),
                )
            )
        return result

    def part(ref, index):
        return ref.at[pl.ds(pl.multiple_of(index * quarter, quarter), quarter)]

    def route(src, out, send, recv):
        return remote(src, part(out, mp), send.at[0], recv.at[mp], at_mp(star))

    def pass_on(out, send, recv, index):
        return remote(
            part(out, index), part(out, index), send.at[1 + index], recv.at[4 + index], mate
        )

    both = ((tok, tok_o, ts, tr), (cot, cot_o, cs, cr))

    @pl.when(jnp.logical_not(is_main))
    def _():
        route(tok, tok_o, ts, tr).start()

    @pl.when(is_main)
    def _():
        pltpu.make_async_copy(meta, meta_o, ml.at[0]).start()
        remote(meta, meta_o, ms.at[0], mr.at[0], mate).start()
        for i, (src, out, send, recv) in enumerate(both):
            pltpu.make_async_copy(src, part(out, mp), tl.at[i]).start()

    count = len(pieces)

    @pl.when(jnp.logical_not(is_mid))
    def _():
        for k in range(count):
            if k == 2:
                route(cot, cot_o, cs, cr).start()
            if k >= 2:
                z_copy(k - 2, 1, at_mp(near)).wait_send()
                z_copy(k - 2, 3, at_mp(far)).wait_send()
            z_copy(k, 1, at_mp(near)).start()
            z_copy(k, 3, at_mp(far)).start()
        for k in range(count - 2, count):
            z_copy(k, 1, at_mp(near)).wait_send()
            z_copy(k, 3, at_mp(far)).wait_send()
        route(tok, tok_o, ts, tr).wait_send()
        route(cot, cot_o, cs, cr).wait_send()

    def arrival(out, recv, index):
        return remote(part(out, index), part(out, index), ts.at[0], recv.at[index], mate)

    def second_arrival(out, recv, index):
        return remote(part(out, index), part(out, index), ts.at[0], recv.at[4 + index], mate)

    def spread(which):
        src, out, send, recv = both[which]

        @pl.when(is_main)
        def _():
            pltpu.make_async_copy(src, part(out, mp), tl.at[which]).wait()
            pass_on(out, send, recv, mp).start()
            for index in (other_mid, 0, 3):
                arrival(out, recv, index).wait_recv()
                pass_on(out, send, recv, index).start()

    @pl.when(is_mid)
    def _():
        own = [
            pltpu.make_async_copy(wb.at[layer], w_o.at[layer, 0, my_rows], own_l.at[layer])
            for layer in range(L)
        ]
        shares = [
            [
                remote(
                    wb.at[layer], w_o.at[layer, 0, my_rows],
                    own_s.at[layer, step - 1], own_r.at[layer, step - 1], at_dp(step),
                )
                for step in range(1, n_dp)
            ]
            for layer in range(L)
        ]
        own[0].start()
        for copy in shares[0]:
            copy.start()
        z_copy(0, 2, at_mp(other_mid)).start()
        z_copy(1, 2, at_mp(other_mid)).start()
        spread(0)
        for k in range(count):
            if k == 2:
                own[1].start()
                for copy in shares[1]:
                    copy.start()
                pl.when(is_second)(lambda: route(cot, cot_o, cs, cr).start())
            for slot in (1, 2, 3):
                z_copy(k, slot, at_mp(other_mid)).wait_recv()
                g_copy(k, slot).start()
                for copy in d_copies(k, slot, True):
                    copy.start()
            if k + 2 < count:
                z_copy(k, 2, at_mp(other_mid)).wait_send()
                z_copy(k + 2, 2, at_mp(other_mid)).start()
            if k >= 1:
                for slot in (1, 2, 3):
                    g_copy(k - 1, slot).wait_recv()
                    for copy in d_copies(k - 1, slot, False):
                        copy.start()
        spread(1)
        for slot in (1, 2, 3):
            g_copy(count - 1, slot).wait_recv()
            for copy in d_copies(count - 1, slot, False):
                copy.start()
        for k in range(count - 2, count):
            z_copy(k, 2, at_mp(other_mid)).wait_send()
        for k in range(count):
            for slot in (1, 2, 3):
                g_copy(k, slot).wait_send()
                for mine in (True, False):
                    for copy in d_copies(k, slot, mine):
                        copy.wait_send()
                    for copy in d_arrivals(k, slot, mine):
                        copy.wait_recv()
        for layer in range(L):
            own[layer].wait()
            for step in range(1, n_dp):
                shares[layer][step - 1].wait_send()
                source = lax.rem(dp + n_dp - step, n_dp)
                place = w_o.at[layer, 0, pl.ds(pl.multiple_of(source * rows, rows), rows)]
                remote(
                    place, place, own_s.at[layer, step - 1], own_r.at[layer, step - 1], at_dp(step)
                ).wait_recv()

    @pl.when(is_main)
    def _():
        pltpu.make_async_copy(meta, meta_o, ml.at[0]).wait()
        remote(meta, meta_o, ms.at[0], mr.at[0], mate).wait_send()
        for src, out, send, recv in both:
            for index in range(4):
                pass_on(out, send, recv, index).wait_send()

    @pl.when(is_second)
    def _():
        remote(meta, meta_o, ms.at[0], mr.at[0], mate).wait_recv()
        route(tok, tok_o, ts, tr).wait_send()
        route(cot, cot_o, cs, cr).wait_send()
        for src, out, send, recv in both:
            for index in range(4):
                second_arrival(out, recv, index).wait_recv()


def gather_all(tok, cot, meta, wb):
    sds = jax.ShapeDtypeStruct
    n_dp = lax.axis_size("dp")
    rows, cols = wb.shape[1], wb.shape[2]
    count = L * cols // PIECE
    far = n_dp - 1
    return pl.pallas_call(
        partial(gather_kernel, n_dp),
        out_shape=(
            sds((CAP, D), bf16), sds((CAP, D), bf16), sds(meta.shape, f32),
            sds((L, 4, rows * n_dp, cols), bf16),
        ),
        in_specs=[any_spec()] * 4,
        out_specs=(any_spec(),) * 4,
        scratch_shapes=[
            DMA((count, 3)), DMA((count, 3)), DMA((count, 3)), DMA((count, 3)),
            DMA((count, 3, 2, far)), DMA((count, 3, 2, far)),
            DMA((L,)), DMA((L, far)), DMA((L, far)),
            DMA((5,)), DMA((8,)), DMA((2,)), DMA((5,)), DMA((8,)), DMA((1,)), DMA((1,)), DMA((1,)),
        ],
        compiler_params=pltpu.CompilerParams(collective_id=1, has_side_effects=True),
    )(tok, cot, meta, wb)


def share_rows(rows, n_grp):
    part = rows // n_grp
    return part if part * n_grp == rows and part % 16 == 0 else rows


def back_kernel(
    n_dp, n_grp,
    xb, pick_t, g_in, clip, idc, idr, mods, lse, xs_0, xm_0, xs_1, xm_1, qo_0, qo_1, ad_0, ad_1,
    w_hbm, par, mom, var,
    recv, avg, mix_o, gin_o,
    g_s, x_b, w_b, a_b, q_b, u_t, d_s, d_t, dh, dq, do_s, acc, out, inbox, st_m, st_a, st_0m, st_0a,
    p_b, p_in, opt, gsum, diff, box, own_avg,
    xsem, wsem, asem, ce_s, ce_r, os_s, os_r, loc, pe_s, pe_r, ro_s, ro_r, rl, osem,
    as_s, as_r, bs_s, bs_r, bl,
):
    grp, dp, mp = lax.axis_index("grp"), lax.axis_index("dp"), lax.axis_index("mp")
    rows, cols = par.shape[1], par.shape[2]
    quarter = mix_o.shape[0]
    share = share_rows(rows, n_grp)
    star = 1 + lax.rem(dp, 2)
    is_mid = jnp.logical_or(mp == 1, mp == 2)
    is_outer = jnp.logical_not(is_mid)
    is_main = mp == star
    is_second = jnp.logical_and(is_mid, mp != star)
    other_mid = 3 - mp
    near_outer = jnp.where(mp == 1, 0, 3)
    far_outer = 3 - near_outer
    heads = 3
    hw = heads * HD
    xs, qo, ad = (xs_0, xm_0, xs_1, xm_1), (qo_0, qo_1), (ad_0, ad_1)
    mate = (grp, flip(dp, 1), mp)
    barrier = pltpu.get_barrier_semaphore()

    def at_mp(where):
        return (grp, dp, where)

    def at_grp(step):
        return (lax.rem(grp + step, n_grp), dp, mp)

    def at_dp(step):
        return (grp, lax.rem(dp + step, n_dp), mp)

    def greet(devices):
        for device in devices:
            pl.semaphore_signal(barrier, inc=1, device_id=device, device_id_type=MESH_ID)
        pl.semaphore_wait(barrier, len(devices))

    peers = [at_grp(step) for step in range(1, n_grp)]

    @pl.when(is_mid)
    def _():
        greet(
            [at_mp(0), at_mp(3), at_mp(other_mid)] + peers + [at_dp(step) for step in range(1, n_dp)]
        )

    @pl.when(is_outer)
    def _():
        greet([at_mp(1), at_mp(2)] + peers)

    def remote(src, dst, send, receive, device):
        return pltpu.make_async_remote_copy(
            src_ref=src, dst_ref=dst, send_sem=send, recv_sem=receive,
            device_id=device, device_id_type=MESH_ID,
        )

    def layer_of(sub):
        return 1 - sub // 2

    def width_of(sub):
        return 2 * D if sub % 2 == 0 else D

    def cols_of(sub):
        return slice(D, cols) if sub % 2 == 0 else slice(0, D)

    def slot_of(step):
        return 3 - step % 4

    def stage(step):
        sub, slot = step // 4, slot_of(step)
        if slot == 0:
            return st_0m if sub % 2 == 0 else st_0a
        return (st_m if sub % 2 == 0 else st_a).at[layer_of(sub), slot - 1]

    def loads(step):
        sub, slot, place = step // 4, slot_of(step), step % 2
        layer, width = layer_of(sub), width_of(sub)
        result = [
            pltpu.make_async_copy(
                w_hbm.at[layer, slot, :, cols_of(sub)], w_b.at[place, :, :width], wsem.at[place]
            )
        ]
        if sub % 2 == 0:
            result.append(pltpu.make_async_copy(ad[layer].at[slot], a_b.at[place], asem.at[place]))
        else:
            result.append(pltpu.make_async_copy(qo[layer].at[slot], q_b.at[place], asem.at[place]))
        return result

    def x_load(sub):
        source = xs[2 * layer_of(sub) + (1 if sub % 2 == 0 else 0)]
        return pltpu.make_async_copy(source, x_b.at[sub % 2], xsem.at[sub % 2])

    def exchange(step, arrive):
        width, place = width_of(step // 4), step % 2
        result = []
        for hop in range(1, n_dp):
            target = lax.rem(dp + hop, n_dp)
            result.append(
                remote(
                    out.at[place, pl.ds(pl.multiple_of(target * rows, rows), rows), :width],
                    inbox.at[place, hop - 1, :, :width],
                    ce_s.at[step, hop - 1], ce_r.at[step, hop - 1], at_dp(hop),
                )
            )
        return result

    def to_owner(step, slot):
        sub = step // 4
        plane = 1 if slot >= 2 else 0
        place = recv.at[plane, layer_of(sub), :, cols_of(sub)]
        if slot == 0:
            return pltpu.make_async_copy(stage(step), place, loc.at[sub])
        device = at_mp((None, near_outer, other_mid, far_outer)[slot])
        return remote(stage(step), place, os_s.at[step], os_r.at[sub, plane], device)

    def owner_arrival(sub, plane):
        place = recv.at[plane, layer_of(sub), :, cols_of(sub)]
        return remote(place, place, os_s.at[0], os_r.at[sub, plane], mate)

    def finish(step):
        width, place = width_of(step // 4), step % 2
        for copy in exchange(step, True):
            copy.wait_recv()
        target = stage(step)
        block = 96 if rows % 96 == 0 else rows
        for at in range(0, rows, block):
            mine = pl.ds(pl.multiple_of(dp * rows + at, 16), block)
            total = out[place, mine, :width].astype(f32)
            for hop in range(1, n_dp):
                total = total + inbox[place, hop - 1, at : at + block, :width].astype(f32)
            target[at : at + block, :] = total.astype(bf16)
        for copy in exchange(step, False):
            copy.wait_send()
        to_owner(step, slot_of(step)).start()

    def put_rows(which, values):
        for at in range(0, CAP, 256):
            p_b[at : at + 256, :] = mm(pick_t[at : at + 256, :], values, 1, 0).astype(bf16)

        @pl.when(is_second)
        def _():
            remote(p_b, p_in, pe_s.at[which], pe_r.at[which], mate).start()

    def quarter_of(index):
        return pl.ds(pl.multiple_of(index * quarter, quarter), quarter)

    def row_copies(which, dest):
        return [
            remote(
                p_b.at[quarter_of(index)], dest, ro_s.at[which, turn], ro_r.at[which], at_mp(index)
            )
            for turn, index in enumerate((other_mid, 0, 3))
        ]

    def send_rows(which, dest):
        @pl.when(is_main)
        def _():
            remote(p_b, p_in, pe_s.at[which], pe_r.at[which], mate).wait_recv()
            for at in range(0, CAP, 256):
                span = slice(at, at + 256)
                p_b[span, :] = p_b[span, :] + p_in[span, :]
            for copy in row_copies(which, dest):
                copy.start()
            pltpu.make_async_copy(p_b.at[quarter_of(mp)], dest, rl.at[which]).start()

    def end_rows(which, dest):
        @pl.when(is_main)
        def _():
            for copy in row_copies(which, dest):
                copy.wait_send()
            pltpu.make_async_copy(p_b.at[quarter_of(mp)], dest, rl.at[which]).wait()

        @pl.when(is_second)
        def _():
            remote(p_b, p_in, pe_s.at[which], pe_r.at[which], mate).wait_send()

    def rows_arrived(which, dest):
        @pl.when(jnp.logical_not(is_main))
        def _():
            remote(
                p_b.at[quarter_of(0)], dest, ro_s.at[which, 0], ro_r.at[which], at_mp(0)
            ).wait_recv()

    def piece_place(piece):
        layer, at = piece
        return layer, slice(at, at + PIECE), layer * (cols // PIECE) + at // PIECE

    def diff_piece(piece):
        layer, span, index = piece_place(piece)
        block = opt.shape[2]

        def block_loads(turn):
            part, place = slice(turn * block, (turn + 1) * block), turn % 2
            return [
                pltpu.make_async_copy(source.at[layer, part, span], opt.at[place, i], osem.at[place, i])
                for i, source in enumerate((par, mom, var))
            ] + [
                pltpu.make_async_copy(
                    recv.at[plane, layer, part, span], gsum.at[place, plane], osem.at[place, 3 + plane]
                )
                for plane in range(2)
            ]

        for copy in block_loads(0):
            copy.start()
        for turn in range(rows // block):
            part, place = slice(turn * block, (turn + 1) * block), turn % 2
            if (turn + 1) * block < rows:
                for copy in block_loads(turn + 1):
                    copy.start()
            for copy in block_loads(turn):
                copy.wait()
            grad = gsum[place, 0].astype(f32) + gsum[place, 1].astype(f32)
            one = beta_one * opt[place, 1] + (1 - beta_one) * grad
            two = beta_two * opt[place, 2] + (1 - beta_two) * grad * grad
            step = one / (1 - beta_one**STEP) / (jnp.sqrt(two / (1 - beta_two**STEP)) + adam_eps)
            diff[index, part, :] = (inner_rate * (step + decay_rate * opt[place, 0])).astype(bf16)
        for copy in first_copies(index):
            copy.start()

    def rows_for(where):
        if share == rows:
            return slice(0, rows)
        return pl.ds(pl.multiple_of(where * share, share), share)

    def first_copies(index):
        return [
            remote(
                diff.at[index, rows_for(lax.rem(grp + hop, n_grp))], box.at[index, hop - 1],
                as_s.at[index, hop - 1], as_r.at[index, hop - 1], at_grp(hop),
            )
            for hop in range(1, n_grp)
        ]

    def second_copies(piece):
        layer, span, index = piece_place(piece)
        place = avg.at[layer, rows_for(grp), span]
        return [
            remote(own_avg.at[index], place, bs_s.at[index, hop - 1], bs_r.at[index, hop - 1], at_grp(hop))
            for hop in range(1, n_grp)
        ]

    def second_arrivals(piece):
        layer, span, index = piece_place(piece)
        result = []
        for hop in range(1, n_grp):
            source = lax.rem(grp + n_grp - hop, n_grp)
            place = avg.at[layer, rows_for(source), span]
            result.append(
                remote(place, place, bs_s.at[index, hop - 1], bs_r.at[index, hop - 1], at_grp(hop))
            )
        return result

    def mean_piece(piece):
        layer, span, index = piece_place(piece)
        for copy in first_copies(index):
            copy.wait_recv()
        total = diff[index, rows_for(grp), :].astype(f32)
        for hop in range(1, n_grp):
            total = total + box[index, hop - 1].astype(f32)
        own_avg[index] = (total / n_grp).astype(bf16)
        pltpu.make_async_copy(own_avg.at[index], avg.at[layer, rows_for(grp), span], bl.at[index]).start()
        if share != rows:
            for copy in second_copies(piece):
                copy.start()

    def end_piece(piece):
        layer, span, index = piece_place(piece)
        for copy in first_copies(index):
            copy.wait_send()
        pltpu.make_async_copy(own_avg.at[index], avg.at[layer, rows_for(grp), span], bl.at[index]).wait()
        if share != rows:
            for copy in second_copies(piece):
                copy.wait_send()
            for copy in second_arrivals(piece):
                copy.wait_recv()

    def pieces_of(sub):
        span = cols_of(sub)
        return [(layer_of(sub), at) for at in range(span.start, span.stop, PIECE)]

    def diffs(sub):
        @pl.when(is_outer)
        def _():
            owner_arrival(sub, 0).wait_recv()

        @pl.when(is_mid)
        def _():
            to_owner(4 * sub + 3, 0).wait()

        owner_arrival(sub, 1).wait_recv()
        for piece in pieces_of(sub):
            diff_piece(piece)

    def means(sub):
        for piece in pieces_of(sub):
            mean_piece(piece)

    def mlp_start(sub):
        layer, place = layer_of(sub), sub % 2
        mod = mods.at[layer]
        x_load(sub).wait()
        for part in chunks():
            normed, _ = moments(x_b[place, part, :])
            shift = row_mod(clip[part, :], mod[3])
            scale = row_mod(clip[part, :], mod[4])
            u_t[:, part] = (normed * (1.0 + scale) + shift).T.astype(bf16)
            down = row_mod(clip[part, :], mod[5]) * g_s[part, :]
            d_s[part, :] = down.astype(bf16)
            d_t[:, part] = down.T.astype(bf16)
        acc[...] = jnp.zeros_like(acc)

    def mlp_step(step):
        place = step % 2
        for part in chunks():
            dact = mm(d_s[part, :], w_b[place, :, D:], 1, 0)
            dh[part, :] = (dact * a_b[place, 1, part, :].astype(f32)).astype(bf16)
        out[place, :, :D] = mm(u_t[...], dh[...], 1, 0).astype(bf16)
        out[place, :, D:] = mm(d_t[...], a_b[place, 0], 1, 0).astype(bf16)
        acc[...] += mm(w_b[place, :, :D], dh[...], 1, 1)

    def attn_start(sub):
        layer, place = layer_of(sub), sub % 2
        mod = mods.at[layer]
        x_load(sub).wait()
        for part in chunks():
            normed, _ = moments(x_b[place, part, :])
            shift = row_mod(clip[part, :], mod[0])
            scale = row_mod(clip[part, :], mod[1])
            u_t[:, part] = (normed * (1.0 + scale) + shift).T.astype(bf16)
            d_t[:, part] = (row_mod(clip[part, :], mod[2]) * g_s[part, :]).T.astype(bf16)
        acc[...] = jnp.zeros_like(acc)

    def attn_step(step):
        layer, place, slot = layer_of(step // 4), step % 2, slot_of(step)
        out[place, :, 3 * hw : D] = mm(d_t[...], q_b[place, 3 * hw :], 1, 1).astype(bf16)
        do_s[...] = mm(w_b[place, :, 3 * hw : D], d_t[...], 0, 0).astype(bf16)

        def head_step(head, carry):
            base = pl.multiple_of(head * HD, HD)
            keys_t = q_b[place, pl.ds(hw + base, HD), :]
            keys = keys_t.T
            values = q_b[place, pl.ds(2 * hw + base, HD), :].T
            dk = jnp.zeros((HD, ROWS), f32)
            dv = jnp.zeros((HD, ROWS), f32)
            for q0 in range(0, ROWS, 256):
                span = slice(q0, q0 + 256)
                query_t = q_b[place, pl.ds(base, HD), span]
                grad_t = do_s[pl.ds(base, HD), span]
                scores = mm(keys, query_t * jnp.asarray(0.125, bf16), 1, 0)
                allowed = idc[layer] == idr[layer, :, span]
                probs = jnp.where(
                    allowed, jnp.exp(scores - lse[layer, slot * heads + head, :, span]), 0.0
                )
                dv = dv + mm(grad_t, probs.astype(bf16), 1, 1)
                weighted = probs * mm(values, grad_t, 1, 0)
                delta = jnp.sum(weighted, axis=0, keepdims=True)
                ds = (weighted - probs * delta).astype(bf16)
                dq[pl.ds(base, HD), span] = (mm(keys_t, ds, 1, 0) * 0.125).astype(bf16)
                dk = dk + mm(query_t, ds, 1, 1)
            dq[pl.ds(hw + base, HD), :] = (dk * 0.125).astype(bf16)
            dq[pl.ds(2 * hw + base, HD), :] = dv.astype(bf16)
            return carry

        lax.fori_loop(0, heads, head_step, 0)
        out[place, :, : 3 * hw] = mm(u_t[...], dq[...], 1, 1).astype(bf16)
        acc[...] += mm(w_b[place, :, : 3 * hw], dq[...], 1, 0)

    def sub_end(sub):
        layer, place = layer_of(sub), sub % 2
        row = 4 if sub % 2 == 0 else 1
        for part in chunks():
            normed, inv_std = moments(x_b[place, part, :])
            scale = row_mod(clip[part, :], mods[layer, row])
            g_s[part, :] = g_s[part, :] + norm_back(acc[:, part].T * (1.0 + scale), normed, inv_std)

    @pl.when(is_mid)
    def _():
        x_load(0).start()
        for copy in loads(0):
            copy.start()
        g_s[...] = g_in[...]
        put_rows(0, xb[...])
        for step in range(16):
            sub = step // 4
            if step + 1 < 16:
                for copy in loads(step + 1):
                    copy.start()
            if step % 4 == 0:
                if sub < 3:
                    x_load(sub + 1).start()
                (mlp_start if sub % 2 == 0 else attn_start)(sub)
            for copy in loads(step):
                copy.wait()
            (mlp_step if sub % 2 == 0 else attn_step)(step)
            if step >= 2:
                finish(step - 1)
            for copy in exchange(step, True):
                copy.start()
            if step == 0:
                finish(0)
                send_rows(0, mix_o)
            if step % 4 == 3:
                sub_end(sub)
            if step == 9:
                diffs(0)
            if step == 11:
                means(0)
            if step == 14:
                diffs(1)
        end_rows(0, mix_o)
        put_rows(1, g_s[...].astype(bf16))
        finish(15)
        means(1)
        send_rows(1, gin_o)
        diffs(2)
        means(2)
        diffs(3)
        means(3)
        for step in range(16):
            if slot_of(step) != 0:
                to_owner(step, slot_of(step)).wait_send()
        end_rows(1, gin_o)

    @pl.when(is_outer)
    def _():
        for sub in range(4):
            diffs(sub)
            means(sub)

    for which, dest in ((0, mix_o), (1, gin_o)):
        rows_arrived(which, dest)
    for layer in range(L):
        for at in range(0, cols, PIECE):
            end_piece((layer, at))


def run_back(xb, pick_t, g, clip, idc, idr, mods, lse, xs, qo, ad, w, par, mom, var, quarter):
    sds = jax.ShapeDtypeStruct
    n_dp, n_grp = lax.axis_size("dp"), lax.axis_size("grp")
    rows, cols = par.shape[1], par.shape[2]
    share = share_rows(rows, n_grp)
    count = L * cols // PIECE
    far, peers = n_dp - 1, n_grp - 1
    block = 96 if rows % 96 == 0 else rows
    return pl.pallas_call(
        partial(back_kernel, n_dp, n_grp),
        out_shape=(
            sds((2, L, rows, cols), bf16), sds((L, rows, cols), bf16),
            sds((quarter, D), bf16), sds((quarter, D), bf16),
        ),
        in_specs=[vm_spec()] * 8 + [any_spec()] * 12,
        out_specs=(any_spec(),) * 4,
        scratch_shapes=[
            VM((ROWS, D), f32), VM((2, ROWS, D), f32), VM((2, D, 2 * D), bf16),
            VM((2, 2, ROWS, D), bf16), VM((2, D, ROWS), bf16),
            VM((D, ROWS), bf16), VM((ROWS, D), bf16), VM((D, ROWS), bf16), VM((ROWS, D), bf16),
            VM((9 * HD, ROWS), bf16), VM((3 * HD, ROWS), bf16), VM((D, ROWS), f32),
            VM((2, D, 2 * D), bf16), VM((2, far, rows, 2 * D), bf16),
            VM((L, 3, rows, 2 * D), bf16), VM((L, 3, rows, D), bf16),
            VM((rows, 2 * D), bf16), VM((rows, D), bf16),
            VM((CAP, D), bf16), VM((CAP, D), bf16),
            VM((2, 3, block, PIECE), f32), VM((2, 2, block, PIECE), bf16),
            VM((count, rows, PIECE), bf16), VM((count, peers, share, PIECE), bf16),
            VM((count, share, PIECE), bf16),
            DMA((2,)), DMA((2,)), DMA((2,)), DMA((16, far)), DMA((16, far)), DMA((16,)), DMA((4, 2)),
            DMA((4,)), DMA((2,)), DMA((2,)), DMA((2, 3)), DMA((2,)), DMA((2,)), DMA((2, 5)),
            DMA((count, peers)), DMA((count, peers)), DMA((count, peers)), DMA((count, peers)),
            DMA((count,)),
        ],
        compiler_params=pltpu.CompilerParams(
            collective_id=2, has_side_effects=True, vmem_limit_bytes=63 * MIB
        ),
    )(xb, pick_t, g, clip, idc, idr, mods, lse, *xs, *qo, *ad, w, par, mom, var)


def last_kernel(par, mom, var, out_mom, ga, gb, avg, new_m, new_v, out_a, out_m, out_w, out_l):
    grad = ga[...].astype(f32) + gb[...].astype(f32)
    new_m[...] = beta_one * mom[...] + (1 - beta_one) * grad
    new_v[...] = beta_two * var[...] + (1 - beta_two) * grad * grad
    average = avg[...].astype(f32)
    momentum = outer_mu * out_mom[...] + average
    updated = par[...] - outer_rate * (average + outer_mu * momentum)
    out_a[...] = average
    out_m[...] = momentum
    out_w[...] = updated
    out_l[...] = updated.astype(bf16)


def run_last(par, mom, var, out_mom, recv, avg):
    rows, cols = par.shape[1], par.shape[2]
    block = 96 if rows % 96 == 0 else rows
    sds = jax.ShapeDtypeStruct
    full = pl.BlockSpec((None, block, cols), lambda i, j: (i, j, 0))

    def plane(which):
        return pl.BlockSpec((None, None, block, cols), lambda i, j: (which, i, j, 0))

    return pl.pallas_call(
        last_kernel,
        grid=(L, rows // block),
        out_shape=(sds(par.shape, f32),) * 5 + (sds(par.shape, bf16),),
        in_specs=[full] * 4 + [plane(0), plane(1), full],
        out_specs=(full,) * 6,
        compiler_params=pltpu.CompilerParams(vmem_limit_bytes=48 * MIB),
    )(par, mom, var, out_mom, recv, recv, avg)


def body(
    tokens, cotangent, modulation, clip_frames, clip_patches, params, first_moment, second_moment,
    outer_momentum,
):
    dp, mp = lax.axis_index("dp"), lax.axis_index("mp")
    quarter = tokens.shape[1]
    mod_cols = modulation.shape[2]
    star = 1 + lax.rem(dp, 2)
    is_mid = jnp.logical_or(mp == 1, mp == 2)
    flag = is_mid.astype(jnp.int32)[None]

    meta = jnp.concatenate(
        [
            modulation[0],
            clip_frames[0].astype(f32)[:, None],
            clip_patches[0].astype(f32)[:, None],
            jnp.zeros((SLOTS, 126), f32),
        ],
        axis=1,
    )
    tok_all, cot_all, meta_all, w = gather_all(tokens[0], cotangent[0], meta, params.astype(bf16))

    mods = meta_all[:, :mod_cols].reshape(SLOTS, L, 6, D).transpose(1, 2, 0, 3)
    frames, patches = meta_all[:, mod_cols], meta_all[:, mod_cols + 1]
    pos, live, clip, space_id, time_id = slot_meta(frames, patches, mp == star)
    every = jnp.arange(CAP, dtype=jnp.int32)
    pick = ((pos[:, None] == every[None, :]) & live[:, None]).astype(bf16)
    pick_t = ((pos[None, :] == every[:, None]) & live[None, :]).astype(bf16)
    clip = clip[:, None]
    ids = jnp.stack([space_id, time_id])

    x = jnp.dot(pick, tok_all, preferred_element_type=f32)
    gradient = jnp.dot(pick, cot_all, preferred_element_type=f32)
    xs, qos, ads, lses = [], [], [], []
    for layer in range(L):
        x1, qo, lse = run_attn_fwd(
            layer, flag, x, clip, ids[layer % 2][:, None], ids[layer % 2][None, :], mods[layer], w
        )
        x2, ad = run_mlp_fwd(layer, flag, x1, clip, mods[layer], w)
        xs += [x, x1]
        qos.append(qo)
        ads.append(ad)
        lses.append(lse)
        x = x2
    recv, avg, mixed_rows, grad_rows = run_back(
        x.astype(bf16), pick_t, gradient, clip, ids[:, :, None], ids[:, None, :], mods,
        jnp.stack(lses), xs, qos, ads, w, params, first_moment[0], second_moment[0], quarter,
    )
    total = jnp.sum(clip_frames[0] * clip_patches[0])
    own_live = (mp * quarter + jnp.arange(quarter, dtype=jnp.int32) < total)[:, None]
    mixed = jnp.where(own_live, mixed_rows, tokens[0])
    input_grad = jnp.where(own_live, grad_rows.astype(f32), 0.0)
    new_m, new_v, average, momentum, updated, low = run_last(
        params, first_moment[0], second_moment[0], outer_momentum, recv, avg
    )
    return (
        mixed[None], input_grad[None], new_m[None], new_v[None], average, momentum, updated, low,
    )


def solution(mesh):
    in_specs = (
        P("grp", ("dp", "mp"), None),
        P("grp", ("dp", "mp"), None),
        P("grp", "dp", None),
        P("grp", "dp"),
        P("grp", "dp"),
        P(None, "dp", "mp"),
        P("grp", None, "dp", "mp"),
        P("grp", None, "dp", "mp"),
        P(None, "dp", "mp"),
    )
    out_specs = (
        P("grp", ("dp", "mp"), None),
        P("grp", ("dp", "mp"), None),
        P("grp", None, "dp", "mp"),
        P("grp", None, "dp", "mp"),
        P(None, "dp", "mp"),
        P(None, "dp", "mp"),
        P(None, "dp", "mp"),
        P(None, "dp", "mp"),
    )
    return jax.shard_map(body, mesh=mesh, in_specs=in_specs, out_specs=out_specs, check_vma=False)
```

```python
from functools import partial

import jax
import jax.numpy as jnp
from jax import lax
from jax.experimental import pallas as pl
from jax.experimental.pallas import tpu as pltpu
from jax.sharding import PartitionSpec as P

D = 768
HEADS = 12
HD = 64
FF = 3072
L = 2
STEP = 5
CAP = 1024
SLOTS = 4
LONGF = 64
ROWS = CAP // 2
CHUNK = 128
PIECE = 768
SIDE = PIECE // 2

ln_eps = 1e-06
neg_fill = -1e30
beta_one = 0.9
beta_two = 0.999
adam_eps = 1e-08
inner_rate = 0.04
decay_rate = 0.1
outer_rate = 0.7
outer_mu = 0.5

f32 = jnp.float32
bf16 = jnp.bfloat16
VM = pltpu.VMEM
DMA = pltpu.SemaphoreType.DMA
MESH_ID = pl.DeviceIdType.MESH
MIB = 2**20
HEADS_DEV = 3
HW = HEADS_DEV * HD


def mm(left, right, lc, rc):
    return lax.dot_general(left, right, (((lc,), (rc,)), ((), ())), preferred_element_type=f32)


def moments(values):
    centered = values - jnp.mean(values, axis=-1, keepdims=True)
    inv_std = lax.rsqrt(jnp.mean(centered * centered, axis=-1, keepdims=True) + ln_eps)
    return centered * inv_std, inv_std


def norm_back(grad_normed, normed, inv_std):
    inner = grad_normed - jnp.mean(grad_normed, axis=-1, keepdims=True)
    inner = inner - normed * jnp.mean(grad_normed * normed, axis=-1, keepdims=True)
    return inv_std * inner


def row_mod(clip_col, mods, layer, kind):
    base = (layer * 6 + kind) * D
    table = mods[:, base : base + D]
    total = jnp.where(clip_col == 0.0, table[0:1, :], 0.0)
    for clip in range(1, SLOTS):
        total = total + jnp.where(clip_col == float(clip), table[clip : clip + 1, :], 0.0)
    return total


def chunks():
    return [slice(at, at + CHUNK) for at in range(0, ROWS, CHUNK)]


def any_spec():
    return pl.BlockSpec(memory_space=pl.ANY)


def vm_spec():
    return pl.BlockSpec(memory_space=VM)


def flip(index, bit):
    return index + bit - 2 * bit * lax.rem(index // bit, 2)


def slot_meta(small, index, long_core):
    frames = [small[0:1, clip : clip + 1] for clip in range(SLOTS)]
    patches = [small[1:2, clip : clip + 1] for clip in range(SLOTS)]
    zero = jnp.zeros_like(frames[0])
    start, long_start, long_size = zero, zero, zero
    starts, ends = [], []
    for clip in range(SLOTS):
        size = frames[clip] * patches[clip]
        is_long = frames[clip] == float(LONGF)
        long_start = long_start + jnp.where(is_long, start, 0.0)
        long_size = long_size + jnp.where(is_long, size, 0.0)
        starts.append(start)
        start = start + size
        ends.append(start)
    pos_long = index + long_start
    pos_short = jnp.where(index < long_start, index, index + long_size)
    pos = jnp.where(long_core, pos_long, pos_short)
    clip_of = jnp.zeros_like(index)
    for clip in range(SLOTS):
        clip_of = clip_of + jnp.where(pos >= ends[clip], 1.0, 0.0)
    limit = jnp.where(long_core, long_start + long_size, start)
    live = pos < limit
    clip_of = jnp.where(live, clip_of, float(SLOTS))
    begin, width = jnp.zeros_like(index), jnp.ones_like(index)
    for clip in range(SLOTS):
        hit = clip_of == float(clip)
        begin = jnp.where(hit, starts[clip], begin)
        width = jnp.where(hit, patches[clip], width)
    offset = pos - begin
    frame = jnp.floor((offset + 0.5) / width)
    patch = offset - frame * width
    space_id = jnp.where(live, clip_of * CAP + frame, -1.0 - index)
    time_id = jnp.where(live, clip_of * CAP + patch, -1.0 - index)
    return jnp.where(live, pos, -1.0), clip_of, space_id, time_id


def remote(src, dst, send, receive, device):
    return pltpu.make_async_remote_copy(
        src_ref=src, dst_ref=dst, send_sem=send, recv_sem=receive,
        device_id=device, device_id_type=MESH_ID,
    )


def greet(devices):
    barrier = pltpu.get_barrier_semaphore()
    for device in devices:
        pl.semaphore_signal(barrier, inc=1, device_id=device, device_id_type=MESH_ID)
    pl.semaphore_wait(barrier, len(devices))


def fwd_kernel(
    n_dp, tok, cot, mod_in, small_in, par,
    w_o, xs_o, qo_o, ad_o, lse_o, g_o, xb_o, clip_o, idc_o, idr_o, pos_o, mod_o,
    w_v, wb, par_f, t_v, c_v, x_v, u_s, acc, qo_v, ad_v, small_v,
    zs, zr, gs, gr, ds, dr, os_s, os_r, ts, tr, cs, cr, tl, ms, mr, psem, wsem, xsem, qsem, asem,
):
    grp, dp, mp = lax.axis_index("grp"), lax.axis_index("dp"), lax.axis_index("mp")
    rows, cols = par.shape[1], par.shape[2]
    quarter = tok.shape[0]
    pieces = [(layer, at) for layer in range(L) for at in range(0, cols, PIECE)]
    count = len(pieces)
    star = 1 + lax.rem(dp, 2)
    is_mid = jnp.logical_or(mp == 1, mp == 2)
    is_outer = jnp.logical_not(is_mid)
    is_main = mp == star
    is_second = jnp.logical_and(is_mid, mp != star)
    other_mid = 3 - mp
    near = jnp.where(mp == 0, 1, 2)
    far = 3 - near
    my_rows = pl.ds(pl.multiple_of(dp * rows, rows), rows)
    mate = (grp, flip(dp, 1), mp)
    hops = range(1, n_dp)

    def at_mp(where):
        return (grp, dp, where)

    def at_grp(bit):
        return (flip(grp, bit), dp, mp)

    def at_dp(step):
        return (grp, lax.rem(dp + step, n_dp), mp)

    @pl.when(is_mid)
    def _():
        greet(
            [at_mp(0), at_mp(3), at_mp(other_mid), at_grp(1), at_grp(2)] + [at_dp(hop) for hop in hops]
        )

    @pl.when(is_outer)
    def _():
        greet([at_mp(1), at_mp(2)])

    def bit_of(k, slot):
        return 1 + (k + slot) % 2

    def half(k, slot, mine):
        index = lax.rem(grp // bit_of(k, slot), 2)
        if not mine:
            index = 1 - index
        return pl.ds(pl.multiple_of(index * SIDE, 128), SIDE)

    def z_copy(k, slot, device):
        span = half(k, slot, True)
        return remote(
            wb.at[k, :, span], w_v.at[k, slot, my_rows, span], zs.at[k, slot - 1], zr.at[k, slot - 1], device
        )

    def g_copy(k, slot):
        place = w_v.at[k, slot, my_rows, half(k, slot, True)]
        return remote(place, place, gs.at[k, slot - 1], gr.at[k, slot - 1], at_grp(bit_of(k, slot)))

    def d_copies(k, slot, mine):
        place, turn = w_v.at[k, slot, my_rows, half(k, slot, mine)], 0 if mine else 1
        return [
            remote(
                place, place, ds.at[k, slot - 1, turn, hop - 1], dr.at[k, slot - 1, turn, hop - 1], at_dp(hop)
            )
            for hop in hops
        ]

    def rows_of(hop):
        source = lax.rem(dp + n_dp - hop, n_dp)
        return pl.ds(pl.multiple_of(source * rows, rows), rows)

    def d_arrivals(k, slot, mine):
        turn = 0 if mine else 1
        result = []
        for hop in hops:
            place = w_v.at[k, slot, rows_of(hop), half(k, slot, mine)]
            result.append(
                remote(
                    place, place, ds.at[k, slot - 1, turn, hop - 1], dr.at[k, slot - 1, turn, hop - 1],
                    at_dp(hop),
                )
            )
        return result

    def own_copies(k):
        return [
            remote(wb.at[k], w_v.at[k, 0, my_rows], os_s.at[k, hop - 1], os_r.at[k, hop - 1], at_dp(hop))
            for hop in hops
        ]

    def own_arrivals(k):
        return [
            remote(
                wb.at[k], w_v.at[k, 0, rows_of(hop)], os_s.at[k, hop - 1], os_r.at[k, hop - 1], at_dp(hop)
            )
            for hop in hops
        ]

    def part(ref, index):
        return ref.at[pl.ds(pl.multiple_of(index * quarter, quarter), quarter)]

    def route(src, out, send, receive):
        return remote(src, part(out, mp), send.at[0], receive.at[mp], at_mp(star))

    def pass_on(out, send, receive, index):
        return remote(part(out, index), part(out, index), send.at[1 + index], receive.at[4 + index], mate)

    def main_arrival(out, send, receive, index):
        return remote(part(out, index), part(out, index), send.at[0], receive.at[index], mate)

    def second_arrival(out, send, receive, index):
        return remote(part(out, index), part(out, index), send.at[0], receive.at[4 + index], mate)

    routes = ((tok, t_v, ts, tr), (cot, c_v, cs, cr))

    def keep(which):
        src, out = routes[which][:2]
        return pltpu.make_async_copy(src, part(out, mp), tl.at[which])

    def collect(which):
        out, send, receive = routes[which][1:]

        @pl.when(is_main)
        def _():
            keep(which).wait()
            pass_on(out, send, receive, mp).start()
            for index in (other_mid, 0, 3):
                main_arrival(out, send, receive, index).wait_recv()
                pass_on(out, send, receive, index).start()

        @pl.when(is_second)
        def _():
            for index in range(4):
                second_arrival(out, send, receive, index).wait_recv()

    def meta_copies():
        return [
            remote(mod_in, mod_o, ms.at[0], mr.at[0], mate),
            remote(small_in, small_v, ms.at[1], mr.at[1], mate),
        ]

    def par_load(k):
        layer, at = pieces[k]
        return pltpu.make_async_copy(par.at[layer, :, at : at + PIECE], par_f.at[k % 2], psem.at[k % 2])

    def cast_piece(k):
        if k == 0:
            par_load(0).start()
        if k + 1 < count:
            par_load(k + 1).start()
        par_load(k).wait()
        block = 96 if rows % 96 == 0 else rows
        for at in range(0, rows, block):
            wb[k, at : at + block, :] = par_f[k % 2, at : at + block, :].astype(bf16)

    def keep_own(k):
        block = 96 if rows % 96 == 0 else rows
        for at in range(0, rows, block):
            spot = pl.ds(pl.multiple_of(dp * rows + at, 16), block)
            w_v[k, 0, spot, :] = wb[k, at : at + block, :]

    def w_out(k, slot):
        return pltpu.make_async_copy(w_v.at[k, slot], w_o.at[k, slot], wsem.at[k, slot])

    def x_out(turn):
        return pltpu.make_async_copy(x_v.at[turn % 2], xs_o.at[turn], xsem.at[turn])

    def qo_out(layer, slot):
        return pltpu.make_async_copy(qo_v.at[slot % 2], qo_o.at[layer, slot], qsem.at[slot % 2])

    def ad_out(layer, slot):
        return pltpu.make_async_copy(ad_v.at[slot % 2], ad_o.at[layer, slot], asem.at[slot % 2])

    def serve_z(k):
        for slot in (1, 2, 3):
            z_copy(k, slot, at_mp(other_mid)).wait_recv()
            g_copy(k, slot).start()
            for copy in d_copies(k, slot, True):
                copy.start()
        if k + 2 < count:
            z_copy(k, 2, at_mp(other_mid)).wait_send()
            z_copy(k + 2, 2, at_mp(other_mid)).start()

    def serve_g(k):
        for slot in (1, 2, 3):
            g_copy(k, slot).wait_recv()
            for copy in d_copies(k, slot, False):
                copy.start()

    def ready(k, slot):
        if slot == 0:
            for copy in own_arrivals(k):
                copy.wait_recv()
        else:
            for mine in (True, False):
                for copy in d_arrivals(k, slot, mine):
                    copy.wait_recv()
        w_out(k, slot).start()

    def lifted(layer, kind, turn):
        for span in chunks():
            normed, _ = moments(x_v[turn % 2, span, :])
            shift = row_mod(clip_o[span, :], mod_o, layer, kind)
            scale = row_mod(clip_o[span, :], mod_o, layer, kind + 1)
            u_s[span, :] = (normed * (1.0 + scale) + shift).astype(bf16)
        acc[...] = jnp.zeros_like(acc)

    def add_branch(layer, kind, turn):
        if turn >= 2:
            x_out(turn - 2).wait()
        for span in chunks():
            gate = row_mod(clip_o[span, :], mod_o, layer, kind)
            x_v[turn % 2, span, :] = x_v[1 - turn % 2, span, :] + gate * acc[:, span].T

    def attn_unit(layer, slot):
        k, place = layer * (cols // PIECE), slot % 2
        ready(k, slot)
        if slot >= 2:
            qo_out(layer, slot - 2).wait()
        qo = qo_v.at[place]
        qo[: 3 * HW, :] = mm(u_s[...], w_v[k, slot, :, : 3 * HW], 1, 0).T.astype(bf16)

        def head_step(head, carry):
            base = pl.multiple_of(head * HD, HD)
            keys = qo[pl.ds(HW + base, HD), :].T
            value_t = qo[pl.ds(2 * HW + base, HD), :]
            for q0 in range(0, ROWS, 256):
                span = slice(q0, q0 + 256)
                query_t = qo[pl.ds(base, HD), span]
                scores = mm(keys, query_t * jnp.asarray(0.125, bf16), 1, 0)
                allowed = idc_o[layer] == idr_o[layer, :, span]
                scores = jnp.where(allowed, scores, neg_fill)
                top = jnp.max(scores, axis=0, keepdims=True)
                raw = jnp.exp(scores - top)
                total = jnp.sum(raw, axis=0, keepdims=True)
                probs = (raw / total).astype(bf16)
                qo[pl.ds(3 * HW + base, HD), span] = mm(value_t, probs, 1, 0).astype(bf16)
                lse_o[layer, slot * HEADS_DEV + head, :, span] = top + jnp.log(total)
            return carry

        lax.fori_loop(0, HEADS_DEV, head_step, 0)
        acc[...] += mm(w_v[k, slot, :, 3 * HW :], qo[3 * HW :, :], 1, 0)
        qo_out(layer, slot).start()

    def mlp_unit(layer, slot):
        k, place = layer * (cols // PIECE) + 1, slot % 2
        ready(k, slot)
        ready(k + 1, slot)
        if slot >= 2:
            ad_out(layer, slot - 2).wait()
        for span in chunks():
            hid = mm(u_s[span, :], w_v[k, slot], 1, 0)
            cdf = 0.5 * (1.0 + lax.erf(hid * 0.7071067811865476))
            pdf = jnp.exp(-0.5 * hid * hid) * 0.3989422804014327
            ad_v[place, 0, span, :] = (hid * cdf).astype(bf16)
            ad_v[place, 1, span, :] = (cdf + hid * pdf).astype(bf16)
        acc[...] += mm(w_v[k + 1, slot], ad_v[place, 0], 1, 1)
        ad_out(layer, slot).start()

    @pl.when(jnp.logical_not(is_main))
    def _():
        route(tok, t_v, ts, tr).start()

    @pl.when(is_main)
    def _():
        keep(0).start()
        keep(1).start()
        for copy in meta_copies():
            copy.start()

    @pl.when(is_outer)
    def _():
        for k in range(count):
            cast_piece(k)
            if k == 0:
                route(tok, t_v, ts, tr).wait_send()
            if k >= 2:
                z_copy(k - 2, 1, at_mp(near)).wait_send()
                z_copy(k - 2, 3, at_mp(far)).wait_send()
            z_copy(k, 1, at_mp(near)).start()
            z_copy(k, 3, at_mp(far)).start()
        for k in range(count - 2, count):
            z_copy(k, 1, at_mp(near)).wait_send()
            z_copy(k, 3, at_mp(far)).wait_send()
        route(cot, c_v, cs, cr).start()
        route(cot, c_v, cs, cr).wait_send()

    @pl.when(is_mid)
    def _():
        for k in range(count):
            cast_piece(k)
            for copy in own_copies(k):
                copy.start()
            if k == 0:
                pl.when(is_second)(lambda: route(tok, t_v, ts, tr).wait_send())
            if k < 2:
                z_copy(k, 2, at_mp(other_mid)).start()
            keep_own(k)

        @pl.when(is_main)
        def _():
            mod_o[...] = mod_in[...]
            small_v[...] = small_in[...]

        @pl.when(is_second)
        def _():
            for copy in meta_copies():
                copy.wait_recv()

        column = lax.broadcasted_iota(jnp.int32, (ROWS, 1), 0).astype(f32)
        line = lax.broadcasted_iota(jnp.int32, (1, ROWS), 1).astype(f32)
        small = small_v[...]
        pos_c, clip_c, space_c, time_c = slot_meta(small, column, is_main)
        clip_o[...] = clip_c
        idc_o[0] = space_c
        idc_o[1] = time_c
        pos_r, _, space_r, time_r = slot_meta(small, line, is_main)
        idr_o[0] = space_r
        idr_o[1] = time_r
        pos_o[...] = pos_r
        collect(0)
        for span in chunks():
            hit = pos_c[span, :] == lax.broadcasted_iota(jnp.int32, (CHUNK, CAP), 1).astype(f32)
            x_v[0, span, :] = mm(jnp.where(hit, 1.0, 0.0).astype(bf16), t_v[...], 1, 0)
        x_out(0).start()

        lifted(0, 0, 0)
        attn_unit(0, 0)
        serve_z(0)
        serve_g(0)
        attn_unit(0, 1)
        serve_z(1)
        attn_unit(0, 2)
        serve_g(1)
        attn_unit(0, 3)
        add_branch(0, 2, 1)
        x_out(1).start()
        lifted(0, 3, 1)
        serve_z(2)
        mlp_unit(0, 0)
        serve_g(2)
        mlp_unit(0, 1)
        mlp_unit(0, 2)
        serve_z(3)
        mlp_unit(0, 3)
        add_branch(0, 5, 2)
        x_out(2).start()
        lifted(1, 0, 2)
        serve_g(3)
        qo_out(0, 2).wait()
        qo_out(0, 3).wait()
        attn_unit(1, 0)
        serve_z(4)
        attn_unit(1, 1)
        serve_g(4)
        attn_unit(1, 2)
        pl.when(is_second)(lambda: route(cot, c_v, cs, cr).start())
        serve_z(5)
        attn_unit(1, 3)
        serve_g(5)
        add_branch(1, 2, 3)
        x_out(3).start()
        lifted(1, 3, 3)
        ad_out(0, 2).wait()
        ad_out(0, 3).wait()
        for slot in range(4):
            mlp_unit(1, slot)
        collect(1)
        for span in chunks():
            gate = row_mod(clip_o[span, :], mod_o, 1, 5)
            xb_o[span, :] = (x_v[1, span, :] + gate * acc[:, span].T).astype(bf16)
            hit = pos_c[span, :] == lax.broadcasted_iota(jnp.int32, (CHUNK, CAP), 1).astype(f32)
            g_o[span, :] = mm(jnp.where(hit, 1.0, 0.0).astype(bf16), c_v[...], 1, 0)
        x_out(2).wait()
        x_out(3).wait()
        for slot in (2, 3):
            qo_out(1, slot).wait()
            ad_out(1, slot).wait()
        for k in range(count):
            for copy in own_copies(k):
                copy.wait_send()
            for slot in range(4):
                w_out(k, slot).wait()
            for slot in (1, 2, 3):
                g_copy(k, slot).wait_send()
                for mine in (True, False):
                    for copy in d_copies(k, slot, mine):
                        copy.wait_send()
        for k in range(count - 2, count):
            z_copy(k, 2, at_mp(other_mid)).wait_send()

    @pl.when(is_main)
    def _():
        for copy in meta_copies():
            copy.wait_send()
        for src, out, send, receive in routes:
            for index in range(4):
                pass_on(out, send, receive, index).wait_send()

    @pl.when(is_second)
    def _():
        route(cot, c_v, cs, cr).wait_send()


def run_forward(tok, cot, mod, small, par):
    sds = jax.ShapeDtypeStruct
    n_dp = lax.axis_size("dp")
    rows, cols = par.shape[1], par.shape[2]
    count = L * cols // PIECE
    peers = n_dp - 1
    return pl.pallas_call(
        partial(fwd_kernel, n_dp),
        out_shape=(
            sds((count, 4, D, PIECE), bf16), sds((2 * L, ROWS, D), f32), sds((L, 4, D, ROWS), bf16),
            sds((L, 4, 2, ROWS, FF // 4), bf16), sds((L, HEADS, 1, ROWS), f32), sds((ROWS, D), f32),
            sds((ROWS, D), bf16), sds((ROWS, 1), f32), sds((2, ROWS, 1), f32), sds((2, 1, ROWS), f32),
            sds((1, ROWS), f32), sds(mod.shape, f32),
        ),
        in_specs=[any_spec(), any_spec(), vm_spec(), vm_spec(), any_spec()],
        out_specs=(any_spec(),) * 4 + (vm_spec(),) * 8,
        scratch_shapes=[
            VM((count, 4, D, PIECE), bf16), VM((count, rows, PIECE), bf16), VM((2, rows, PIECE), f32),
            VM((CAP, D), bf16), VM((CAP, D), bf16), VM((2, ROWS, D), f32), VM((ROWS, D), bf16),
            VM((D, ROWS), f32), VM((2, D, ROWS), bf16), VM((2, 2, ROWS, FF // 4), bf16), VM((8, 128), f32),
            DMA((count, 3)), DMA((count, 3)), DMA((count, 3)), DMA((count, 3)),
            DMA((count, 3, 2, peers)), DMA((count, 3, 2, peers)), DMA((count, peers)), DMA((count, peers)),
            DMA((5,)), DMA((8,)), DMA((5,)), DMA((8,)), DMA((2,)), DMA((2,)), DMA((2,)),
            DMA((2,)), DMA((count, 4)), DMA((2 * L,)), DMA((2,)), DMA((2,)),
        ],
        compiler_params=pltpu.CompilerParams(
            collective_id=1, has_side_effects=True, vmem_limit_bytes=63 * MIB
        ),
    )(tok, cot, mod, small, par)


def share_rows(rows, n_grp):
    part = rows // n_grp
    return part if part * n_grp == rows and part % 16 == 0 else rows


def back_kernel(
    n_dp, n_grp,
    xb, pos_r, g_in, clip, idc, idr, mods, lse, xs, qo, ad,
    w_hbm, par, mom, var,
    recv, avg, mix_o, gin_o,
    g_s, x_b, w_b, a_b, q_b, u_t, d_s, d_t, dh, dq, do_s, acc, out, inbox, st_m, st_a, st_0m, st_0a,
    p_b, p_in, opt, gsum, diff, box, own_avg,
    xsem, wsem, asem, ce_s, ce_r, os_s, os_r, loc, pe_s, pe_r, ro_s, ro_r, rl, osem,
    as_s, as_r, bs_s, bs_r, bl,
):
    grp, dp, mp = lax.axis_index("grp"), lax.axis_index("dp"), lax.axis_index("mp")
    rows, cols = par.shape[1], par.shape[2]
    quarter = mix_o.shape[0]
    share = share_rows(rows, n_grp)
    star = 1 + lax.rem(dp, 2)
    is_mid = jnp.logical_or(mp == 1, mp == 2)
    is_outer = jnp.logical_not(is_mid)
    is_main = mp == star
    is_second = jnp.logical_and(is_mid, mp != star)
    other_mid = 3 - mp
    near_outer = jnp.where(mp == 1, 0, 3)
    far_outer = 3 - near_outer
    heads = HEADS_DEV
    hw = HW
    mate = (grp, flip(dp, 1), mp)

    def at_mp(where):
        return (grp, dp, where)

    def at_grp(step):
        return (lax.rem(grp + step, n_grp), dp, mp)

    def at_dp(step):
        return (grp, lax.rem(dp + step, n_dp), mp)

    peers = [at_grp(step) for step in range(1, n_grp)]

    @pl.when(is_mid)
    def _():
        greet(
            [at_mp(0), at_mp(3), at_mp(other_mid)] + peers + [at_dp(step) for step in range(1, n_dp)]
        )

    @pl.when(is_outer)
    def _():
        greet([at_mp(1), at_mp(2)] + peers)

    def layer_of(sub):
        return 1 - sub // 2

    def width_of(sub):
        return 2 * D if sub % 2 == 0 else D

    def cols_of(sub):
        return slice(D, cols) if sub % 2 == 0 else slice(0, D)

    def slot_of(step):
        return 3 - step % 4

    def stage(step):
        sub, slot = step // 4, slot_of(step)
        if slot == 0:
            return st_0m if sub % 2 == 0 else st_0a
        return (st_m if sub % 2 == 0 else st_a).at[layer_of(sub), slot - 1]

    def loads(step):
        sub, slot, place = step // 4, slot_of(step), step % 2
        layer, width = layer_of(sub), width_of(sub)
        first = layer * (cols // PIECE) + (1 if sub % 2 == 0 else 0)
        result = [
            pltpu.make_async_copy(
                w_hbm.at[first + turn, slot], w_b.at[place, :, turn * D : turn * D + D], wsem.at[place, turn]
            )
            for turn in range(width // D)
        ]
        if sub % 2 == 0:
            result.append(pltpu.make_async_copy(ad.at[layer, slot], a_b.at[place], asem.at[place]))
        else:
            result.append(pltpu.make_async_copy(qo.at[layer, slot], q_b.at[place], asem.at[place]))
        return result

    def x_load(sub):
        source = xs.at[2 * layer_of(sub) + (1 if sub % 2 == 0 else 0)]
        return pltpu.make_async_copy(source, x_b.at[sub % 2], xsem.at[sub % 2])

    def exchange(step, arrive):
        width, place = width_of(step // 4), step % 2
        result = []
        for hop in range(1, n_dp):
            target = lax.rem(dp + hop, n_dp)
            result.append(
                remote(
                    out.at[place, pl.ds(pl.multiple_of(target * rows, rows), rows), :width],
                    inbox.at[place, hop - 1, :, :width],
                    ce_s.at[step, hop - 1], ce_r.at[step, hop - 1], at_dp(hop),
                )
            )
        return result

    def to_owner(step, slot):
        sub = step // 4
        plane = 1 if slot >= 2 else 0
        place = recv.at[plane, layer_of(sub), :, cols_of(sub)]
        if slot == 0:
            return pltpu.make_async_copy(stage(step), place, loc.at[sub])
        device = at_mp((None, near_outer, other_mid, far_outer)[slot])
        return remote(stage(step), place, os_s.at[step], os_r.at[sub, plane], device)

    def owner_arrival(sub, plane):
        place = recv.at[plane, layer_of(sub), :, cols_of(sub)]
        return remote(place, place, os_s.at[0], os_r.at[sub, plane], mate)

    def finish(step):
        width, place = width_of(step // 4), step % 2
        for copy in exchange(step, True):
            copy.wait_recv()
        target = stage(step)
        block = 96 if rows % 96 == 0 else rows
        for at in range(0, rows, block):
            mine = pl.ds(pl.multiple_of(dp * rows + at, 16), block)
            total = out[place, mine, :width].astype(f32)
            for hop in range(1, n_dp):
                total = total + inbox[place, hop - 1, at : at + block, :width].astype(f32)
            target[at : at + block, :] = total.astype(bf16)
        for copy in exchange(step, False):
            copy.wait_send()
        to_owner(step, slot_of(step)).start()

    def put_rows(which, values):
        for at in range(0, CAP, 256):
            hit = lax.broadcasted_iota(jnp.int32, (256, ROWS), 0).astype(f32) + float(at) == pos_r[...]
            p_b[at : at + 256, :] = mm(jnp.where(hit, 1.0, 0.0).astype(bf16), values, 1, 0).astype(bf16)

        @pl.when(is_second)
        def _():
            remote(p_b, p_in, pe_s.at[which], pe_r.at[which], mate).start()

    def quarter_of(index):
        return pl.ds(pl.multiple_of(index * quarter, quarter), quarter)

    def row_copies(which, dest):
        return [
            remote(
                p_b.at[quarter_of(index)], dest, ro_s.at[which, turn], ro_r.at[which], at_mp(index)
            )
            for turn, index in enumerate((other_mid, 0, 3))
        ]

    def send_rows(which, dest):
        @pl.when(is_main)
        def _():
            remote(p_b, p_in, pe_s.at[which], pe_r.at[which], mate).wait_recv()
            for at in range(0, CAP, 256):
                span = slice(at, at + 256)
                p_b[span, :] = p_b[span, :] + p_in[span, :]
            for copy in row_copies(which, dest):
                copy.start()
            pltpu.make_async_copy(p_b.at[quarter_of(mp)], dest, rl.at[which]).start()

    def end_rows(which, dest):
        @pl.when(is_main)
        def _():
            for copy in row_copies(which, dest):
                copy.wait_send()
            pltpu.make_async_copy(p_b.at[quarter_of(mp)], dest, rl.at[which]).wait()

        @pl.when(is_second)
        def _():
            remote(p_b, p_in, pe_s.at[which], pe_r.at[which], mate).wait_send()

    def rows_arrived(which, dest):
        @pl.when(jnp.logical_not(is_main))
        def _():
            remote(
                p_b.at[quarter_of(0)], dest, ro_s.at[which, 0], ro_r.at[which], at_mp(0)
            ).wait_recv()

    def piece_place(piece):
        layer, at = piece
        return layer, slice(at, at + PIECE), layer * (cols // PIECE) + at // PIECE

    def diff_piece(piece):
        layer, span, index = piece_place(piece)
        block = opt.shape[2]

        def block_loads(turn):
            part, place = slice(turn * block, (turn + 1) * block), turn % 2
            return [
                pltpu.make_async_copy(source.at[layer, part, span], opt.at[place, i], osem.at[place, i])
                for i, source in enumerate((par, mom, var))
            ] + [
                pltpu.make_async_copy(
                    recv.at[plane, layer, part, span], gsum.at[place, plane], osem.at[place, 3 + plane]
                )
                for plane in range(2)
            ]

        for copy in block_loads(0):
            copy.start()
        for turn in range(rows // block):
            part, place = slice(turn * block, (turn + 1) * block), turn % 2
            if (turn + 1) * block < rows:
                for copy in block_loads(turn + 1):
                    copy.start()
            for copy in block_loads(turn):
                copy.wait()
            grad = gsum[place, 0].astype(f32) + gsum[place, 1].astype(f32)
            one = beta_one * opt[place, 1] + (1 - beta_one) * grad
            two = beta_two * opt[place, 2] + (1 - beta_two) * grad * grad
            step = one / (1 - beta_one**STEP) / (jnp.sqrt(two / (1 - beta_two**STEP)) + adam_eps)
            diff[index, part, :] = (inner_rate * (step + decay_rate * opt[place, 0])).astype(bf16)
        for copy in first_copies(index):
            copy.start()

    def rows_for(where):
        if share == rows:
            return slice(0, rows)
        return pl.ds(pl.multiple_of(where * share, share), share)

    def first_copies(index):
        return [
            remote(
                diff.at[index, rows_for(lax.rem(grp + hop, n_grp))], box.at[index, hop - 1],
                as_s.at[index, hop - 1], as_r.at[index, hop - 1], at_grp(hop),
            )
            for hop in range(1, n_grp)
        ]

    def second_copies(piece):
        layer, span, index = piece_place(piece)
        place = avg.at[layer, rows_for(grp), span]
        return [
            remote(own_avg.at[index], place, bs_s.at[index, hop - 1], bs_r.at[index, hop - 1], at_grp(hop))
            for hop in range(1, n_grp)
        ]

    def second_arrivals(piece):
        layer, span, index = piece_place(piece)
        result = []
        for hop in range(1, n_grp):
            source = lax.rem(grp + n_grp - hop, n_grp)
            place = avg.at[layer, rows_for(source), span]
            result.append(
                remote(place, place, bs_s.at[index, hop - 1], bs_r.at[index, hop - 1], at_grp(hop))
            )
        return result

    def mean_piece(piece):
        layer, span, index = piece_place(piece)
        for copy in first_copies(index):
            copy.wait_recv()
        total = diff[index, rows_for(grp), :].astype(f32)
        for hop in range(1, n_grp):
            total = total + box[index, hop - 1].astype(f32)
        own_avg[index] = (total / n_grp).astype(bf16)
        pltpu.make_async_copy(own_avg.at[index], avg.at[layer, rows_for(grp), span], bl.at[index]).start()
        if share != rows:
            for copy in second_copies(piece):
                copy.start()

    def end_piece(piece):
        layer, span, index = piece_place(piece)
        for copy in first_copies(index):
            copy.wait_send()
        pltpu.make_async_copy(own_avg.at[index], avg.at[layer, rows_for(grp), span], bl.at[index]).wait()
        if share != rows:
            for copy in second_copies(piece):
                copy.wait_send()
            for copy in second_arrivals(piece):
                copy.wait_recv()

    def pieces_of(sub):
        span = cols_of(sub)
        return [(layer_of(sub), at) for at in range(span.start, span.stop, PIECE)]

    def diffs(sub):
        @pl.when(is_outer)
        def _():
            owner_arrival(sub, 0).wait_recv()

        @pl.when(is_mid)
        def _():
            to_owner(4 * sub + 3, 0).wait()

        owner_arrival(sub, 1).wait_recv()
        for piece in pieces_of(sub):
            diff_piece(piece)

    def means(sub):
        for piece in pieces_of(sub):
            mean_piece(piece)

    def mlp_start(sub):
        layer, place = layer_of(sub), sub % 2
        x_load(sub).wait()
        for part in chunks():
            normed, _ = moments(x_b[place, part, :])
            shift = row_mod(clip[part, :], mods, layer, 3)
            scale = row_mod(clip[part, :], mods, layer, 4)
            u_t[:, part] = (normed * (1.0 + scale) + shift).T.astype(bf16)
            down = row_mod(clip[part, :], mods, layer, 5) * g_s[part, :]
            d_s[part, :] = down.astype(bf16)
            d_t[:, part] = down.T.astype(bf16)
        acc[...] = jnp.zeros_like(acc)

    def mlp_step(step):
        place = step % 2
        for part in chunks():
            dact = mm(d_s[part, :], w_b[place, :, D:], 1, 0)
            dh[part, :] = (dact * a_b[place, 1, part, :].astype(f32)).astype(bf16)
        out[place, :, :D] = mm(u_t[...], dh[...], 1, 0).astype(bf16)
        out[place, :, D:] = mm(d_t[...], a_b[place, 0], 1, 0).astype(bf16)
        acc[...] += mm(w_b[place, :, :D], dh[...], 1, 1)

    def attn_start(sub):
        layer, place = layer_of(sub), sub % 2
        x_load(sub).wait()
        for part in chunks():
            normed, _ = moments(x_b[place, part, :])
            shift = row_mod(clip[part, :], mods, layer, 0)
            scale = row_mod(clip[part, :], mods, layer, 1)
            u_t[:, part] = (normed * (1.0 + scale) + shift).T.astype(bf16)
            d_t[:, part] = (row_mod(clip[part, :], mods, layer, 2) * g_s[part, :]).T.astype(bf16)
        acc[...] = jnp.zeros_like(acc)

    def attn_step(step):
        layer, place, slot = layer_of(step // 4), step % 2, slot_of(step)
        out[place, :, 3 * hw : D] = mm(d_t[...], q_b[place, 3 * hw :], 1, 1).astype(bf16)
        do_s[...] = mm(w_b[place, :, 3 * hw : D], d_t[...], 0, 0).astype(bf16)

        def head_step(head, carry):
            base = pl.multiple_of(head * HD, HD)
            keys_t = q_b[place, pl.ds(hw + base, HD), :]
            keys = keys_t.T
            values = q_b[place, pl.ds(2 * hw + base, HD), :].T
            dk = jnp.zeros((HD, ROWS), f32)
            dv = jnp.zeros((HD, ROWS), f32)
            for q0 in range(0, ROWS, 256):
                span = slice(q0, q0 + 256)
                query_t = q_b[place, pl.ds(base, HD), span]
                grad_t = do_s[pl.ds(base, HD), span]
                scores = mm(keys, query_t * jnp.asarray(0.125, bf16), 1, 0)
                allowed = idc[layer] == idr[layer, :, span]
                probs = jnp.where(
                    allowed, jnp.exp(scores - lse[layer, slot * heads + head, :, span]), 0.0
                )
                dv = dv + mm(grad_t, probs.astype(bf16), 1, 1)
                weighted = probs * mm(values, grad_t, 1, 0)
                delta = jnp.sum(weighted, axis=0, keepdims=True)
                ds = (weighted - probs * delta).astype(bf16)
                dq[pl.ds(base, HD), span] = (mm(keys_t, ds, 1, 0) * 0.125).astype(bf16)
                dk = dk + mm(query_t, ds, 1, 1)
            dq[pl.ds(hw + base, HD), :] = (dk * 0.125).astype(bf16)
            dq[pl.ds(2 * hw + base, HD), :] = dv.astype(bf16)
            return carry

        lax.fori_loop(0, heads, head_step, 0)
        out[place, :, : 3 * hw] = mm(u_t[...], dq[...], 1, 1).astype(bf16)
        acc[...] += mm(w_b[place, :, : 3 * hw], dq[...], 1, 0)

    def sub_end(sub):
        layer, place = layer_of(sub), sub % 2
        row = 4 if sub % 2 == 0 else 1
        for part in chunks():
            normed, inv_std = moments(x_b[place, part, :])
            scale = row_mod(clip[part, :], mods, layer, row)
            g_s[part, :] = g_s[part, :] + norm_back(acc[:, part].T * (1.0 + scale), normed, inv_std)

    @pl.when(is_mid)
    def _():
        x_load(0).start()
        for copy in loads(0):
            copy.start()
        g_s[...] = g_in[...]
        put_rows(0, xb[...])
        for step in range(16):
            sub = step // 4
            if step + 1 < 16:
                for copy in loads(step + 1):
                    copy.start()
            if step % 4 == 0:
                if sub < 3:
                    x_load(sub + 1).start()
                (mlp_start if sub % 2 == 0 else attn_start)(sub)
            for copy in loads(step):
                copy.wait()
            (mlp_step if sub % 2 == 0 else attn_step)(step)
            if step >= 2:
                finish(step - 1)
            for copy in exchange(step, True):
                copy.start()
            if step == 0:
                finish(0)
                send_rows(0, mix_o)
            if step % 4 == 3:
                sub_end(sub)
            if step == 9:
                diffs(0)
            if step == 11:
                means(0)
            if step == 14:
                diffs(1)
        end_rows(0, mix_o)
        put_rows(1, g_s[...].astype(bf16))
        finish(15)
        means(1)
        send_rows(1, gin_o)
        diffs(2)
        means(2)
        diffs(3)
        means(3)
        for step in range(16):
            if slot_of(step) != 0:
                to_owner(step, slot_of(step)).wait_send()
        end_rows(1, gin_o)

    @pl.when(is_outer)
    def _():
        for sub in range(4):
            diffs(sub)
            means(sub)

    for which, dest in ((0, mix_o), (1, gin_o)):
        rows_arrived(which, dest)
    for layer in range(L):
        for at in range(0, cols, PIECE):
            end_piece((layer, at))


def run_back(xb, pos, g, clip, idc, idr, mods, lse, xs, qo, ad, w, par, mom, var, quarter):
    sds = jax.ShapeDtypeStruct
    n_dp, n_grp = lax.axis_size("dp"), lax.axis_size("grp")
    rows, cols = par.shape[1], par.shape[2]
    share = share_rows(rows, n_grp)
    count = L * cols // PIECE
    far, peers = n_dp - 1, n_grp - 1
    block = 96 if rows % 96 == 0 else rows
    return pl.pallas_call(
        partial(back_kernel, n_dp, n_grp),
        out_shape=(
            sds((2, L, rows, cols), bf16), sds((L, rows, cols), bf16),
            sds((quarter, D), bf16), sds((quarter, D), bf16),
        ),
        in_specs=[vm_spec()] * 8 + [any_spec()] * 7,
        out_specs=(any_spec(),) * 4,
        scratch_shapes=[
            VM((ROWS, D), f32), VM((2, ROWS, D), f32), VM((2, D, 2 * D), bf16),
            VM((2, 2, ROWS, D), bf16), VM((2, D, ROWS), bf16),
            VM((D, ROWS), bf16), VM((ROWS, D), bf16), VM((D, ROWS), bf16), VM((ROWS, D), bf16),
            VM((9 * HD, ROWS), bf16), VM((3 * HD, ROWS), bf16), VM((D, ROWS), f32),
            VM((2, D, 2 * D), bf16), VM((2, far, rows, 2 * D), bf16),
            VM((L, 3, rows, 2 * D), bf16), VM((L, 3, rows, D), bf16),
            VM((rows, 2 * D), bf16), VM((rows, D), bf16),
            VM((CAP, D), bf16), VM((CAP, D), bf16),
            VM((2, 3, block, PIECE), f32), VM((2, 2, block, PIECE), bf16),
            VM((count, rows, PIECE), bf16), VM((count, peers, share, PIECE), bf16),
            VM((count, share, PIECE), bf16),
            DMA((2,)), DMA((2, 2)), DMA((2,)), DMA((16, far)), DMA((16, far)), DMA((16,)), DMA((4, 2)),
            DMA((4,)), DMA((2,)), DMA((2,)), DMA((2, 3)), DMA((2,)), DMA((2,)), DMA((2, 5)),
            DMA((count, peers)), DMA((count, peers)), DMA((count, peers)), DMA((count, peers)),
            DMA((count,)),
        ],
        compiler_params=pltpu.CompilerParams(
            collective_id=2, has_side_effects=True, vmem_limit_bytes=63 * MIB
        ),
    )(xb, pos, g, clip, idc, idr, mods, lse, xs, qo, ad, w, par, mom, var)


def last_kernel(par, mom, var, out_mom, ga, gb, avg, new_m, new_v, out_a, out_m, out_w, out_l):
    grad = ga[...].astype(f32) + gb[...].astype(f32)
    new_m[...] = beta_one * mom[...] + (1 - beta_one) * grad
    new_v[...] = beta_two * var[...] + (1 - beta_two) * grad * grad
    average = avg[...].astype(f32)
    momentum = outer_mu * out_mom[...] + average
    updated = par[...] - outer_rate * (average + outer_mu * momentum)
    out_a[...] = average
    out_m[...] = momentum
    out_w[...] = updated
    out_l[...] = updated.astype(bf16)


def run_last(par, mom, var, out_mom, recv, avg):
    rows, cols = par.shape[1], par.shape[2]
    block = 96 if rows % 96 == 0 else rows
    sds = jax.ShapeDtypeStruct
    full = pl.BlockSpec((None, block, cols), lambda i, j: (i, j, 0))

    def plane(which):
        return pl.BlockSpec((None, None, block, cols), lambda i, j: (which, i, j, 0))

    return pl.pallas_call(
        last_kernel,
        grid=(L, rows // block),
        out_shape=(sds(par.shape, f32),) * 5 + (sds(par.shape, bf16),),
        in_specs=[full] * 4 + [plane(0), plane(1), full],
        out_specs=(full,) * 6,
        compiler_params=pltpu.CompilerParams(vmem_limit_bytes=48 * MIB),
    )(par, mom, var, out_mom, recv, recv, avg)


def body(
    tokens, cotangent, modulation, clip_frames, clip_patches, params, first_moment, second_moment,
    outer_momentum,
):
    mp = lax.axis_index("mp")
    quarter = tokens.shape[1]
    small = jnp.concatenate([clip_frames, clip_patches], axis=0).astype(f32)
    small = jnp.pad(small, ((0, 6), (0, 128 - SLOTS)))
    w, xs, qo, ad, lse, gradient, xb, clip, idc, idr, pos, mods = run_forward(
        tokens[0], cotangent[0], modulation[0], small, params
    )
    recv, avg, mixed_rows, grad_rows = run_back(
        xb, pos, gradient, clip, idc, idr, mods, lse, xs, qo, ad, w,
        params, first_moment[0], second_moment[0], quarter,
    )
    total = jnp.sum(clip_frames[0] * clip_patches[0])
    own_live = (mp * quarter + jnp.arange(quarter, dtype=jnp.int32) < total)[:, None]
    mixed = jnp.where(own_live, mixed_rows, tokens[0])
    input_grad = jnp.where(own_live, grad_rows.astype(f32), 0.0)
    new_m, new_v, average, momentum, updated, low = run_last(
        params, first_moment[0], second_moment[0], outer_momentum, recv, avg
    )
    return (
        mixed[None], input_grad[None], new_m[None], new_v[None], average, momentum, updated, low,
    )


def solution(mesh):
    in_specs = (
        P("grp", ("dp", "mp"), None),
        P("grp", ("dp", "mp"), None),
        P("grp", "dp", None),
        P("grp", "dp"),
        P("grp", "dp"),
        P(None, "dp", "mp"),
        P("grp", None, "dp", "mp"),
        P("grp", None, "dp", "mp"),
        P(None, "dp", "mp"),
    )
    out_specs = (
        P("grp", ("dp", "mp"), None),
        P("grp", ("dp", "mp"), None),
        P("grp", None, "dp", "mp"),
        P("grp", None, "dp", "mp"),
        P(None, "dp", "mp"),
        P(None, "dp", "mp"),
        P(None, "dp", "mp"),
        P(None, "dp", "mp"),
    )
    return jax.shard_map(body, mesh=mesh, in_specs=in_specs, out_specs=out_specs, check_vma=False)
```

```python
from functools import partial

import jax
import jax.numpy as jnp
from jax import lax
from jax.experimental import pallas as pl
from jax.experimental.pallas import tpu as pltpu
from jax.sharding import PartitionSpec as P

D = 768
HEADS = 12
HD = 64
FF = 3072
L = 2
STEP = 5
CAP = 1024
SLOTS = 4
LONGF = 64
ROWS = CAP // 2
CHUNK = 128
PIECE = 768
SIDE = PIECE // 2

ln_eps = 1e-06
neg_fill = -1e30
beta_one = 0.9
beta_two = 0.999
adam_eps = 1e-08
inner_rate = 0.04
decay_rate = 0.1
outer_rate = 0.7
outer_mu = 0.5

f32 = jnp.float32
bf16 = jnp.bfloat16
VM = pltpu.VMEM
DMA = pltpu.SemaphoreType.DMA
MESH_ID = pl.DeviceIdType.MESH
MIB = 2**20
HEADS_DEV = 3
HW = HEADS_DEV * HD


def mm(left, right, lc, rc):
    return lax.dot_general(left, right, (((lc,), (rc,)), ((), ())), preferred_element_type=f32)


def moments(values):
    centered = values - jnp.mean(values, axis=-1, keepdims=True)
    inv_std = lax.rsqrt(jnp.mean(centered * centered, axis=-1, keepdims=True) + ln_eps)
    return centered * inv_std, inv_std


def norm_back(grad_normed, normed, inv_std):
    inner = grad_normed - jnp.mean(grad_normed, axis=-1, keepdims=True)
    inner = inner - normed * jnp.mean(grad_normed * normed, axis=-1, keepdims=True)
    return inv_std * inner


def row_mod(clip_col, mods, layer, kind):
    base = (layer * 6 + kind) * D
    table = mods[:, base : base + D]
    total = jnp.where(clip_col == 0.0, table[0:1, :], 0.0)
    for clip in range(1, SLOTS):
        total = total + jnp.where(clip_col == float(clip), table[clip : clip + 1, :], 0.0)
    return total


def chunks():
    return [slice(at, at + CHUNK) for at in range(0, ROWS, CHUNK)]


def any_spec():
    return pl.BlockSpec(memory_space=pl.ANY)


def vm_spec():
    return pl.BlockSpec(memory_space=VM)


def flip(index, bit):
    return index + bit - 2 * bit * lax.rem(index // bit, 2)


def slot_meta(small, index, long_core, by_patch):
    frames = [small[0:1, clip : clip + 1] for clip in range(SLOTS)]
    patches = [small[1:2, clip : clip + 1] for clip in range(SLOTS)]
    zero = jnp.zeros_like(frames[0])
    start, long_start, long_size = zero, zero, zero
    starts, ends = [], []
    for clip in range(SLOTS):
        size = frames[clip] * patches[clip]
        is_long = frames[clip] == float(LONGF)
        long_start = long_start + jnp.where(is_long, start, 0.0)
        long_size = long_size + jnp.where(is_long, size, 0.0)
        starts.append(start)
        start = start + size
        ends.append(start)
    pos_long = index + long_start
    pos_short = jnp.where(index < long_start, index, index + long_size)
    pos = jnp.where(long_core, pos_long, pos_short)
    clip_of = jnp.zeros_like(index)
    for clip in range(SLOTS):
        clip_of = clip_of + jnp.where(pos >= ends[clip], 1.0, 0.0)
    limit = jnp.where(long_core, long_start + long_size, start)
    live = pos < limit
    clip_of = jnp.where(live, clip_of, float(SLOTS))
    begin, many, wide = jnp.zeros_like(index), jnp.ones_like(index), jnp.ones_like(index)
    for clip in range(SLOTS):
        hit = clip_of == float(clip)
        begin = jnp.where(hit, starts[clip], begin)
        many = jnp.where(hit, frames[clip], many)
        wide = jnp.where(hit, patches[clip], wide)
    offset = pos - begin
    inner = many if by_patch else wide
    group = jnp.floor((offset + 0.5) / inner)
    within = offset - group * inner
    source = within * wide + group if by_patch else offset
    ident = jnp.where(live, clip_of * CAP + group, -1.0 - index)
    origin = jnp.where(live, index - offset + source, index)
    return jnp.where(live, begin + source, -1.0), clip_of, ident, origin


def one_hot(left, right):
    return jnp.where(left == right, 1.0, 0.0).astype(bf16)


def counted(shape, dim, first=0):
    return lax.broadcasted_iota(jnp.int32, shape, dim).astype(f32) + float(first)


def bands(layer):
    halo = 32 if layer % 2 == 0 else 64
    return [
        (slice(at, at + CHUNK), slice(max(at - halo, 0), min(at + CHUNK + halo, ROWS)))
        for at in range(0, ROWS, CHUNK)
    ]


def remote(src, dst, send, receive, device):
    return pltpu.make_async_remote_copy(
        src_ref=src, dst_ref=dst, send_sem=send, recv_sem=receive,
        device_id=device, device_id_type=MESH_ID,
    )


def greet(devices):
    barrier = pltpu.get_barrier_semaphore()
    for device in devices:
        pl.semaphore_signal(barrier, inc=1, device_id=device, device_id_type=MESH_ID)
    pl.semaphore_wait(barrier, len(devices))


def fwd_kernel(
    n_dp, tok, cot, mod_in, small_in, par,
    w_o, xs_o, qo_o, ad_o, lse_o, g_o, xb_o, clip_o, idc_o, idr_o, pos_o, mod_o,
    w_v, wb, par_f, t_v, c_v, x_v, u_s, acc, qo_v, ad_v, small_v, pos_s,
    zs, zr, gs, gr, ds, dr, os_s, os_r, ts, tr, cs, cr, tl, ms, mr, psem, wsem, xsem, qsem, asem,
):
    grp, dp, mp = lax.axis_index("grp"), lax.axis_index("dp"), lax.axis_index("mp")
    rows, cols = par.shape[1], par.shape[2]
    quarter = tok.shape[0]
    pieces = [(layer, at) for layer in range(L) for at in range(0, cols, PIECE)]
    count = len(pieces)
    star = 1 + lax.rem(dp, 2)
    is_mid = jnp.logical_or(mp == 1, mp == 2)
    is_outer = jnp.logical_not(is_mid)
    is_main = mp == star
    is_second = jnp.logical_and(is_mid, mp != star)
    other_mid = 3 - mp
    near = jnp.where(mp == 0, 1, 2)
    far = 3 - near
    my_rows = pl.ds(pl.multiple_of(dp * rows, rows), rows)
    mate = (grp, flip(dp, 1), mp)
    hops = range(1, n_dp)

    def at_mp(where):
        return (grp, dp, where)

    def at_grp(bit):
        return (flip(grp, bit), dp, mp)

    def at_dp(step):
        return (grp, lax.rem(dp + step, n_dp), mp)

    @pl.when(is_mid)
    def _():
        greet(
            [at_mp(0), at_mp(3), at_mp(other_mid), at_grp(1), at_grp(2)] + [at_dp(hop) for hop in hops]
        )

    @pl.when(is_outer)
    def _():
        greet([at_mp(1), at_mp(2)])

    def bit_of(k, slot):
        return 1 + (k + slot) % 2

    def half(k, slot, mine):
        index = lax.rem(grp // bit_of(k, slot), 2)
        if not mine:
            index = 1 - index
        return pl.ds(pl.multiple_of(index * SIDE, 128), SIDE)

    def z_copy(k, slot, device):
        span = half(k, slot, True)
        return remote(
            wb.at[k, :, span], w_v.at[k, slot, my_rows, span], zs.at[k, slot - 1], zr.at[k, slot - 1], device
        )

    def g_copy(k, slot):
        place = w_v.at[k, slot, my_rows, half(k, slot, True)]
        return remote(place, place, gs.at[k, slot - 1], gr.at[k, slot - 1], at_grp(bit_of(k, slot)))

    def d_copies(k, slot, mine):
        place, turn = w_v.at[k, slot, my_rows, half(k, slot, mine)], 0 if mine else 1
        return [
            remote(
                place, place, ds.at[k, slot - 1, turn, hop - 1], dr.at[k, slot - 1, turn, hop - 1], at_dp(hop)
            )
            for hop in hops
        ]

    def rows_of(hop):
        source = lax.rem(dp + n_dp - hop, n_dp)
        return pl.ds(pl.multiple_of(source * rows, rows), rows)

    def d_arrivals(k, slot, mine):
        turn = 0 if mine else 1
        result = []
        for hop in hops:
            place = w_v.at[k, slot, rows_of(hop), half(k, slot, mine)]
            result.append(
                remote(
                    place, place, ds.at[k, slot - 1, turn, hop - 1], dr.at[k, slot - 1, turn, hop - 1],
                    at_dp(hop),
                )
            )
        return result

    def own_copies(k):
        return [
            remote(wb.at[k], w_v.at[k, 0, my_rows], os_s.at[k, hop - 1], os_r.at[k, hop - 1], at_dp(hop))
            for hop in hops
        ]

    def own_arrivals(k):
        return [
            remote(
                wb.at[k], w_v.at[k, 0, rows_of(hop)], os_s.at[k, hop - 1], os_r.at[k, hop - 1], at_dp(hop)
            )
            for hop in hops
        ]

    def part(ref, index):
        return ref.at[pl.ds(pl.multiple_of(index * quarter, quarter), quarter)]

    def route(src, out, send, receive):
        return remote(src, part(out, mp), send.at[0], receive.at[mp], at_mp(star))

    def pass_on(out, send, receive, index):
        return remote(part(out, index), part(out, index), send.at[1 + index], receive.at[4 + index], mate)

    def main_arrival(out, send, receive, index):
        return remote(part(out, index), part(out, index), send.at[0], receive.at[index], mate)

    def second_arrival(out, send, receive, index):
        return remote(part(out, index), part(out, index), send.at[0], receive.at[4 + index], mate)

    routes = ((tok, t_v, ts, tr), (cot, c_v, cs, cr))

    def keep(which):
        src, out = routes[which][:2]
        return pltpu.make_async_copy(src, part(out, mp), tl.at[which])

    def collect(which):
        out, send, receive = routes[which][1:]

        @pl.when(is_main)
        def _():
            keep(which).wait()
            pass_on(out, send, receive, mp).start()
            for index in (other_mid, 0, 3):
                main_arrival(out, send, receive, index).wait_recv()
                pass_on(out, send, receive, index).start()

        @pl.when(is_second)
        def _():
            for index in range(4):
                second_arrival(out, send, receive, index).wait_recv()

    def meta_copies():
        return [
            remote(mod_in, mod_o, ms.at[0], mr.at[0], mate),
            remote(small_in, small_v, ms.at[1], mr.at[1], mate),
        ]

    def par_load(k):
        layer, at = pieces[k]
        return pltpu.make_async_copy(par.at[layer, :, at : at + PIECE], par_f.at[k % 2], psem.at[k % 2])

    def cast_piece(k):
        if k == 0:
            par_load(0).start()
        if k + 1 < count:
            par_load(k + 1).start()
        par_load(k).wait()
        block = 96 if rows % 96 == 0 else rows
        for at in range(0, rows, block):
            wb[k, at : at + block, :] = par_f[k % 2, at : at + block, :].astype(bf16)

    def keep_own(k):
        block = 96 if rows % 96 == 0 else rows
        for at in range(0, rows, block):
            spot = pl.ds(pl.multiple_of(dp * rows + at, 16), block)
            w_v[k, 0, spot, :] = wb[k, at : at + block, :]

    def w_out(k, slot):
        return pltpu.make_async_copy(w_v.at[k, slot], w_o.at[k, slot], wsem.at[k, slot])

    def x_out(turn):
        return pltpu.make_async_copy(x_v.at[turn % 2], xs_o.at[turn], xsem.at[turn])

    def qo_out(layer, slot):
        return pltpu.make_async_copy(qo_v.at[slot % 2], qo_o.at[layer, slot], qsem.at[slot % 2])

    def ad_out(layer, slot):
        return pltpu.make_async_copy(ad_v.at[slot], ad_o.at[layer, slot], asem.at[slot])

    def serve_z(k):
        for slot in (1, 2, 3):
            z_copy(k, slot, at_mp(other_mid)).wait_recv()
            g_copy(k, slot).start()
            for copy in d_copies(k, slot, True):
                copy.start()
        if k + 2 < count:
            z_copy(k, 2, at_mp(other_mid)).wait_send()
            z_copy(k + 2, 2, at_mp(other_mid)).start()

    def serve_g(k):
        for slot in (1, 2, 3):
            g_copy(k, slot).wait_recv()
            for copy in d_copies(k, slot, False):
                copy.start()

    def ready(k, slot):
        if slot == 0:
            for copy in own_arrivals(k):
                copy.wait_recv()
        else:
            for mine in (True, False):
                for copy in d_arrivals(k, slot, mine):
                    copy.wait_recv()
        w_out(k, slot).start()

    def lifted(layer, kind, turn):
        for span in chunks():
            normed, _ = moments(x_v[turn % 2, span, :])
            shift = row_mod(clip_o[span, :], mod_o, layer, kind)
            scale = row_mod(clip_o[span, :], mod_o, layer, kind + 1)
            u_s[span, :] = (normed * (1.0 + scale) + shift).astype(bf16)
        acc[...] = jnp.zeros_like(acc)

    def branch_rows(layer, kind, turn, span):
        gate = row_mod(clip_o[span, :], mod_o, layer, kind)
        return x_v[1 - turn % 2, span, :] + gate * acc[span, :]

    def add_branch(layer, kind, turn):
        if turn >= 2:
            x_out(turn - 2).wait()
        for span in chunks():
            x_v[turn % 2, span, :] = branch_rows(layer, kind, turn, span)

    def attn_unit(layer, slot):
        k, place = layer * (cols // PIECE), slot % 2
        ready(k, slot)
        if slot >= 2:
            qo_out(layer, slot - 2).wait()
        qo = qo_v.at[place]
        qo[:, : 3 * HW] = mm(u_s[...], w_v[k, slot, :, : 3 * HW], 1, 0).astype(bf16)
        for head in range(HEADS_DEV):
            base = head * HD
            for span, near_by in bands(layer):
                query = qo[span, base : base + HD] * jnp.asarray(0.125, bf16)
                keys = qo[near_by, HW + base : HW + base + HD]
                values = qo[near_by, 2 * HW + base : 2 * HW + base + HD]
                scores = mm(keys, query, 1, 1)
                allowed = idc_o[layer, near_by, :] == idr_o[layer, :, span]
                scores = jnp.where(allowed, scores, neg_fill)
                top = jnp.max(scores, axis=0, keepdims=True)
                raw = jnp.exp(scores - top)
                total = jnp.sum(raw, axis=0, keepdims=True)
                probs = (raw * (1.0 / total)).astype(bf16)
                qo[span, 3 * HW + base : 3 * HW + base + HD] = mm(values, probs, 0, 0).T.astype(bf16)
                lse_o[layer, slot * HEADS_DEV + head, :, span] = top + jnp.log(total)
        acc[...] += mm(qo[:, 3 * HW :], w_v[k, slot, :, 3 * HW :], 1, 1)
        qo_out(layer, slot).start()

    def up_unit(layer, slot):
        k = layer * (cols // PIECE) + 1
        ready(k, slot)
        if layer > 0:
            ad_out(layer - 1, slot).wait()
        for span in chunks():
            hid = mm(u_s[span, :], w_v[k, slot], 1, 0)
            cdf = 0.5 * (1.0 + lax.erf(hid * 0.7071067811865476))
            pdf = jnp.exp(-0.5 * hid * hid) * 0.3989422804014327
            ad_v[slot, 0, span, :] = (hid * cdf).astype(bf16)
            ad_v[slot, 1, span, :] = (cdf + hid * pdf).astype(bf16)
        ad_out(layer, slot).start()

    def down_unit(layer, slot):
        k = layer * (cols // PIECE) + 2
        ready(k, slot)
        acc[...] += mm(ad_v[slot, 0], w_v[k, slot], 1, 1)

    @pl.when(jnp.logical_not(is_main))
    def _():
        route(tok, t_v, ts, tr).start()

    @pl.when(is_main)
    def _():
        keep(0).start()
        keep(1).start()
        for copy in meta_copies():
            copy.start()

    @pl.when(is_outer)
    def _():
        for k in range(count):
            cast_piece(k)
            if k == 0:
                route(tok, t_v, ts, tr).wait_send()
            if k >= 2:
                z_copy(k - 2, 1, at_mp(near)).wait_send()
                z_copy(k - 2, 3, at_mp(far)).wait_send()
            z_copy(k, 1, at_mp(near)).start()
            z_copy(k, 3, at_mp(far)).start()
        for k in range(count - 2, count):
            z_copy(k, 1, at_mp(near)).wait_send()
            z_copy(k, 3, at_mp(far)).wait_send()
        route(cot, c_v, cs, cr).start()
        route(cot, c_v, cs, cr).wait_send()

    @pl.when(is_mid)
    def _():
        for k in range(count):
            cast_piece(k)
            for copy in own_copies(k):
                copy.start()
            if k == 0:
                pl.when(is_second)(lambda: route(tok, t_v, ts, tr).wait_send())
            if k < 2:
                z_copy(k, 2, at_mp(other_mid)).start()
            keep_own(k)

        @pl.when(is_main)
        def _():
            mod_o[...] = mod_in[...]
            small_v[...] = small_in[...]

        @pl.when(is_second)
        def _():
            for copy in meta_copies():
                copy.wait_recv()

        column = counted((ROWS, 1), 0)
        line = counted((1, ROWS), 1)
        small = small_v[...]
        for layer in range(L):
            pos_c, clip_c, id_c, from_c = slot_meta(small, column, is_main, layer % 2 == 1)
            clip_o[...] = clip_c
            idc_o[layer] = id_c
            pos_s[layer] = pos_c
            pos_r, _, id_r, from_r = slot_meta(small, line, is_main, layer % 2 == 1)
            idr_o[layer] = id_r
            pos_o[layer] = pos_r
        pos_s[2] = from_c
        pos_o[2] = from_r
        collect(0)
        for span in chunks():
            x_v[0, span, :] = mm(one_hot(pos_s[0, span, :], counted((CHUNK, CAP), 1)), t_v[...], 1, 0)
        x_out(0).start()

        lifted(0, 0, 0)
        attn_unit(0, 0)
        serve_z(0)
        serve_g(0)
        attn_unit(0, 1)
        attn_unit(0, 2)
        serve_z(1)
        attn_unit(0, 3)
        add_branch(0, 2, 1)
        x_out(1).start()
        lifted(0, 3, 1)
        up_unit(0, 0)
        serve_g(1)
        up_unit(0, 1)
        serve_z(2)
        up_unit(0, 2)
        up_unit(0, 3)
        down_unit(0, 0)
        serve_g(2)
        for slot in (1, 2, 3):
            down_unit(0, slot)
        x_out(0).wait()

        @pl.when(is_main)
        def _():
            for index in range(4):
                pass_on(t_v, ts, tr, index).wait_send()

        for span in chunks():
            value = branch_rows(0, 5, 2, span)
            high = value.astype(bf16)
            rest = value - high.astype(f32)
            middle = rest.astype(bf16)
            t_v[span, :] = high
            t_v[slice(ROWS + span.start, ROWS + span.stop), :] = middle
            u_s[span, :] = (rest - middle.astype(f32)).astype(bf16)
        for span in chunks():
            move = one_hot(pos_s[2, span, :], counted((CHUNK, ROWS), 1))
            x_v[0, span, :] = (
                mm(move, t_v[:ROWS, :], 1, 0) + mm(move, t_v[ROWS:, :], 1, 0) + mm(move, u_s[...], 1, 0)
            )
        x_out(2).start()
        lifted(1, 0, 2)
        qo_out(0, 2).wait()
        qo_out(0, 3).wait()
        serve_z(3)
        attn_unit(1, 0)
        serve_g(3)
        attn_unit(1, 1)
        attn_unit(1, 2)
        serve_z(4)
        attn_unit(1, 3)
        add_branch(1, 2, 3)
        x_out(3).start()
        lifted(1, 3, 3)
        up_unit(1, 0)
        serve_g(4)
        up_unit(1, 1)
        pl.when(is_second)(lambda: route(cot, c_v, cs, cr).start())
        serve_z(5)
        up_unit(1, 2)
        up_unit(1, 3)
        down_unit(1, 0)
        serve_g(5)
        for slot in (1, 2, 3):
            down_unit(1, slot)
        for span in chunks():
            xb_o[span, :] = branch_rows(1, 5, 4, span).astype(bf16)
        collect(1)
        for span in chunks():
            g_o[span, :] = mm(one_hot(pos_s[1, span, :], counted((CHUNK, CAP), 1)), c_v[...], 1, 0)
        x_out(2).wait()
        x_out(3).wait()
        for slot in (2, 3):
            qo_out(1, slot).wait()
        for slot in range(4):
            ad_out(1, slot).wait()
        for k in range(count):
            for copy in own_copies(k):
                copy.wait_send()
            for slot in range(4):
                w_out(k, slot).wait()
            for slot in (1, 2, 3):
                g_copy(k, slot).wait_send()
                for mine in (True, False):
                    for copy in d_copies(k, slot, mine):
                        copy.wait_send()
        for k in range(count - 2, count):
            z_copy(k, 2, at_mp(other_mid)).wait_send()

    @pl.when(is_main)
    def _():
        for copy in meta_copies():
            copy.wait_send()
        for index in range(4):
            pass_on(c_v, cs, cr, index).wait_send()

    @pl.when(is_second)
    def _():
        route(cot, c_v, cs, cr).wait_send()


def run_forward(tok, cot, mod, small, par):
    sds = jax.ShapeDtypeStruct
    n_dp = lax.axis_size("dp")
    rows, cols = par.shape[1], par.shape[2]
    count = L * cols // PIECE
    peers = n_dp - 1
    return pl.pallas_call(
        partial(fwd_kernel, n_dp),
        out_shape=(
            sds((count, 4, D, PIECE), bf16), sds((2 * L, ROWS, D), f32), sds((L, 4, ROWS, D), bf16),
            sds((L, 4, 2, ROWS, FF // 4), bf16), sds((L, HEADS, 1, ROWS), f32), sds((ROWS, D), f32),
            sds((ROWS, D), bf16), sds((ROWS, 1), f32), sds((L, ROWS, 1), f32), sds((L, 1, ROWS), f32),
            sds((3, 1, ROWS), f32), sds(mod.shape, f32),
        ),
        in_specs=[any_spec(), any_spec(), vm_spec(), vm_spec(), any_spec()],
        out_specs=(any_spec(),) * 4 + (vm_spec(),) * 8,
        scratch_shapes=[
            VM((count, 4, D, PIECE), bf16), VM((count, rows, PIECE), bf16), VM((2, rows, PIECE), f32),
            VM((CAP, D), bf16), VM((CAP, D), bf16), VM((2, ROWS, D), f32), VM((ROWS, D), bf16),
            VM((ROWS, D), f32), VM((2, ROWS, D), bf16), VM((4, 2, ROWS, FF // 4), bf16), VM((8, 128), f32),
            VM((3, ROWS, 1), f32),
            DMA((count, 3)), DMA((count, 3)), DMA((count, 3)), DMA((count, 3)),
            DMA((count, 3, 2, peers)), DMA((count, 3, 2, peers)), DMA((count, peers)), DMA((count, peers)),
            DMA((5,)), DMA((8,)), DMA((5,)), DMA((8,)), DMA((2,)), DMA((2,)), DMA((2,)),
            DMA((2,)), DMA((count, 4)), DMA((2 * L,)), DMA((2,)), DMA((4,)),
        ],
        compiler_params=pltpu.CompilerParams(
            collective_id=1, has_side_effects=True, vmem_limit_bytes=63 * MIB
        ),
    )(tok, cot, mod, small, par)


def share_rows(rows, n_grp):
    part = rows // n_grp
    return part if part * n_grp == rows and part % 16 == 0 else rows


def back_kernel(
    n_dp, n_grp,
    xb, pos_r, g_in, clip, idc, idr, mods, lse, xs, qo, ad,
    w_hbm, par, mom, var,
    recv, avg, mix_o, gin_o,
    g_s, x_b, w_b, a_b, q_b, u_t, d_s, d_t, dh, dq, do_s, dk_s, acc, out, inbox, st_m, st_a, st_0m, st_0a,
    p_b, p_in, opt, gsum, diff, box, own_avg,
    xsem, wsem, asem, ce_s, ce_r, os_s, os_r, loc, pe_s, pe_r, ro_s, ro_r, rl, osem,
    as_s, as_r, bs_s, bs_r, bl,
):
    grp, dp, mp = lax.axis_index("grp"), lax.axis_index("dp"), lax.axis_index("mp")
    rows, cols = par.shape[1], par.shape[2]
    quarter = mix_o.shape[0]
    share = share_rows(rows, n_grp)
    star = 1 + lax.rem(dp, 2)
    is_mid = jnp.logical_or(mp == 1, mp == 2)
    is_outer = jnp.logical_not(is_mid)
    is_main = mp == star
    is_second = jnp.logical_and(is_mid, mp != star)
    other_mid = 3 - mp
    near_outer = jnp.where(mp == 1, 0, 3)
    far_outer = 3 - near_outer
    heads = HEADS_DEV
    hw = HW
    mate = (grp, flip(dp, 1), mp)

    def at_mp(where):
        return (grp, dp, where)

    def at_grp(step):
        return (lax.rem(grp + step, n_grp), dp, mp)

    def at_dp(step):
        return (grp, lax.rem(dp + step, n_dp), mp)

    peers = [at_grp(step) for step in range(1, n_grp)]

    @pl.when(is_mid)
    def _():
        greet(
            [at_mp(0), at_mp(3), at_mp(other_mid)] + peers + [at_dp(step) for step in range(1, n_dp)]
        )

    @pl.when(is_outer)
    def _():
        greet([at_mp(1), at_mp(2)] + peers)

    def layer_of(sub):
        return 1 - sub // 2

    def width_of(sub):
        return 2 * D if sub % 2 == 0 else D

    def cols_of(sub):
        return slice(D, cols) if sub % 2 == 0 else slice(0, D)

    def slot_of(step):
        return 3 - step % 4

    def stage(step):
        sub, slot = step // 4, slot_of(step)
        if slot == 0:
            return st_0m if sub % 2 == 0 else st_0a
        return (st_m if sub % 2 == 0 else st_a).at[layer_of(sub), slot - 1]

    def loads(step):
        sub, slot, place = step // 4, slot_of(step), step % 2
        layer, width = layer_of(sub), width_of(sub)
        first = layer * (cols // PIECE) + (1 if sub % 2 == 0 else 0)
        result = [
            pltpu.make_async_copy(
                w_hbm.at[first + turn, slot], w_b.at[place, :, turn * D : turn * D + D], wsem.at[place, turn]
            )
            for turn in range(width // D)
        ]
        if sub % 2 == 0:
            result.append(pltpu.make_async_copy(ad.at[layer, slot], a_b.at[place], asem.at[place]))
        else:
            result.append(pltpu.make_async_copy(qo.at[layer, slot], q_b.at[place], asem.at[place]))
        return result

    def x_load(sub):
        source = xs.at[2 * layer_of(sub) + (1 if sub % 2 == 0 else 0)]
        return pltpu.make_async_copy(source, x_b.at[sub % 2], xsem.at[sub % 2])

    def exchange(step, arrive):
        width, place = width_of(step // 4), step % 2
        result = []
        for hop in range(1, n_dp):
            target = lax.rem(dp + hop, n_dp)
            result.append(
                remote(
                    out.at[place, pl.ds(pl.multiple_of(target * rows, rows), rows), :width],
                    inbox.at[place, hop - 1, :, :width],
                    ce_s.at[step, hop - 1], ce_r.at[step, hop - 1], at_dp(hop),
                )
            )
        return result

    def to_owner(step, slot):
        sub = step // 4
        plane = 1 if slot >= 2 else 0
        place = recv.at[plane, layer_of(sub), :, cols_of(sub)]
        if slot == 0:
            return pltpu.make_async_copy(stage(step), place, loc.at[sub])
        device = at_mp((None, near_outer, other_mid, far_outer)[slot])
        return remote(stage(step), place, os_s.at[step], os_r.at[sub, plane], device)

    def owner_arrival(sub, plane):
        place = recv.at[plane, layer_of(sub), :, cols_of(sub)]
        return remote(place, place, os_s.at[0], os_r.at[sub, plane], mate)

    def finish(step):
        width, place = width_of(step // 4), step % 2
        for copy in exchange(step, True):
            copy.wait_recv()
        target = stage(step)
        block = 96 if rows % 96 == 0 else rows
        for at in range(0, rows, block):
            mine = pl.ds(pl.multiple_of(dp * rows + at, 16), block)
            total = out[place, mine, :width].astype(f32)
            for hop in range(1, n_dp):
                total = total + inbox[place, hop - 1, at : at + block, :width].astype(f32)
            target[at : at + block, :] = total.astype(bf16)
        for copy in exchange(step, False):
            copy.wait_send()
        to_owner(step, slot_of(step)).start()

    def put_rows(which, values):
        for at in range(0, CAP, 256):
            place = one_hot(counted((256, ROWS), 0, at), pos_r[1 - which])
            p_b[at : at + 256, :] = mm(place, values, 1, 0).astype(bf16)

        @pl.when(is_second)
        def _():
            remote(p_b, p_in, pe_s.at[which], pe_r.at[which], mate).start()

    def quarter_of(index):
        return pl.ds(pl.multiple_of(index * quarter, quarter), quarter)

    def row_copies(which, dest):
        return [
            remote(
                p_b.at[quarter_of(index)], dest, ro_s.at[which, turn], ro_r.at[which], at_mp(index)
            )
            for turn, index in enumerate((other_mid, 0, 3))
        ]

    def send_rows(which, dest):
        @pl.when(is_main)
        def _():
            remote(p_b, p_in, pe_s.at[which], pe_r.at[which], mate).wait_recv()
            for at in range(0, CAP, 256):
                span = slice(at, at + 256)
                p_b[span, :] = p_b[span, :] + p_in[span, :]
            for copy in row_copies(which, dest):
                copy.start()
            pltpu.make_async_copy(p_b.at[quarter_of(mp)], dest, rl.at[which]).start()

    def end_rows(which, dest):
        @pl.when(is_main)
        def _():
            for copy in row_copies(which, dest):
                copy.wait_send()
            pltpu.make_async_copy(p_b.at[quarter_of(mp)], dest, rl.at[which]).wait()

        @pl.when(is_second)
        def _():
            remote(p_b, p_in, pe_s.at[which], pe_r.at[which], mate).wait_send()

    def rows_arrived(which, dest):
        @pl.when(jnp.logical_not(is_main))
        def _():
            remote(
                p_b.at[quarter_of(0)], dest, ro_s.at[which, 0], ro_r.at[which], at_mp(0)
            ).wait_recv()

    def piece_place(piece):
        layer, at = piece
        return layer, slice(at, at + PIECE), layer * (cols // PIECE) + at // PIECE

    def diff_piece(piece):
        layer, span, index = piece_place(piece)
        block = opt.shape[2]

        def block_loads(turn):
            part, place = slice(turn * block, (turn + 1) * block), turn % 2
            return [
                pltpu.make_async_copy(source.at[layer, part, span], opt.at[place, i], osem.at[place, i])
                for i, source in enumerate((par, mom, var))
            ] + [
                pltpu.make_async_copy(
                    recv.at[plane, layer, part, span], gsum.at[place, plane], osem.at[place, 3 + plane]
                )
                for plane in range(2)
            ]

        for copy in block_loads(0):
            copy.start()
        for turn in range(rows // block):
            part, place = slice(turn * block, (turn + 1) * block), turn % 2
            if (turn + 1) * block < rows:
                for copy in block_loads(turn + 1):
                    copy.start()
            for copy in block_loads(turn):
                copy.wait()
            grad = gsum[place, 0].astype(f32) + gsum[place, 1].astype(f32)
            one = beta_one * opt[place, 1] + (1 - beta_one) * grad
            two = beta_two * opt[place, 2] + (1 - beta_two) * grad * grad
            step = one / (1 - beta_one**STEP) / (jnp.sqrt(two / (1 - beta_two**STEP)) + adam_eps)
            diff[index, part, :] = (inner_rate * (step + decay_rate * opt[place, 0])).astype(bf16)
        for copy in first_copies(index):
            copy.start()

    def rows_for(where):
        if share == rows:
            return slice(0, rows)
        return pl.ds(pl.multiple_of(where * share, share), share)

    def first_copies(index):
        return [
            remote(
                diff.at[index, rows_for(lax.rem(grp + hop, n_grp))], box.at[index, hop - 1],
                as_s.at[index, hop - 1], as_r.at[index, hop - 1], at_grp(hop),
            )
            for hop in range(1, n_grp)
        ]

    def second_copies(piece):
        layer, span, index = piece_place(piece)
        place = avg.at[layer, rows_for(grp), span]
        return [
            remote(own_avg.at[index], place, bs_s.at[index, hop - 1], bs_r.at[index, hop - 1], at_grp(hop))
            for hop in range(1, n_grp)
        ]

    def second_arrivals(piece):
        layer, span, index = piece_place(piece)
        result = []
        for hop in range(1, n_grp):
            source = lax.rem(grp + n_grp - hop, n_grp)
            place = avg.at[layer, rows_for(source), span]
            result.append(
                remote(place, place, bs_s.at[index, hop - 1], bs_r.at[index, hop - 1], at_grp(hop))
            )
        return result

    def mean_piece(piece):
        layer, span, index = piece_place(piece)
        for copy in first_copies(index):
            copy.wait_recv()
        total = diff[index, rows_for(grp), :].astype(f32)
        for hop in range(1, n_grp):
            total = total + box[index, hop - 1].astype(f32)
        own_avg[index] = (total / n_grp).astype(bf16)
        pltpu.make_async_copy(own_avg.at[index], avg.at[layer, rows_for(grp), span], bl.at[index]).start()
        if share != rows:
            for copy in second_copies(piece):
                copy.start()

    def end_piece(piece):
        layer, span, index = piece_place(piece)
        for copy in first_copies(index):
            copy.wait_send()
        pltpu.make_async_copy(own_avg.at[index], avg.at[layer, rows_for(grp), span], bl.at[index]).wait()
        if share != rows:
            for copy in second_copies(piece):
                copy.wait_send()
            for copy in second_arrivals(piece):
                copy.wait_recv()

    def pieces_of(sub):
        span = cols_of(sub)
        return [(layer_of(sub), at) for at in range(span.start, span.stop, PIECE)]

    def diffs(sub):
        @pl.when(is_outer)
        def _():
            owner_arrival(sub, 0).wait_recv()

        @pl.when(is_mid)
        def _():
            to_owner(4 * sub + 3, 0).wait()

        owner_arrival(sub, 1).wait_recv()
        for piece in pieces_of(sub):
            diff_piece(piece)

    def means(sub):
        for piece in pieces_of(sub):
            mean_piece(piece)

    def mlp_start(sub):
        layer, place = layer_of(sub), sub % 2
        x_load(sub).wait()
        for part in chunks():
            normed, _ = moments(x_b[place, part, :])
            shift = row_mod(clip[part, :], mods, layer, 3)
            scale = row_mod(clip[part, :], mods, layer, 4)
            u_t[:, part] = (normed * (1.0 + scale) + shift).T.astype(bf16)
            down = row_mod(clip[part, :], mods, layer, 5) * g_s[part, :]
            d_s[part, :] = down.astype(bf16)
            d_t[:, part] = down.T.astype(bf16)
        acc[...] = jnp.zeros_like(acc)

    def mlp_step(step):
        place = step % 2
        for part in chunks():
            dact = mm(d_s[part, :], w_b[place, :, D:], 1, 0)
            dh[part, :] = (dact * a_b[place, 1, part, :].astype(f32)).astype(bf16)
        out[place, :, :D] = mm(u_t[...], dh[...], 1, 0).astype(bf16)
        out[place, :, D:] = mm(d_t[...], a_b[place, 0], 1, 0).astype(bf16)
        acc[...] += mm(dh[...], w_b[place, :, :D], 1, 1)

    def attn_start(sub):
        layer, place = layer_of(sub), sub % 2
        x_load(sub).wait()
        for part in chunks():
            normed, _ = moments(x_b[place, part, :])
            shift = row_mod(clip[part, :], mods, layer, 0)
            scale = row_mod(clip[part, :], mods, layer, 1)
            u_t[:, part] = (normed * (1.0 + scale) + shift).T.astype(bf16)
            branch = row_mod(clip[part, :], mods, layer, 2) * g_s[part, :]
            d_s[part, :] = branch.astype(bf16)
            d_t[:, part] = branch.T.astype(bf16)
        acc[...] = jnp.zeros_like(acc)

    def attn_step(step):
        layer, place, slot = layer_of(step // 4), step % 2, slot_of(step)
        out[place, :, 3 * hw : D] = mm(d_t[...], q_b[place, :, 3 * hw :], 1, 0).astype(bf16)
        do_s[...] = mm(d_s[...], w_b[place, :, 3 * hw : D], 1, 0).astype(bf16)
        for head in range(heads):
            base = head * HD
            dk_s[...] = jnp.zeros_like(dk_s)
            for span, near_by in bands(layer):
                query = q_b[place, span, base : base + HD]
                keys = q_b[place, near_by, hw + base : hw + base + HD]
                values = q_b[place, near_by, 2 * hw + base : 2 * hw + base + HD]
                grad = do_s[span, base : base + HD]
                scores = mm(keys, query * jnp.asarray(0.125, bf16), 1, 1)
                allowed = idc[layer, near_by, :] == idr[layer, :, span]
                probs = jnp.where(
                    allowed, jnp.exp(scores - lse[layer, slot * heads + head, :, span]), 0.0
                )
                dk_s[1, near_by, :] += mm(probs.astype(bf16), grad, 1, 0)
                weighted = probs * mm(values, grad, 1, 1)
                delta = jnp.sum(weighted, axis=0, keepdims=True)
                ds = (weighted - probs * delta).astype(bf16)
                dq[span, base : base + HD] = (mm(keys, ds, 0, 0).T * 0.125).astype(bf16)
                dk_s[0, near_by, :] += mm(ds, query, 1, 0)
            dq[:, hw + base : hw + base + HD] = (dk_s[0] * 0.125).astype(bf16)
            dq[:, 2 * hw + base : 2 * hw + base + HD] = dk_s[1].astype(bf16)
        out[place, :, : 3 * hw] = mm(u_t[...], dq[...], 1, 0).astype(bf16)
        acc[...] += mm(dq[...], w_b[place, :, : 3 * hw], 1, 1)

    def sub_end(sub):
        layer, place = layer_of(sub), sub % 2
        row = 4 if sub % 2 == 0 else 1
        for part in chunks():
            normed, inv_std = moments(x_b[place, part, :])
            scale = row_mod(clip[part, :], mods, layer, row)
            g_s[part, :] = g_s[part, :] + norm_back(acc[part, :] * (1.0 + scale), normed, inv_std)

    def to_frame_order():
        for part in chunks():
            high = g_s[part, :].astype(bf16)
            dh[part, :] = high
            d_s[part, :] = (g_s[part, :] - high.astype(f32)).astype(bf16)
        for part in chunks():
            move = one_hot(counted((CHUNK, ROWS), 0, part.start), pos_r[2])
            g_s[part, :] = mm(move, dh[...], 1, 0) + mm(move, d_s[...], 1, 0)

    @pl.when(is_mid)
    def _():
        x_load(0).start()
        for copy in loads(0):
            copy.start()
        g_s[...] = g_in[...]
        put_rows(0, xb[...])
        for step in range(16):
            sub = step // 4
            if step + 1 < 16:
                for copy in loads(step + 1):
                    copy.start()
            if step % 4 == 0:
                if sub < 3:
                    x_load(sub + 1).start()
                (mlp_start if sub % 2 == 0 else attn_start)(sub)
            for copy in loads(step):
                copy.wait()
            (mlp_step if sub % 2 == 0 else attn_step)(step)
            if step >= 2:
                finish(step - 1)
            for copy in exchange(step, True):
                copy.start()
            if step == 0:
                finish(0)
                send_rows(0, mix_o)
            if step % 4 == 3:
                sub_end(sub)
            if step == 7:
                to_frame_order()
            if step == 9:
                diffs(0)
            if step == 11:
                means(0)
            if step == 14:
                diffs(1)
        end_rows(0, mix_o)
        put_rows(1, g_s[...].astype(bf16))
        finish(15)
        means(1)
        send_rows(1, gin_o)
        diffs(2)
        means(2)
        diffs(3)
        means(3)
        for step in range(16):
            if slot_of(step) != 0:
                to_owner(step, slot_of(step)).wait_send()
        end_rows(1, gin_o)

    @pl.when(is_outer)
    def _():
        for sub in range(4):
            diffs(sub)
            means(sub)

    for which, dest in ((0, mix_o), (1, gin_o)):
        rows_arrived(which, dest)
    for layer in range(L):
        for at in range(0, cols, PIECE):
            end_piece((layer, at))


def run_back(xb, pos, g, clip, idc, idr, mods, lse, xs, qo, ad, w, par, mom, var, quarter):
    sds = jax.ShapeDtypeStruct
    n_dp, n_grp = lax.axis_size("dp"), lax.axis_size("grp")
    rows, cols = par.shape[1], par.shape[2]
    share = share_rows(rows, n_grp)
    count = L * cols // PIECE
    far, peers = n_dp - 1, n_grp - 1
    block = 96 if rows % 96 == 0 else rows
    return pl.pallas_call(
        partial(back_kernel, n_dp, n_grp),
        out_shape=(
            sds((2, L, rows, cols), bf16), sds((L, rows, cols), bf16),
            sds((quarter, D), bf16), sds((quarter, D), bf16),
        ),
        in_specs=[vm_spec()] * 8 + [any_spec()] * 7,
        out_specs=(any_spec(),) * 4,
        scratch_shapes=[
            VM((ROWS, D), f32), VM((2, ROWS, D), f32), VM((2, D, 2 * D), bf16),
            VM((2, 2, ROWS, D), bf16), VM((2, ROWS, D), bf16),
            VM((D, ROWS), bf16), VM((ROWS, D), bf16), VM((D, ROWS), bf16), VM((ROWS, D), bf16),
            VM((ROWS, 9 * HD), bf16), VM((ROWS, 3 * HD), bf16), VM((2, ROWS, HD), f32), VM((ROWS, D), f32),
            VM((2, D, 2 * D), bf16), VM((2, far, rows, 2 * D), bf16),
            VM((L, 3, rows, 2 * D), bf16), VM((L, 3, rows, D), bf16),
            VM((rows, 2 * D), bf16), VM((rows, D), bf16),
            VM((CAP, D), bf16), VM((CAP, D), bf16),
            VM((2, 3, block, PIECE), f32), VM((2, 2, block, PIECE), bf16),
            VM((count, rows, PIECE), bf16), VM((count, peers, share, PIECE), bf16),
            VM((count, share, PIECE), bf16),
            DMA((2,)), DMA((2, 2)), DMA((2,)), DMA((16, far)), DMA((16, far)), DMA((16,)), DMA((4, 2)),
            DMA((4,)), DMA((2,)), DMA((2,)), DMA((2, 3)), DMA((2,)), DMA((2,)), DMA((2, 5)),
            DMA((count, peers)), DMA((count, peers)), DMA((count, peers)), DMA((count, peers)),
            DMA((count,)),
        ],
        compiler_params=pltpu.CompilerParams(
            collective_id=2, has_side_effects=True, vmem_limit_bytes=63 * MIB
        ),
    )(xb, pos, g, clip, idc, idr, mods, lse, xs, qo, ad, w, par, mom, var)


def last_kernel(
    par, mom, var, out_mom, ga, gb, avg, rows_m, rows_g, tok, live,
    new_m, new_v, out_a, out_m, out_w, out_l, mixed, grad_in,
):
    @pl.when(jnp.logical_and(pl.program_id(0) == 0, pl.program_id(1) == 0))
    def _():
        mixed[...] = jnp.where(live[...] > 0.0, rows_m[...].astype(f32), tok[...].astype(f32)).astype(bf16)
        grad_in[...] = jnp.where(live[...] > 0.0, rows_g[...].astype(f32), 0.0)

    grad = ga[...].astype(f32) + gb[...].astype(f32)
    new_m[...] = beta_one * mom[...] + (1 - beta_one) * grad
    new_v[...] = beta_two * var[...] + (1 - beta_two) * grad * grad
    average = avg[...].astype(f32)
    momentum = outer_mu * out_mom[...] + average
    updated = par[...] - outer_rate * (average + outer_mu * momentum)
    out_a[...] = average
    out_m[...] = momentum
    out_w[...] = updated
    out_l[...] = updated.astype(bf16)


def run_last(par, mom, var, out_mom, recv, avg, rows_m, rows_g, tok, live):
    rows, cols = par.shape[1], par.shape[2]
    block = 96 if rows % 96 == 0 else rows
    sds = jax.ShapeDtypeStruct
    full = pl.BlockSpec((None, block, cols), lambda i, j: (i, j, 0))

    def plane(which):
        return pl.BlockSpec((None, None, block, cols), lambda i, j: (which, i, j, 0))

    return pl.pallas_call(
        last_kernel,
        grid=(L, rows // block),
        out_shape=(sds(par.shape, f32),) * 5 + (sds(par.shape, bf16), sds(tok.shape, bf16), sds(tok.shape, f32)),
        in_specs=[full] * 4 + [plane(0), plane(1), full] + [vm_spec()] * 4,
        out_specs=(full,) * 6 + (vm_spec(),) * 2,
        compiler_params=pltpu.CompilerParams(vmem_limit_bytes=48 * MIB),
    )(par, mom, var, out_mom, recv, recv, avg, rows_m, rows_g, tok, live)


def body(
    tokens, cotangent, modulation, clip_frames, clip_patches, params, first_moment, second_moment,
    outer_momentum,
):
    mp = lax.axis_index("mp")
    quarter = tokens.shape[1]
    small = jnp.concatenate([clip_frames, clip_patches], axis=0).astype(f32)
    small = jnp.pad(small, ((0, 6), (0, 128 - SLOTS)))
    w, xs, qo, ad, lse, gradient, xb, clip, idc, idr, pos, mods = run_forward(
        tokens[0], cotangent[0], modulation[0], small, params
    )
    recv, avg, mixed_rows, grad_rows = run_back(
        xb, pos, gradient, clip, idc, idr, mods, lse, xs, qo, ad, w,
        params, first_moment[0], second_moment[0], quarter,
    )
    total = jnp.sum(clip_frames[0] * clip_patches[0])
    own_live = (mp * quarter + jnp.arange(quarter, dtype=jnp.int32) < total).astype(f32)[:, None]
    new_m, new_v, average, momentum, updated, low, mixed, input_grad = run_last(
        params, first_moment[0], second_moment[0], outer_momentum, recv, avg,
        mixed_rows, grad_rows, tokens[0], own_live,
    )
    return (
        mixed[None], input_grad[None], new_m[None], new_v[None], average, momentum, updated, low,
    )


def solution(mesh):
    in_specs = (
        P("grp", ("dp", "mp"), None),
        P("grp", ("dp", "mp"), None),
        P("grp", "dp", None),
        P("grp", "dp"),
        P("grp", "dp"),
        P(None, "dp", "mp"),
        P("grp", None, "dp", "mp"),
        P("grp", None, "dp", "mp"),
        P(None, "dp", "mp"),
    )
    out_specs = (
        P("grp", ("dp", "mp"), None),
        P("grp", ("dp", "mp"), None),
        P("grp", None, "dp", "mp"),
        P("grp", None, "dp", "mp"),
        P(None, "dp", "mp"),
        P(None, "dp", "mp"),
        P(None, "dp", "mp"),
        P(None, "dp", "mp"),
    )
    return jax.shard_map(body, mesh=mesh, in_specs=in_specs, out_specs=out_specs, check_vma=False)
```

```python
from functools import partial

import jax
import jax.numpy as jnp
from jax import lax
from jax.experimental import pallas as pl
from jax.experimental.pallas import tpu as pltpu
from jax.sharding import PartitionSpec as P

D = 768
HEADS = 12
HD = 64
FF = 3072
L = 2
STEP = 5
CAP = 1024
SLOTS = 4
LONGF = 64
ROWS = CAP // 2
CHUNK = 128
PIECE = 768
SIDE = PIECE // 2

ln_eps = 1e-06
neg_fill = -1e30
beta_one = 0.9
beta_two = 0.999
adam_eps = 1e-08
inner_rate = 0.04
decay_rate = 0.1
outer_rate = 0.7
outer_mu = 0.5

f32 = jnp.float32
bf16 = jnp.bfloat16
VM = pltpu.VMEM
DMA = pltpu.SemaphoreType.DMA
MESH_ID = pl.DeviceIdType.MESH
MIB = 2**20
HEADS_DEV = 3
HW = HEADS_DEV * HD


def mm(left, right, lc, rc):
    return lax.dot_general(left, right, (((lc,), (rc,)), ((), ())), preferred_element_type=f32)


def moments(values):
    centered = values - jnp.mean(values, axis=-1, keepdims=True)
    inv_std = lax.rsqrt(jnp.mean(centered * centered, axis=-1, keepdims=True) + ln_eps)
    return centered * inv_std, inv_std


def norm_back(grad_normed, normed, inv_std):
    inner = grad_normed - jnp.mean(grad_normed, axis=-1, keepdims=True)
    inner = inner - normed * jnp.mean(grad_normed * normed, axis=-1, keepdims=True)
    return inv_std * inner


def row_mod(clip_col, mods, layer, kind):
    base = (layer * 6 + kind) * D
    table = mods[:, base : base + D]
    total = jnp.where(clip_col == 0.0, table[0:1, :], 0.0)
    for clip in range(1, SLOTS):
        total = total + jnp.where(clip_col == float(clip), table[clip : clip + 1, :], 0.0)
    return total


def chunks():
    return [slice(at, at + CHUNK) for at in range(0, ROWS, CHUNK)]


def any_spec():
    return pl.BlockSpec(memory_space=pl.ANY)


def vm_spec():
    return pl.BlockSpec(memory_space=VM)


def flip(index, bit):
    return index + bit - 2 * bit * lax.rem(index // bit, 2)


def slot_meta(small, index, long_core, by_patch):
    frames = [small[0:1, clip : clip + 1] for clip in range(SLOTS)]
    patches = [small[1:2, clip : clip + 1] for clip in range(SLOTS)]
    zero = jnp.zeros_like(frames[0])
    start, long_start, long_size = zero, zero, zero
    starts, ends = [], []
    for clip in range(SLOTS):
        size = frames[clip] * patches[clip]
        is_long = frames[clip] == float(LONGF)
        long_start = long_start + jnp.where(is_long, start, 0.0)
        long_size = long_size + jnp.where(is_long, size, 0.0)
        starts.append(start)
        start = start + size
        ends.append(start)
    pos_long = index + long_start
    pos_short = jnp.where(index < long_start, index, index + long_size)
    pos = jnp.where(long_core, pos_long, pos_short)
    clip_of = jnp.zeros_like(index)
    for clip in range(SLOTS):
        clip_of = clip_of + jnp.where(pos >= ends[clip], 1.0, 0.0)
    limit = jnp.where(long_core, long_start + long_size, start)
    live = pos < limit
    clip_of = jnp.where(live, clip_of, float(SLOTS))
    begin, many, wide = jnp.zeros_like(index), jnp.ones_like(index), jnp.ones_like(index)
    for clip in range(SLOTS):
        hit = clip_of == float(clip)
        begin = jnp.where(hit, starts[clip], begin)
        many = jnp.where(hit, frames[clip], many)
        wide = jnp.where(hit, patches[clip], wide)
    offset = pos - begin
    inner = many if by_patch else wide
    group = jnp.floor((offset + 0.5) / inner)
    within = offset - group * inner
    source = within * wide + group if by_patch else offset
    ident = jnp.where(live, clip_of * CAP + group, -1.0 - index)
    origin = jnp.where(live, index - offset + source, index)
    return jnp.where(live, begin + source, -1.0), clip_of, ident, origin


def one_hot(left, right):
    return jnp.where(left == right, 1.0, 0.0).astype(bf16)


def counted(shape, dim, first=0):
    return lax.broadcasted_iota(jnp.int32, shape, dim).astype(f32) + float(first)


def bands(layer):
    halo = 32 if layer % 2 == 0 else 64
    return [
        (slice(at, at + CHUNK), slice(max(at - halo, 0), min(at + CHUNK + halo, ROWS)))
        for at in range(0, ROWS, CHUNK)
    ]


def remote(src, dst, send, receive, device):
    return pltpu.make_async_remote_copy(
        src_ref=src, dst_ref=dst, send_sem=send, recv_sem=receive,
        device_id=device, device_id_type=MESH_ID,
    )


def greet(devices):
    barrier = pltpu.get_barrier_semaphore()
    for device in devices:
        pl.semaphore_signal(barrier, inc=1, device_id=device, device_id_type=MESH_ID)
    pl.semaphore_wait(barrier, len(devices))


def fwd_kernel(
    n_dp, tok, cot, mod_in, small_in, par,
    w_o, xs_o, qo_o, ad_o, lse_o, g_o, xb_o, clip_o, idc_o, idr_o, pos_o, mod_o,
    w_v, wb, par_f, t_v, c_v, x_v, u_s, acc, qo_v, ad_v, small_v, pos_s,
    zs, zr, gs, gr, ds, dr, os_s, os_r, ts, tr, cs, cr, tl, ms, mr, psem, wsem, xsem, qsem, asem,
):
    grp, dp, mp = lax.axis_index("grp"), lax.axis_index("dp"), lax.axis_index("mp")
    rows, cols = par.shape[1], par.shape[2]
    quarter = tok.shape[0]
    pieces = [(layer, at) for layer in range(L) for at in range(0, cols, PIECE)]
    count = len(pieces)
    star = 1 + lax.rem(dp, 2)
    is_mid = jnp.logical_or(mp == 1, mp == 2)
    is_outer = jnp.logical_not(is_mid)
    is_main = mp == star
    is_second = jnp.logical_and(is_mid, mp != star)
    other_mid = 3 - mp
    near = jnp.where(mp == 0, 1, 2)
    far = 3 - near
    my_rows = pl.ds(pl.multiple_of(dp * rows, rows), rows)
    mate = (grp, flip(dp, 1), mp)
    hops = range(1, n_dp)

    def at_mp(where):
        return (grp, dp, where)

    def at_grp(bit):
        return (flip(grp, bit), dp, mp)

    def at_dp(step):
        return (grp, lax.rem(dp + step, n_dp), mp)

    @pl.when(is_mid)
    def _():
        greet(
            [at_mp(0), at_mp(3), at_mp(other_mid), at_grp(1), at_grp(2)] + [at_dp(hop) for hop in hops]
        )

    @pl.when(is_outer)
    def _():
        greet([at_mp(1), at_mp(2)])

    def bit_of(k, slot):
        return 1 + (k + slot) % 2

    def half(k, slot, mine):
        index = lax.rem(grp // bit_of(k, slot), 2)
        if not mine:
            index = 1 - index
        return pl.ds(pl.multiple_of(index * SIDE, 128), SIDE)

    def z_copy(k, slot, device):
        span = half(k, slot, True)
        return remote(
            wb.at[k, :, span], w_v.at[k, slot, my_rows, span], zs.at[k, slot - 1], zr.at[k, slot - 1], device
        )

    def g_copy(k, slot):
        place = w_v.at[k, slot, my_rows, half(k, slot, True)]
        return remote(place, place, gs.at[k, slot - 1], gr.at[k, slot - 1], at_grp(bit_of(k, slot)))

    def d_copies(k, slot, mine):
        place, turn = w_v.at[k, slot, my_rows, half(k, slot, mine)], 0 if mine else 1
        return [
            remote(
                place, place, ds.at[k, slot - 1, turn, hop - 1], dr.at[k, slot - 1, turn, hop - 1], at_dp(hop)
            )
            for hop in hops
        ]

    def rows_of(hop):
        source = lax.rem(dp + n_dp - hop, n_dp)
        return pl.ds(pl.multiple_of(source * rows, rows), rows)

    def d_arrivals(k, slot, mine):
        turn = 0 if mine else 1
        result = []
        for hop in hops:
            place = w_v.at[k, slot, rows_of(hop), half(k, slot, mine)]
            result.append(
                remote(
                    place, place, ds.at[k, slot - 1, turn, hop - 1], dr.at[k, slot - 1, turn, hop - 1],
                    at_dp(hop),
                )
            )
        return result

    def own_copies(k):
        return [
            remote(wb.at[k], w_v.at[k, 0, my_rows], os_s.at[k, hop - 1], os_r.at[k, hop - 1], at_dp(hop))
            for hop in hops
        ]

    def own_arrivals(k):
        return [
            remote(
                wb.at[k], w_v.at[k, 0, rows_of(hop)], os_s.at[k, hop - 1], os_r.at[k, hop - 1], at_dp(hop)
            )
            for hop in hops
        ]

    def part(ref, index):
        return ref.at[pl.ds(pl.multiple_of(index * quarter, quarter), quarter)]

    def route(src, out, send, receive):
        return remote(src, part(out, mp), send.at[0], receive.at[mp], at_mp(star))

    def pass_on(out, send, receive, index):
        return remote(part(out, index), part(out, index), send.at[1 + index], receive.at[4 + index], mate)

    def main_arrival(out, send, receive, index):
        return remote(part(out, index), part(out, index), send.at[0], receive.at[index], mate)

    def second_arrival(out, send, receive, index):
        return remote(part(out, index), part(out, index), send.at[0], receive.at[4 + index], mate)

    routes = ((tok, t_v, ts, tr), (cot, c_v, cs, cr))

    def keep(which):
        src, out = routes[which][:2]
        return pltpu.make_async_copy(src, part(out, mp), tl.at[which])

    def collect(which):
        out, send, receive = routes[which][1:]

        @pl.when(is_main)
        def _():
            keep(which).wait()
            pass_on(out, send, receive, mp).start()
            for index in (other_mid, 0, 3):
                main_arrival(out, send, receive, index).wait_recv()
                pass_on(out, send, receive, index).start()

        @pl.when(is_second)
        def _():
            for index in range(4):
                second_arrival(out, send, receive, index).wait_recv()

    def meta_copies():
        return [
            remote(mod_in, mod_o, ms.at[0], mr.at[0], mate),
            remote(small_in, small_v, ms.at[1], mr.at[1], mate),
        ]

    def par_load(k):
        layer, at = pieces[k]
        return pltpu.make_async_copy(par.at[layer, :, at : at + PIECE], par_f.at[k % 2], psem.at[k % 2])

    def cast_piece(k):
        if k == 0:
            par_load(0).start()
        if k + 1 < count:
            par_load(k + 1).start()
        par_load(k).wait()
        block = 96 if rows % 96 == 0 else rows
        for at in range(0, rows, block):
            wb[k, at : at + block, :] = par_f[k % 2, at : at + block, :].astype(bf16)

    def keep_own(k):
        block = 96 if rows % 96 == 0 else rows
        for at in range(0, rows, block):
            spot = pl.ds(pl.multiple_of(dp * rows + at, 16), block)
            w_v[k, 0, spot, :] = wb[k, at : at + block, :]

    def w_out(k, slot):
        return pltpu.make_async_copy(w_v.at[k, slot], w_o.at[k, slot], wsem.at[k, slot])

    def x_out(turn):
        return pltpu.make_async_copy(x_v.at[turn % 2], xs_o.at[turn], xsem.at[turn])

    def qo_out(layer, slot):
        return pltpu.make_async_copy(qo_v.at[slot % 2], qo_o.at[layer, slot], qsem.at[slot % 2])

    def ad_out(layer, slot):
        return pltpu.make_async_copy(ad_v.at[slot], ad_o.at[layer, slot], asem.at[slot])

    def serve_z(k, *slots):
        for slot in slots:
            z_copy(k, slot, at_mp(other_mid)).wait_recv()
            g_copy(k, slot).start()
            for copy in d_copies(k, slot, True):
                copy.start()

    def serve_g(k, *slots):
        for slot in slots:
            g_copy(k, slot).wait_recv()
            for copy in d_copies(k, slot, False):
                copy.start()

    def ready(k, slot):
        if slot == 0:
            for copy in own_arrivals(k):
                copy.wait_recv()
        else:
            for mine in (True, False):
                for copy in d_arrivals(k, slot, mine):
                    copy.wait_recv()
        w_out(k, slot).start()

    def lifted(layer, kind, turn):
        for span in chunks():
            normed, _ = moments(x_v[turn % 2, span, :])
            shift = row_mod(clip_o[span, :], mod_o, layer, kind)
            scale = row_mod(clip_o[span, :], mod_o, layer, kind + 1)
            u_s[span, :] = (normed * (1.0 + scale) + shift).astype(bf16)
        acc[...] = jnp.zeros_like(acc)

    def branch_rows(layer, kind, turn, span):
        gate = row_mod(clip_o[span, :], mod_o, layer, kind)
        return x_v[1 - turn % 2, span, :] + gate * acc[span, :]

    def add_branch(layer, kind, turn):
        if turn >= 2:
            x_out(turn - 2).wait()
        for span in chunks():
            x_v[turn % 2, span, :] = branch_rows(layer, kind, turn, span)

    def attn_unit(layer, slot):
        k, place = layer * (cols // PIECE), slot % 2
        ready(k, slot)
        if slot >= 2:
            qo_out(layer, slot - 2).wait()
        qo = qo_v.at[place]
        qo[:, : 3 * HW] = mm(u_s[...], w_v[k, slot, :, : 3 * HW], 1, 0).astype(bf16)
        for head in range(HEADS_DEV):
            base = head * HD
            for span, near_by in bands(layer):
                query = qo[span, base : base + HD] * jnp.asarray(0.125, bf16)
                keys = qo[near_by, HW + base : HW + base + HD]
                values = qo[near_by, 2 * HW + base : 2 * HW + base + HD]
                scores = mm(keys, query, 1, 1)
                allowed = idc_o[layer, near_by, :] == idr_o[layer, :, span]
                scores = jnp.where(allowed, scores, neg_fill)
                top = jnp.max(scores, axis=0, keepdims=True)
                raw = jnp.exp(scores - top)
                total = jnp.sum(raw, axis=0, keepdims=True)
                probs = (raw * (1.0 / total)).astype(bf16)
                qo[span, 3 * HW + base : 3 * HW + base + HD] = mm(values, probs, 0, 0).T.astype(bf16)
                lse_o[layer, slot * HEADS_DEV + head, :, span] = top + jnp.log(total)
        acc[...] += mm(qo[:, 3 * HW :], w_v[k, slot, :, 3 * HW :], 1, 1)
        qo_out(layer, slot).start()

    def up_unit(layer, slot):
        k = layer * (cols // PIECE) + 1
        ready(k, slot)
        if layer > 0:
            ad_out(layer - 1, slot).wait()
        for span in chunks():
            hid = mm(u_s[span, :], w_v[k, slot], 1, 0)
            cdf = 0.5 * (1.0 + lax.erf(hid * 0.7071067811865476))
            pdf = jnp.exp(-0.5 * hid * hid) * 0.3989422804014327
            ad_v[slot, 0, span, :] = (hid * cdf).astype(bf16)
            ad_v[slot, 1, span, :] = (cdf + hid * pdf).astype(bf16)
        ad_out(layer, slot).start()

    def down_unit(layer, slot):
        k = layer * (cols // PIECE) + 2
        ready(k, slot)
        acc[...] += mm(ad_v[slot, 0], w_v[k, slot], 1, 1)

    @pl.when(jnp.logical_not(is_main))
    def _():
        route(tok, t_v, ts, tr).start()

    @pl.when(is_main)
    def _():
        keep(0).start()
        keep(1).start()
        for copy in meta_copies():
            copy.start()

    @pl.when(is_outer)
    def _():
        for k in range(count):
            cast_piece(k)
            z_copy(k, 1, at_mp(near)).start()
            z_copy(k, 3, at_mp(far)).start()
        route(cot, c_v, cs, cr).start()
        for k in range(count):
            z_copy(k, 1, at_mp(near)).wait_send()
            z_copy(k, 3, at_mp(far)).wait_send()
        route(tok, t_v, ts, tr).wait_send()
        route(cot, c_v, cs, cr).wait_send()

    @pl.when(is_mid)
    def _():
        for k in range(count):
            cast_piece(k)
            for copy in own_copies(k):
                copy.start()
            z_copy(k, 2, at_mp(other_mid)).start()
            keep_own(k)
        pl.when(is_second)(lambda: route(cot, c_v, cs, cr).start())

        @pl.when(is_main)
        def _():
            mod_o[...] = mod_in[...]
            small_v[...] = small_in[...]

        @pl.when(is_second)
        def _():
            for copy in meta_copies():
                copy.wait_recv()

        column = counted((ROWS, 1), 0)
        line = counted((1, ROWS), 1)
        small = small_v[...]
        for layer in range(L):
            pos_c, clip_c, id_c, from_c = slot_meta(small, column, is_main, layer % 2 == 1)
            clip_o[...] = clip_c
            idc_o[layer] = id_c
            pos_s[layer] = pos_c
            pos_r, _, id_r, from_r = slot_meta(small, line, is_main, layer % 2 == 1)
            idr_o[layer] = id_r
            pos_o[layer] = pos_r
        pos_s[2] = from_c
        pos_o[2] = from_r
        collect(0)
        for span in chunks():
            x_v[0, span, :] = mm(one_hot(pos_s[0, span, :], counted((CHUNK, CAP), 1)), t_v[...], 1, 0)
        x_out(0).start()

        lifted(0, 0, 0)
        attn_unit(0, 0)
        serve_z(0, 1, 2, 3)
        serve_g(0, 1, 2)
        attn_unit(0, 1)
        serve_z(1, 1, 2)
        attn_unit(0, 2)
        serve_g(0, 3)
        serve_z(1, 3)
        attn_unit(0, 3)
        serve_g(1, 1, 2)
        add_branch(0, 2, 1)
        x_out(1).start()
        lifted(0, 3, 1)
        up_unit(0, 0)
        serve_z(2, 1, 2)
        up_unit(0, 1)
        up_unit(0, 2)
        serve_g(1, 3)
        serve_z(2, 3)
        up_unit(0, 3)
        down_unit(0, 0)
        serve_g(2, 1, 2)
        down_unit(0, 1)
        down_unit(0, 2)
        serve_z(3, 1, 2)
        serve_g(2, 3)
        down_unit(0, 3)
        serve_z(3, 3)
        x_out(0).wait()

        @pl.when(is_main)
        def _():
            for index in range(4):
                pass_on(t_v, ts, tr, index).wait_send()

        for span in chunks():
            value = branch_rows(0, 5, 2, span)
            high = value.astype(bf16)
            rest = value - high.astype(f32)
            middle = rest.astype(bf16)
            t_v[span, :] = high
            t_v[slice(ROWS + span.start, ROWS + span.stop), :] = middle
            u_s[span, :] = (rest - middle.astype(f32)).astype(bf16)
        for span in chunks():
            move = one_hot(pos_s[2, span, :], counted((CHUNK, ROWS), 1))
            x_v[0, span, :] = (
                mm(move, t_v[:ROWS, :], 1, 0) + mm(move, t_v[ROWS:, :], 1, 0) + mm(move, u_s[...], 1, 0)
            )
        x_out(2).start()
        lifted(1, 0, 2)
        qo_out(0, 2).wait()
        qo_out(0, 3).wait()
        attn_unit(1, 0)
        serve_g(3, 1, 2)
        serve_z(4, 1, 2)
        attn_unit(1, 1)
        serve_g(3, 3)
        attn_unit(1, 2)
        serve_z(4, 3)
        attn_unit(1, 3)
        serve_g(4, 1, 2)
        add_branch(1, 2, 3)
        x_out(3).start()
        lifted(1, 3, 3)
        serve_z(5, 1, 2)
        up_unit(1, 0)
        up_unit(1, 1)
        serve_g(4, 3)
        serve_z(5, 3)
        up_unit(1, 2)
        up_unit(1, 3)
        down_unit(1, 0)
        serve_g(5, 1, 2)
        down_unit(1, 1)
        down_unit(1, 2)
        serve_g(5, 3)
        down_unit(1, 3)
        for span in chunks():
            xb_o[span, :] = branch_rows(1, 5, 4, span).astype(bf16)
        collect(1)
        for span in chunks():
            g_o[span, :] = mm(one_hot(pos_s[1, span, :], counted((CHUNK, CAP), 1)), c_v[...], 1, 0)
        x_out(2).wait()
        x_out(3).wait()
        for slot in (2, 3):
            qo_out(1, slot).wait()
        for slot in range(4):
            ad_out(1, slot).wait()
        for k in range(count):
            for copy in own_copies(k):
                copy.wait_send()
            for slot in range(4):
                w_out(k, slot).wait()
            for slot in (1, 2, 3):
                g_copy(k, slot).wait_send()
                for mine in (True, False):
                    for copy in d_copies(k, slot, mine):
                        copy.wait_send()
        for k in range(count):
            z_copy(k, 2, at_mp(other_mid)).wait_send()

    @pl.when(is_main)
    def _():
        for copy in meta_copies():
            copy.wait_send()
        for index in range(4):
            pass_on(c_v, cs, cr, index).wait_send()

    @pl.when(is_second)
    def _():
        route(tok, t_v, ts, tr).wait_send()
        route(cot, c_v, cs, cr).wait_send()


def run_forward(tok, cot, mod, small, par):
    sds = jax.ShapeDtypeStruct
    n_dp = lax.axis_size("dp")
    rows, cols = par.shape[1], par.shape[2]
    count = L * cols // PIECE
    peers = n_dp - 1
    return pl.pallas_call(
        partial(fwd_kernel, n_dp),
        out_shape=(
            sds((count, 4, D, PIECE), bf16), sds((2 * L, ROWS, D), f32), sds((L, 4, ROWS, D), bf16),
            sds((L, 4, 2, ROWS, FF // 4), bf16), sds((L, HEADS, 1, ROWS), f32), sds((ROWS, D), f32),
            sds((ROWS, D), bf16), sds((ROWS, 1), f32), sds((L, ROWS, 1), f32), sds((L, 1, ROWS), f32),
            sds((3, 1, ROWS), f32), sds(mod.shape, f32),
        ),
        in_specs=[any_spec(), any_spec(), vm_spec(), vm_spec(), any_spec()],
        out_specs=(any_spec(),) * 4 + (vm_spec(),) * 8,
        scratch_shapes=[
            VM((count, 4, D, PIECE), bf16), VM((count, rows, PIECE), bf16), VM((2, rows, PIECE), f32),
            VM((CAP, D), bf16), VM((CAP, D), bf16), VM((2, ROWS, D), f32), VM((ROWS, D), bf16),
            VM((ROWS, D), f32), VM((2, ROWS, D), bf16), VM((4, 2, ROWS, FF // 4), bf16), VM((8, 128), f32),
            VM((3, ROWS, 1), f32),
            DMA((count, 3)), DMA((count, 3)), DMA((count, 3)), DMA((count, 3)),
            DMA((count, 3, 2, peers)), DMA((count, 3, 2, peers)), DMA((count, peers)), DMA((count, peers)),
            DMA((5,)), DMA((8,)), DMA((5,)), DMA((8,)), DMA((2,)), DMA((2,)), DMA((2,)),
            DMA((2,)), DMA((count, 4)), DMA((2 * L,)), DMA((2,)), DMA((4,)),
        ],
        compiler_params=pltpu.CompilerParams(
            collective_id=1, has_side_effects=True, vmem_limit_bytes=63 * MIB
        ),
    )(tok, cot, mod, small, par)


def share_rows(rows, n_grp):
    part = rows // n_grp
    return part if part * n_grp == rows and part % 16 == 0 else rows


def back_kernel(
    n_dp, n_grp,
    xb, pos_r, g_in, clip, idc, idr, mods, lse, xs, qo, ad,
    w_hbm, par, mom, var,
    recv, avg, mix_o, gin_o,
    g_s, x_b, w_b, a_b, q_b, u_t, d_s, d_t, dh, dq, do_s, dk_s, acc, out, inbox, stage,
    p_b, p_in, opt, gsum, diff, box, own_avg,
    xsem, wsem, asem, ce_s, ce_r, os_s, os_r, loc, pe_s, pe_r, ro_s, ro_r, rl, osem,
    as_s, as_r, bs_s, bs_r, bl,
):
    grp, dp, mp = lax.axis_index("grp"), lax.axis_index("dp"), lax.axis_index("mp")
    rows, cols = par.shape[1], par.shape[2]
    quarter = mix_o.shape[0]
    share = share_rows(rows, n_grp)
    star = 1 + lax.rem(dp, 2)
    is_mid = jnp.logical_or(mp == 1, mp == 2)
    is_outer = jnp.logical_not(is_mid)
    is_main = mp == star
    is_second = jnp.logical_and(is_mid, mp != star)
    other_mid = 3 - mp
    near_outer = jnp.where(mp == 1, 0, 3)
    far_outer = 3 - near_outer
    heads = HEADS_DEV
    hw = HW
    mate = (grp, flip(dp, 1), mp)

    def at_mp(where):
        return (grp, dp, where)

    def at_grp(step):
        return (lax.rem(grp + step, n_grp), dp, mp)

    def at_dp(step):
        return (grp, lax.rem(dp + step, n_dp), mp)

    peers = [at_grp(step) for step in range(1, n_grp)]

    @pl.when(is_mid)
    def _():
        greet(
            [at_mp(0), at_mp(3), at_mp(other_mid)] + peers + [at_dp(step) for step in range(1, n_dp)]
        )

    @pl.when(is_outer)
    def _():
        greet([at_mp(1), at_mp(2)] + peers)

    def layer_of(sub):
        return 1 - sub // 2

    def slot_of(step):
        return 3 - step % 4

    units = []
    for sub in range(4):
        steps = range(4 * sub, 4 * sub + 4)
        if sub % 2:
            units += [(step, "attn") for step in steps]
        else:
            units += [(step, kind) for step in steps for kind in ("down", "up")]
    units[1], units[2] = units[2], units[1]

    def piece_of(unit):
        step, kind = units[unit]
        return layer_of(step // 4), {"attn": 0, "up": PIECE, "down": 2 * PIECE}[kind]

    def index_of(piece):
        return piece[0] * (cols // PIECE) + piece[1] // PIECE

    def halves(piece):
        return [(0, SIDE), (SIDE, PIECE)] if piece == (0, 0) else [(0, PIECE)]

    def weight_loads(step):
        sub, slot, place = step // 4, slot_of(step), step % 2
        first = layer_of(sub) * (cols // PIECE) + (1 if sub % 2 == 0 else 0)
        return [
            pltpu.make_async_copy(
                w_hbm.at[first + turn, slot], w_b.at[place, :, turn * D : turn * D + D], wsem.at[place, turn]
            )
            for turn in range(2 if sub % 2 == 0 else 1)
        ]

    def kept_load(step):
        sub, slot, place = step // 4, slot_of(step), step % 2
        layer = layer_of(sub)
        if sub % 2 == 0:
            return pltpu.make_async_copy(ad.at[layer, slot], a_b.at[place], asem.at[place])
        return pltpu.make_async_copy(qo.at[layer, slot], q_b.at[place], asem.at[place])

    def load(step):
        for copy in (kept_load(step), *weight_loads(step)):
            copy.start()

    def x_load(sub):
        source = xs.at[2 * layer_of(sub) + (1 if sub % 2 == 0 else 0)]
        return pltpu.make_async_copy(source, x_b.at[sub % 2], xsem.at[sub % 2])

    def exchange(unit):
        place = unit % 2
        result = []
        for hop in range(1, n_dp):
            target = lax.rem(dp + hop, n_dp)
            result.append(
                remote(
                    out.at[place, pl.ds(pl.multiple_of(target * rows, rows), rows)],
                    inbox.at[place, hop - 1],
                    ce_s.at[unit, hop - 1], ce_r.at[unit, hop - 1], at_dp(hop),
                )
            )
        return result

    def to_owner(unit, turns=(0, 1)):
        piece, slot = piece_of(unit), slot_of(units[unit][0])
        plane, index = (1 if slot >= 2 else 0), index_of(piece)
        result = []
        for turn, (low, high) in enumerate(halves(piece)):
            if turn not in turns:
                continue
            source = stage.at[unit, :, low:high]
            place = recv.at[plane, piece[0], :, piece[1] + low : piece[1] + high]
            if slot == 0:
                result.append(pltpu.make_async_copy(source, place, loc.at[index, turn]))
            else:
                device = at_mp((None, near_outer, other_mid, far_outer)[slot])
                result.append(
                    remote(source, place, os_s.at[unit, turn], os_r.at[index, plane, turn], device)
                )
        return result

    def owner_arrival(piece, plane, turn):
        low, high = halves(piece)[turn]
        place = recv.at[plane, piece[0], :, piece[1] + low : piece[1] + high]
        return remote(place, place, os_s.at[0, 0], os_r.at[index_of(piece), plane, turn], mate)

    def finish(unit):
        place = unit % 2
        for copy in exchange(unit):
            copy.wait_recv()
        block = 96 if rows % 96 == 0 else rows
        for at in range(0, rows, block):
            mine = pl.ds(pl.multiple_of(dp * rows + at, 16), block)
            total = out[place, mine, :].astype(f32)
            for hop in range(1, n_dp):
                total = total + inbox[place, hop - 1, at : at + block, :].astype(f32)
            stage[unit, at : at + block, :] = total.astype(bf16)
        for copy in exchange(unit):
            copy.wait_send()
        for copy in to_owner(unit):
            copy.start()

    def put_rows(which, values):
        for at in range(0, CAP, 256):
            place = one_hot(counted((256, ROWS), 0, at), pos_r[1 - which])
            p_b[at : at + 256, :] = mm(place, values, 1, 0).astype(bf16)

        @pl.when(is_second)
        def _():
            remote(p_b, p_in, pe_s.at[which], pe_r.at[which], mate).start()

    def quarter_of(index):
        return pl.ds(pl.multiple_of(index * quarter, quarter), quarter)

    def row_copies(which, dest):
        return [
            remote(
                p_b.at[quarter_of(index)], dest, ro_s.at[which, turn], ro_r.at[which], at_mp(index)
            )
            for turn, index in enumerate((other_mid, 0, 3))
        ]

    def send_rows(which, dest):
        @pl.when(is_main)
        def _():
            remote(p_b, p_in, pe_s.at[which], pe_r.at[which], mate).wait_recv()
            for at in range(0, CAP, 256):
                span = slice(at, at + 256)
                p_b[span, :] = p_b[span, :] + p_in[span, :]
            for copy in row_copies(which, dest):
                copy.start()
            pltpu.make_async_copy(p_b.at[quarter_of(mp)], dest, rl.at[which]).start()

    def end_rows(which, dest):
        @pl.when(is_main)
        def _():
            for copy in row_copies(which, dest):
                copy.wait_send()
            pltpu.make_async_copy(p_b.at[quarter_of(mp)], dest, rl.at[which]).wait()

        @pl.when(is_second)
        def _():
            remote(p_b, p_in, pe_s.at[which], pe_r.at[which], mate).wait_send()

    def rows_arrived(which, dest):
        @pl.when(jnp.logical_not(is_main))
        def _():
            remote(
                p_b.at[quarter_of(0)], dest, ro_s.at[which, 0], ro_r.at[which], at_mp(0)
            ).wait_recv()

    def diff_piece(piece, turn):
        layer, index = piece[0], index_of(piece)
        low, high = halves(piece)[turn]
        width = high - low
        span = slice(piece[1] + low, piece[1] + high)
        block = opt.shape[2]

        def opt_loads(lap):
            part, place = slice(lap * block, (lap + 1) * block), lap % 2
            return [
                pltpu.make_async_copy(
                    source.at[layer, part, span], opt.at[place, i, :, :width], osem.at[place, i]
                )
                for i, source in enumerate((par, mom, var))
            ] + [
                pltpu.make_async_copy(
                    recv.at[plane, layer, part, span], gsum.at[place, plane, :, :width],
                    osem.at[place, 3 + plane],
                )
                for plane in range(2)
            ]

        @pl.when(is_outer)
        def _():
            owner_arrival(piece, 0, turn).wait_recv()

        @pl.when(is_mid)
        def _():
            own = [u for u in range(len(units)) if piece_of(u) == piece and slot_of(units[u][0]) == 0][0]
            to_owner(own, (turn,))[0].wait()

        owner_arrival(piece, 1, turn).wait_recv()
        for copy in opt_loads(0):
            copy.start()
        for lap in range(rows // block):
            part, place = slice(lap * block, (lap + 1) * block), lap % 2
            if (lap + 1) * block < rows:
                for copy in opt_loads(lap + 1):
                    copy.start()
            for copy in opt_loads(lap):
                copy.wait()
            grad = gsum[place, 0, :, :width].astype(f32) + gsum[place, 1, :, :width].astype(f32)
            one = beta_one * opt[place, 1, :, :width] + (1 - beta_one) * grad
            two = beta_two * opt[place, 2, :, :width] + (1 - beta_two) * grad * grad
            step = one / (1 - beta_one**STEP) / (jnp.sqrt(two / (1 - beta_two**STEP)) + adam_eps)
            diff[index, part, low:high] = (
                inner_rate * (step + decay_rate * opt[place, 0, :, :width])
            ).astype(bf16)
        for copy in first_copies(piece, turn):
            copy.start()

    def rows_for(where):
        if share == rows:
            return slice(0, rows)
        return pl.ds(pl.multiple_of(where * share, share), share)

    def first_copies(piece, turn):
        index = index_of(piece)
        low, high = halves(piece)[turn]
        return [
            remote(
                diff.at[index, rows_for(lax.rem(grp + hop, n_grp)), low:high],
                box.at[index, hop - 1, :, low:high],
                as_s.at[index, turn, hop - 1], as_r.at[index, turn, hop - 1], at_grp(hop),
            )
            for hop in range(1, n_grp)
        ]

    def second_copies(piece, turn):
        index = index_of(piece)
        low, high = halves(piece)[turn]
        place = avg.at[piece[0], rows_for(grp), piece[1] + low : piece[1] + high]
        return [
            remote(
                own_avg.at[index, :, low:high], place,
                bs_s.at[index, turn, hop - 1], bs_r.at[index, turn, hop - 1], at_grp(hop),
            )
            for hop in range(1, n_grp)
        ]

    def second_arrivals(piece, turn):
        index = index_of(piece)
        low, high = halves(piece)[turn]
        result = []
        for hop in range(1, n_grp):
            source = lax.rem(grp + n_grp - hop, n_grp)
            place = avg.at[piece[0], rows_for(source), piece[1] + low : piece[1] + high]
            result.append(
                remote(
                    place, place, bs_s.at[index, turn, hop - 1], bs_r.at[index, turn, hop - 1], at_grp(hop)
                )
            )
        return result

    def own_copy(piece, turn):
        index = index_of(piece)
        low, high = halves(piece)[turn]
        place = avg.at[piece[0], rows_for(grp), piece[1] + low : piece[1] + high]
        return pltpu.make_async_copy(own_avg.at[index, :, low:high], place, bl.at[index, turn])

    def mean_piece(piece, turn):
        index = index_of(piece)
        low, high = halves(piece)[turn]
        for copy in first_copies(piece, turn):
            copy.wait_recv()
        total = diff[index, rows_for(grp), low:high].astype(f32)
        for hop in range(1, n_grp):
            total = total + box[index, hop - 1, :, low:high].astype(f32)
        own_avg[index, :, low:high] = (total / n_grp).astype(bf16)
        own_copy(piece, turn).start()
        if share != rows:
            for copy in second_copies(piece, turn):
                copy.start()

    def end_piece(piece, turn):
        for copy in first_copies(piece, turn):
            copy.wait_send()
        own_copy(piece, turn).wait()
        if share != rows:
            for copy in second_copies(piece, turn):
                copy.wait_send()
            for copy in second_arrivals(piece, turn):
                copy.wait_recv()

    def down_start(sub):
        layer = layer_of(sub)
        for part in chunks():
            down = row_mod(clip[part, :], mods, layer, 5) * g_s[part, :]
            d_s[part, :] = down.astype(bf16)
            d_t[:, part] = down.T.astype(bf16)

    def up_start(sub):
        layer, place = layer_of(sub), sub % 2
        x_load(sub).wait()
        for part in chunks():
            normed, _ = moments(x_b[place, part, :])
            shift = row_mod(clip[part, :], mods, layer, 3)
            scale = row_mod(clip[part, :], mods, layer, 4)
            u_t[:, part] = (normed * (1.0 + scale) + shift).T.astype(bf16)
        acc[...] = jnp.zeros_like(acc)

    def down_unit(step, turn):
        out[turn] = mm(d_t[...], a_b[step % 2, 0], 1, 0).astype(bf16)

    def up_unit(step, turn):
        place = step % 2
        for part in chunks():
            dact = mm(d_s[part, :], w_b[place, :, D:], 1, 0)
            dh[part, :] = (dact * a_b[place, 1, part, :].astype(f32)).astype(bf16)
        out[turn] = mm(u_t[...], dh[...], 1, 0).astype(bf16)
        acc[...] += mm(dh[...], w_b[place, :, :D], 1, 1)

    def attn_start(sub):
        layer, place = layer_of(sub), sub % 2
        x_load(sub).wait()
        for part in chunks():
            normed, _ = moments(x_b[place, part, :])
            shift = row_mod(clip[part, :], mods, layer, 0)
            scale = row_mod(clip[part, :], mods, layer, 1)
            u_t[:, part] = (normed * (1.0 + scale) + shift).T.astype(bf16)
            branch = row_mod(clip[part, :], mods, layer, 2) * g_s[part, :]
            d_s[part, :] = branch.astype(bf16)
            d_t[:, part] = branch.T.astype(bf16)
        acc[...] = jnp.zeros_like(acc)

    def attn_unit(step, turn):
        layer, place, slot = layer_of(step // 4), step % 2, slot_of(step)
        out[turn, :, 3 * hw : D] = mm(d_t[...], q_b[place, :, 3 * hw :], 1, 0).astype(bf16)
        do_s[...] = mm(d_s[...], w_b[place, :, 3 * hw : D], 1, 0).astype(bf16)
        for head in range(heads):
            base = head * HD
            dk_s[...] = jnp.zeros_like(dk_s)
            for span, near_by in bands(layer):
                query = q_b[place, span, base : base + HD]
                keys = q_b[place, near_by, hw + base : hw + base + HD]
                values = q_b[place, near_by, 2 * hw + base : 2 * hw + base + HD]
                grad = do_s[span, base : base + HD]
                scores = mm(keys, query * jnp.asarray(0.125, bf16), 1, 1)
                allowed = idc[layer, near_by, :] == idr[layer, :, span]
                probs = jnp.where(
                    allowed, jnp.exp(scores - lse[layer, slot * heads + head, :, span]), 0.0
                )
                dk_s[1, near_by, :] += mm(probs.astype(bf16), grad, 1, 0)
                weighted = probs * mm(values, grad, 1, 1)
                delta = jnp.sum(weighted, axis=0, keepdims=True)
                ds = (weighted - probs * delta).astype(bf16)
                dq[span, base : base + HD] = (mm(keys, ds, 0, 0).T * 0.125).astype(bf16)
                dk_s[0, near_by, :] += mm(ds, query, 1, 0)
            dq[:, hw + base : hw + base + HD] = (dk_s[0] * 0.125).astype(bf16)
            dq[:, 2 * hw + base : 2 * hw + base + HD] = dk_s[1].astype(bf16)
        out[turn, :, : 3 * hw] = mm(u_t[...], dq[...], 1, 0).astype(bf16)
        acc[...] += mm(dq[...], w_b[place, :, : 3 * hw], 1, 1)

    def sub_end(sub):
        layer, place = layer_of(sub), sub % 2
        row = 4 if sub % 2 == 0 else 1
        for part in chunks():
            normed, inv_std = moments(x_b[place, part, :])
            scale = row_mod(clip[part, :], mods, layer, row)
            g_s[part, :] = g_s[part, :] + norm_back(acc[part, :] * (1.0 + scale), normed, inv_std)

    def to_frame_order():
        for part in chunks():
            high = g_s[part, :].astype(bf16)
            dh[part, :] = high
            d_s[part, :] = (g_s[part, :] - high.astype(f32)).astype(bf16)
        for part in chunks():
            move = one_hot(counted((CHUNK, ROWS), 0, part.start), pos_r[2])
            g_s[part, :] = mm(move, dh[...], 1, 0) + mm(move, d_s[...], 1, 0)

    def chunk(sub, kind):
        return layer_of(sub), {"attn": 0, "up": PIECE, "down": 2 * PIECE}[kind]

    order = [chunk(0, "down"), chunk(0, "up"), chunk(1, "attn"), chunk(2, "down"), chunk(2, "up"), chunk(3, "attn")]
    served = {13: (diff_piece, 0), 16: (mean_piece, 0), 18: (diff_piece, 1), 21: (mean_piece, 1)}

    @pl.when(is_mid)
    def _():
        x_load(0).start()
        load(0)
        load(1)
        g_s[...] = g_in[...]
        for unit, (step, kind) in enumerate(units):
            sub = step // 4
            first_of_sub = unit == 0 or units[unit - 1][0] // 4 != sub
            last_of_step = unit + 1 == len(units) or step not in [s for s, _ in units[unit + 1 :]]
            last_of_sub = unit + 1 == len(units) or units[unit + 1][0] // 4 != sub
            if first_of_sub:
                if sub < 3:
                    x_load(sub + 1).start()
                (attn_start if kind == "attn" else down_start)(sub)
            if kind != "up":
                kept_load(step).wait()
            if kind != "down":
                if kind == "up" and step % 4 == 0:
                    up_start(sub)
                for copy in weight_loads(step):
                    copy.wait()
            {"attn": attn_unit, "up": up_unit, "down": down_unit}[kind](step, unit % 2)
            if unit > 0:
                finish(unit - 1)
            for copy in exchange(unit):
                copy.start()
            if last_of_step and step + 2 < 16:
                load(step + 2)
            if unit == 3:
                put_rows(0, xb[...])
            if unit == 5:
                send_rows(0, mix_o)
            if last_of_sub:
                sub_end(sub)
                if sub == 1:
                    to_frame_order()
            if unit in served:
                action, which = served[unit]
                action(order[which], 0)
        end_rows(0, mix_o)
        put_rows(1, g_s[...].astype(bf16))
        finish(len(units) - 1)
        send_rows(1, gin_o)
        for piece in order[2:5]:
            diff_piece(piece, 0)
            mean_piece(piece, 0)
        for turn in range(2):
            diff_piece(order[5], turn)
        for turn in range(2):
            mean_piece(order[5], turn)
        for unit, (step, _) in enumerate(units):
            if slot_of(step) != 0:
                for copy in to_owner(unit):
                    copy.wait_send()
        end_rows(1, gin_o)

    @pl.when(is_outer)
    def _():
        for piece in order[:5]:
            diff_piece(piece, 0)
            mean_piece(piece, 0)
        for turn in range(2):
            diff_piece(order[5], turn)
        for turn in range(2):
            mean_piece(order[5], turn)

    for which, dest in ((0, mix_o), (1, gin_o)):
        rows_arrived(which, dest)
    for piece in order:
        for turn in range(len(halves(piece))):
            end_piece(piece, turn)


def run_back(xb, pos, g, clip, idc, idr, mods, lse, xs, qo, ad, w, par, mom, var, quarter):
    sds = jax.ShapeDtypeStruct
    n_dp, n_grp = lax.axis_size("dp"), lax.axis_size("grp")
    rows, cols = par.shape[1], par.shape[2]
    share = share_rows(rows, n_grp)
    count = L * cols // PIECE
    far, peers = n_dp - 1, n_grp - 1
    block = 96 if rows % 96 == 0 else rows
    return pl.pallas_call(
        partial(back_kernel, n_dp, n_grp),
        out_shape=(
            sds((2, L, rows, cols), bf16), sds((L, rows, cols), bf16),
            sds((quarter, D), bf16), sds((quarter, D), bf16),
        ),
        in_specs=[vm_spec()] * 8 + [any_spec()] * 7,
        out_specs=(any_spec(),) * 4,
        scratch_shapes=[
            VM((ROWS, D), f32), VM((2, ROWS, D), f32), VM((2, D, 2 * D), bf16),
            VM((2, 2, ROWS, D), bf16), VM((2, ROWS, D), bf16),
            VM((D, ROWS), bf16), VM((ROWS, D), bf16), VM((D, ROWS), bf16), VM((ROWS, D), bf16),
            VM((ROWS, 9 * HD), bf16), VM((ROWS, 3 * HD), bf16), VM((2, ROWS, HD), f32), VM((ROWS, D), f32),
            VM((2, D, PIECE), bf16), VM((2, far, rows, PIECE), bf16), VM((4 * count, rows, PIECE), bf16),
            VM((CAP, D), bf16), VM((CAP, D), bf16),
            VM((2, 3, block, PIECE), f32), VM((2, 2, block, PIECE), bf16),
            VM((count, rows, PIECE), bf16), VM((count, peers, share, PIECE), bf16),
            VM((count, share, PIECE), bf16),
            DMA((2,)), DMA((2, 2)), DMA((2,)), DMA((4 * count, far)), DMA((4 * count, far)),
            DMA((4 * count, 2)), DMA((count, 2, 2)), DMA((count, 2)),
            DMA((2,)), DMA((2,)), DMA((2, 3)), DMA((2,)), DMA((2,)), DMA((2, 5)),
            DMA((count, 2, peers)), DMA((count, 2, peers)), DMA((count, 2, peers)), DMA((count, 2, peers)),
            DMA((count, 2)),
        ],
        compiler_params=pltpu.CompilerParams(
            collective_id=2, has_side_effects=True, vmem_limit_bytes=63 * MIB
        ),
    )(xb, pos, g, clip, idc, idr, mods, lse, xs, qo, ad, w, par, mom, var)


def last_kernel(
    par, mom, var, out_mom, ga, gb, avg, rows_m, rows_g, tok, live,
    new_m, new_v, out_a, out_m, out_w, out_l, mixed, grad_in,
):
    @pl.when(jnp.logical_and(pl.program_id(0) == 0, pl.program_id(1) == 0))
    def _():
        mixed[...] = jnp.where(live[...] > 0.0, rows_m[...].astype(f32), tok[...].astype(f32)).astype(bf16)
        grad_in[...] = jnp.where(live[...] > 0.0, rows_g[...].astype(f32), 0.0)

    grad = ga[...].astype(f32) + gb[...].astype(f32)
    new_m[...] = beta_one * mom[...] + (1 - beta_one) * grad
    new_v[...] = beta_two * var[...] + (1 - beta_two) * grad * grad
    average = avg[...].astype(f32)
    momentum = outer_mu * out_mom[...] + average
    updated = par[...] - outer_rate * (average + outer_mu * momentum)
    out_a[...] = average
    out_m[...] = momentum
    out_w[...] = updated
    out_l[...] = updated.astype(bf16)


def run_last(par, mom, var, out_mom, recv, avg, rows_m, rows_g, tok, live):
    rows, cols = par.shape[1], par.shape[2]
    block = 96 if rows % 96 == 0 else rows
    sds = jax.ShapeDtypeStruct
    full = pl.BlockSpec((None, block, cols), lambda i, j: (i, j, 0))

    def plane(which):
        return pl.BlockSpec((None, None, block, cols), lambda i, j: (which, i, j, 0))

    return pl.pallas_call(
        last_kernel,
        grid=(L, rows // block),
        out_shape=(sds(par.shape, f32),) * 5 + (sds(par.shape, bf16), sds(tok.shape, bf16), sds(tok.shape, f32)),
        in_specs=[full] * 4 + [plane(0), plane(1), full] + [vm_spec()] * 4,
        out_specs=(full,) * 6 + (vm_spec(),) * 2,
        compiler_params=pltpu.CompilerParams(vmem_limit_bytes=62 * MIB),
    )(par, mom, var, out_mom, recv, recv, avg, rows_m, rows_g, tok, live)


def body(
    tokens, cotangent, modulation, clip_frames, clip_patches, params, first_moment, second_moment,
    outer_momentum,
):
    mp = lax.axis_index("mp")
    quarter = tokens.shape[1]
    small = jnp.concatenate([clip_frames, clip_patches], axis=0).astype(f32)
    small = jnp.pad(small, ((0, 6), (0, 128 - SLOTS)))
    w, xs, qo, ad, lse, gradient, xb, clip, idc, idr, pos, mods = run_forward(
        tokens[0], cotangent[0], modulation[0], small, params
    )
    recv, avg, mixed_rows, grad_rows = run_back(
        xb, pos, gradient, clip, idc, idr, mods, lse, xs, qo, ad, w,
        params, first_moment[0], second_moment[0], quarter,
    )
    total = jnp.sum(clip_frames[0] * clip_patches[0])
    own_live = (mp * quarter + jnp.arange(quarter, dtype=jnp.int32) < total).astype(f32)[:, None]
    new_m, new_v, average, momentum, updated, low, mixed, input_grad = run_last(
        params, first_moment[0], second_moment[0], outer_momentum, recv, avg,
        mixed_rows, grad_rows, tokens[0], own_live,
    )
    return (
        mixed[None], input_grad[None], new_m[None], new_v[None], average, momentum, updated, low,
    )


def solution(mesh):
    in_specs = (
        P("grp", ("dp", "mp"), None),
        P("grp", ("dp", "mp"), None),
        P("grp", "dp", None),
        P("grp", "dp"),
        P("grp", "dp"),
        P(None, "dp", "mp"),
        P("grp", None, "dp", "mp"),
        P("grp", None, "dp", "mp"),
        P(None, "dp", "mp"),
    )
    out_specs = (
        P("grp", ("dp", "mp"), None),
        P("grp", ("dp", "mp"), None),
        P("grp", None, "dp", "mp"),
        P("grp", None, "dp", "mp"),
        P(None, "dp", "mp"),
        P(None, "dp", "mp"),
        P(None, "dp", "mp"),
        P(None, "dp", "mp"),
    )
    return jax.shard_map(body, mesh=mesh, in_specs=in_specs, out_specs=out_specs, check_vma=False)
```

```python
from functools import partial

import jax
import jax.numpy as jnp
from jax import lax
from jax.experimental import pallas as pl
from jax.experimental.pallas import tpu as pltpu
from jax.sharding import PartitionSpec as P

D = 768
HEADS = 12
HD = 64
FF = 3072
L = 2
STEP = 5
CAP = 1024
SLOTS = 4
LONGF = 64
ROWS = CAP // 2
CHUNK = 128
PIECE = 768
SIDE = PIECE // 2

ln_eps = 1e-06
neg_fill = -1e30
beta_one = 0.9
beta_two = 0.999
adam_eps = 1e-08
inner_rate = 0.04
decay_rate = 0.1
outer_rate = 0.7
outer_mu = 0.5

f32 = jnp.float32
bf16 = jnp.bfloat16
VM = pltpu.VMEM
DMA = pltpu.SemaphoreType.DMA
MESH_ID = pl.DeviceIdType.MESH
MIB = 2**20
HEADS_DEV = 3
HW = HEADS_DEV * HD


def mm(left, right, lc, rc):
    return lax.dot_general(left, right, (((lc,), (rc,)), ((), ())), preferred_element_type=f32)


def moments(values):
    centered = values - jnp.mean(values, axis=-1, keepdims=True)
    inv_std = lax.rsqrt(jnp.mean(centered * centered, axis=-1, keepdims=True) + ln_eps)
    return centered * inv_std, inv_std


def norm_back(grad_normed, normed, inv_std):
    inner = grad_normed - jnp.mean(grad_normed, axis=-1, keepdims=True)
    inner = inner - normed * jnp.mean(grad_normed * normed, axis=-1, keepdims=True)
    return inv_std * inner


def split_table(table):
    high = table.astype(bf16).astype(f32)
    rest = table - high
    middle = rest.astype(bf16).astype(f32)
    return jnp.concatenate([high, middle, rest - middle, jnp.zeros_like(table)], axis=0).astype(bf16)


def row_mod(hot, tables, layer, kind):
    return mm(hot, tables[layer * 6 + kind], 1, 0)


def chunks():
    return [slice(at, at + CHUNK) for at in range(0, ROWS, CHUNK)]


def any_spec():
    return pl.BlockSpec(memory_space=pl.ANY)


def vm_spec():
    return pl.BlockSpec(memory_space=VM)


def flip(index, bit):
    return index + bit - 2 * bit * lax.rem(index // bit, 2)


def slot_meta(small, index, long_core, by_patch):
    frames = [small[0:1, clip : clip + 1] for clip in range(SLOTS)]
    patches = [small[1:2, clip : clip + 1] for clip in range(SLOTS)]
    zero = jnp.zeros_like(frames[0])
    start, long_start, long_size = zero, zero, zero
    starts, ends = [], []
    for clip in range(SLOTS):
        size = frames[clip] * patches[clip]
        is_long = frames[clip] == float(LONGF)
        long_start = long_start + jnp.where(is_long, start, 0.0)
        long_size = long_size + jnp.where(is_long, size, 0.0)
        starts.append(start)
        start = start + size
        ends.append(start)
    pos_long = index + long_start
    pos_short = jnp.where(index < long_start, index, index + long_size)
    pos = jnp.where(long_core, pos_long, pos_short)
    clip_of = jnp.zeros_like(index)
    for clip in range(SLOTS):
        clip_of = clip_of + jnp.where(pos >= ends[clip], 1.0, 0.0)
    limit = jnp.where(long_core, long_start + long_size, start)
    live = pos < limit
    clip_of = jnp.where(live, clip_of, float(SLOTS))
    begin, many, wide = jnp.zeros_like(index), jnp.ones_like(index), jnp.ones_like(index)
    for clip in range(SLOTS):
        hit = clip_of == float(clip)
        begin = jnp.where(hit, starts[clip], begin)
        many = jnp.where(hit, frames[clip], many)
        wide = jnp.where(hit, patches[clip], wide)
    offset = pos - begin
    inner = many if by_patch else wide
    group = jnp.floor((offset + 0.5) / inner)
    within = offset - group * inner
    source = within * wide + group if by_patch else offset
    ident = jnp.where(live, clip_of * CAP + group, -1.0 - index)
    origin = jnp.where(live, index - offset + source, index)
    return jnp.where(live, begin + source, -1.0), clip_of, ident, origin


def one_hot(left, right):
    return jnp.where(left == right, 1.0, 0.0).astype(bf16)


def counted(shape, dim, first=0):
    return lax.broadcasted_iota(jnp.int32, shape, dim).astype(f32) + float(first)


def bands(layer):
    halo = 32 if layer % 2 == 0 else 64
    return [
        (slice(at, at + CHUNK), slice(max(at - halo, 0), min(at + CHUNK + halo, ROWS)))
        for at in range(0, ROWS, CHUNK)
    ]


def remote(src, dst, send, receive, device):
    return pltpu.make_async_remote_copy(
        src_ref=src, dst_ref=dst, send_sem=send, recv_sem=receive,
        device_id=device, device_id_type=MESH_ID,
    )


def greet(devices):
    barrier = pltpu.get_barrier_semaphore()
    for device in devices:
        pl.semaphore_signal(barrier, inc=1, device_id=device, device_id_type=MESH_ID)
    pl.semaphore_wait(barrier, len(devices))


def fwd_kernel(
    n_dp, tok, cot, mod_in, small_in, par,
    w_o, xs_o, qo_o, ad_o, early_o, rows_o, lse_o, g_o, hot_o, idc_o, idr_o, pos_o, tab_o,
    w_v, wb, par_f, t_v, c_v, x_v, u_s, acc, qo_v, ad_v, small_v, mod_v, pos_s, d_t, out, inbox, stage,
    zs, zr, gs, gr, ds, dr, os_s, os_r, ts, tr, cs, cr, tl, ms, mr, psem, wsem, xsem, qsem, asem, ce_s, ce_r, ow_s, ow_r, pe_s, pe_r, psend,
):
    grp, dp, mp = lax.axis_index("grp"), lax.axis_index("dp"), lax.axis_index("mp")
    rows, cols = par.shape[1], par.shape[2]
    quarter = tok.shape[0]
    pieces = [(layer, at) for layer in range(L) for at in range(0, cols, PIECE)]
    count = len(pieces)
    star = 1 + lax.rem(dp, 2)
    is_mid = jnp.logical_or(mp == 1, mp == 2)
    is_outer = jnp.logical_not(is_mid)
    is_main = mp == star
    is_second = jnp.logical_and(is_mid, mp != star)
    other_mid = 3 - mp
    near = jnp.where(mp == 0, 1, 2)
    far = 3 - near
    my_rows = pl.ds(pl.multiple_of(dp * rows, rows), rows)
    mate = (grp, flip(dp, 1), mp)
    hops = range(1, n_dp)

    def at_mp(where):
        return (grp, dp, where)

    def at_grp(bit):
        return (flip(grp, bit), dp, mp)

    def at_dp(step):
        return (grp, lax.rem(dp + step, n_dp), mp)

    @pl.when(is_mid)
    def _():
        greet(
            [at_mp(0), at_mp(3), at_mp(other_mid), at_grp(1), at_grp(2)] + [at_dp(hop) for hop in hops]
        )

    @pl.when(is_outer)
    def _():
        greet([at_mp(1), at_mp(2)])

    def bit_of(k, slot):
        return 1 + (k + slot) % 2

    def half(k, slot, mine):
        index = lax.rem(grp // bit_of(k, slot), 2)
        if not mine:
            index = 1 - index
        return pl.ds(pl.multiple_of(index * SIDE, 128), SIDE)

    def z_copy(k, slot, device):
        span = half(k, slot, True)
        return remote(
            wb.at[k, :, span], w_v.at[k, slot, my_rows, span], zs.at[k, slot - 1], zr.at[k, slot - 1], device
        )

    def g_copy(k, slot):
        place = w_v.at[k, slot, my_rows, half(k, slot, True)]
        return remote(place, place, gs.at[k, slot - 1], gr.at[k, slot - 1], at_grp(bit_of(k, slot)))

    def d_copies(k, slot, mine):
        place, turn = w_v.at[k, slot, my_rows, half(k, slot, mine)], 0 if mine else 1
        return [
            remote(
                place, place, ds.at[k, slot - 1, turn, hop - 1], dr.at[k, slot - 1, turn, hop - 1], at_dp(hop)
            )
            for hop in hops
        ]

    def rows_of(hop):
        source = lax.rem(dp + n_dp - hop, n_dp)
        return pl.ds(pl.multiple_of(source * rows, rows), rows)

    def d_arrivals(k, slot, mine):
        turn = 0 if mine else 1
        result = []
        for hop in hops:
            place = w_v.at[k, slot, rows_of(hop), half(k, slot, mine)]
            result.append(
                remote(
                    place, place, ds.at[k, slot - 1, turn, hop - 1], dr.at[k, slot - 1, turn, hop - 1],
                    at_dp(hop),
                )
            )
        return result

    def own_copies(k):
        return [
            remote(wb.at[k], w_v.at[k, 0, my_rows], os_s.at[k, hop - 1], os_r.at[k, hop - 1], at_dp(hop))
            for hop in hops
        ]

    def own_arrivals(k):
        return [
            remote(
                wb.at[k], w_v.at[k, 0, rows_of(hop)], os_s.at[k, hop - 1], os_r.at[k, hop - 1], at_dp(hop)
            )
            for hop in hops
        ]

    def part(ref, index):
        return ref.at[pl.ds(pl.multiple_of(index * quarter, quarter), quarter)]

    def route(src, out, send, receive):
        return remote(src, part(out, mp), send.at[0], receive.at[mp], at_mp(star))

    def pass_on(out, send, receive, index):
        return remote(part(out, index), part(out, index), send.at[1 + index], receive.at[4 + index], mate)

    def main_arrival(out, send, receive, index):
        return remote(part(out, index), part(out, index), send.at[0], receive.at[index], mate)

    def second_arrival(out, send, receive, index):
        return remote(part(out, index), part(out, index), send.at[0], receive.at[4 + index], mate)

    routes = ((tok, t_v, ts, tr), (cot, c_v, cs, cr))

    def keep(which):
        src, out = routes[which][:2]
        return pltpu.make_async_copy(src, part(out, mp), tl.at[which])

    def collect(which):
        out, send, receive = routes[which][1:]

        @pl.when(is_main)
        def _():
            keep(which).wait()
            pass_on(out, send, receive, mp).start()
            for index in (other_mid, 0, 3):
                main_arrival(out, send, receive, index).wait_recv()
                pass_on(out, send, receive, index).start()

        @pl.when(is_second)
        def _():
            for index in range(4):
                second_arrival(out, send, receive, index).wait_recv()

    def meta_copies():
        return [
            remote(mod_in, mod_v, ms.at[0], mr.at[0], mate),
            remote(small_in, small_v, ms.at[1], mr.at[1], mate),
        ]

    def par_load(k):
        layer, at = pieces[k]
        return pltpu.make_async_copy(par.at[layer, :, at : at + PIECE], par_f.at[k % 2], psem.at[k % 2])

    def cast_piece(k):
        if k == 0:
            par_load(0).start()
        if k + 1 < count:
            par_load(k + 1).start()
        par_load(k).wait()
        block = 96 if rows % 96 == 0 else rows
        for at in range(0, rows, block):
            wb[k, at : at + block, :] = par_f[k % 2, at : at + block, :].astype(bf16)

    def keep_own(k):
        block = 96 if rows % 96 == 0 else rows
        for at in range(0, rows, block):
            spot = pl.ds(pl.multiple_of(dp * rows + at, 16), block)
            w_v[k, 0, spot, :] = wb[k, at : at + block, :]

    def w_out(k, slot):
        return pltpu.make_async_copy(w_v.at[k, slot], w_o.at[k, slot], wsem.at[k, slot])

    def x_out(turn):
        return pltpu.make_async_copy(x_v.at[turn % 2], xs_o.at[turn], xsem.at[turn])

    def qo_out(layer, slot):
        return pltpu.make_async_copy(qo_v.at[slot % 2], qo_o.at[layer, slot], qsem.at[slot % 2])

    def ad_out(layer, slot):
        return pltpu.make_async_copy(ad_v.at[slot], ad_o.at[layer, slot], asem.at[slot])

    def serve_z(k, *slots):
        for slot in slots:
            z_copy(k, slot, at_mp(other_mid)).wait_recv()
            g_copy(k, slot).start()
            for copy in d_copies(k, slot, True):
                copy.start()

    def serve_g(k, *slots):
        for slot in slots:
            g_copy(k, slot).wait_recv()
            for copy in d_copies(k, slot, False):
                copy.start()

    def ready(k, slot):
        if slot == 0:
            for copy in own_arrivals(k):
                copy.wait_recv()
        else:
            for mine in (True, False):
                for copy in d_arrivals(k, slot, mine):
                    copy.wait_recv()
        w_out(k, slot).start()

    def lifted(layer, kind, turn):
        for span in chunks():
            normed, _ = moments(x_v[turn % 2, span, :])
            shift = row_mod(hot_o[span, :], tab_o, layer, kind)
            scale = row_mod(hot_o[span, :], tab_o, layer, kind + 1)
            u_s[span, :] = (normed * (1.0 + scale) + shift).astype(bf16)
        acc[...] = jnp.zeros_like(acc)

    def exchange(turn):
        result = []
        for hop in hops:
            target = lax.rem(dp + hop, n_dp)
            result.append(
                remote(
                    out.at[turn % 2, pl.ds(pl.multiple_of(target * rows, rows), rows)],
                    inbox.at[turn % 2, hop - 1],
                    ce_s.at[turn, hop - 1], ce_r.at[turn, hop - 1], at_dp(hop),
                )
            )
        return result

    def to_owner(turn):
        close = jnp.where(mp == 1, 0, 3)
        device = at_mp((other_mid, 3 - close, close)[turn])
        plane = (1, 1, 0)[turn]
        return remote(stage.at[turn], early_o.at[plane], ow_s.at[turn], ow_r.at[plane], device)

    def early_arrival(plane):
        return remote(early_o.at[plane], early_o.at[plane], ow_s.at[0], ow_r.at[plane], mate)

    def finish(turn):
        for copy in exchange(turn):
            copy.wait_recv()
        block = 96 if rows % 96 == 0 else rows
        for at in range(0, rows, block):
            mine = pl.ds(pl.multiple_of(dp * rows + at, 16), block)
            total = out[turn % 2, mine, :].astype(f32)
            for hop in hops:
                total = total + inbox[turn % 2, hop - 1, at : at + block, :].astype(f32)
            stage[turn, at : at + block, :] = total.astype(bf16)
        for copy in exchange(turn):
            copy.wait_send()
        to_owner(turn).start()

    def early_unit(turn):
        out[turn % 2] = mm(d_t[...], ad_v[(2, 3, 1)[turn], 0], 1, 0).astype(bf16)

    def rows_copy():
        return remote(c_v, t_v, pe_s.at[0], pe_r.at[0], mate)

    def rows_out():
        return pltpu.make_async_copy(c_v, rows_o, psend.at[0])

    def branch_rows(layer, kind, turn, span):
        gate = row_mod(hot_o[span, :], tab_o, layer, kind)
        return x_v[1 - turn % 2, span, :] + gate * acc[span, :]

    def add_branch(layer, kind, turn):
        if turn >= 2:
            x_out(turn - 2).wait()
        for span in chunks():
            x_v[turn % 2, span, :] = branch_rows(layer, kind, turn, span)

    def attn_unit(layer, slot):
        k, place = layer * (cols // PIECE), slot % 2
        ready(k, slot)
        if slot >= 2:
            qo_out(layer, slot - 2).wait()
        qo = qo_v.at[place]
        qo[:, : 3 * HW] = mm(u_s[...], w_v[k, slot, :, : 3 * HW], 1, 0).astype(bf16)
        for head in range(HEADS_DEV):
            base = head * HD
            for span, near_by in bands(layer):
                query = qo[span, base : base + HD] * jnp.asarray(0.125, bf16)
                keys = qo[near_by, HW + base : HW + base + HD]
                values = qo[near_by, 2 * HW + base : 2 * HW + base + HD]
                scores = mm(keys, query, 1, 1)
                allowed = idc_o[layer, near_by, :] == idr_o[layer, :, span]
                scores = jnp.where(allowed, scores, neg_fill)
                top = jnp.max(scores, axis=0, keepdims=True)
                raw = jnp.exp(scores - top)
                total = jnp.sum(raw, axis=0, keepdims=True)
                probs = (raw * (1.0 / total)).astype(bf16)
                qo[span, 3 * HW + base : 3 * HW + base + HD] = mm(values, probs, 0, 0).T.astype(bf16)
                lse_o[layer, slot * HEADS_DEV + head, :, span] = top + jnp.log(total)
        acc[...] += mm(qo[:, 3 * HW :], w_v[k, slot, :, 3 * HW :], 1, 1)
        qo_out(layer, slot).start()

    def up_unit(layer, slot):
        k = layer * (cols // PIECE) + 1
        ready(k, slot)
        if layer > 0:
            ad_out(layer - 1, slot).wait()
        for span in chunks():
            hid = mm(u_s[span, :], w_v[k, slot], 1, 0)
            cdf = 0.5 * (1.0 + lax.erf(hid * 0.7071067811865476))
            pdf = jnp.exp(-0.5 * hid * hid) * 0.3989422804014327
            ad_v[slot, 0, span, :] = (hid * cdf).astype(bf16)
            ad_v[slot, 1, span, :] = (cdf + hid * pdf).astype(bf16)
        ad_out(layer, slot).start()

    def down_unit(layer, slot):
        k = layer * (cols // PIECE) + 2
        ready(k, slot)
        acc[...] += mm(ad_v[slot, 0], w_v[k, slot], 1, 1)

    @pl.when(jnp.logical_not(is_main))
    def _():
        route(tok, t_v, ts, tr).start()

    @pl.when(is_main)
    def _():
        keep(0).start()
        keep(1).start()
        for copy in meta_copies():
            copy.start()

    @pl.when(is_outer)
    def _():
        for k in range(count):
            cast_piece(k)
            if k == count - 1:
                route(cot, c_v, cs, cr).start()
            z_copy(k, 1, at_mp(near)).start()
            z_copy(k, 3, at_mp(far)).start()
        for plane in range(2):
            early_arrival(plane).wait_recv()
        for k in range(count):
            z_copy(k, 1, at_mp(near)).wait_send()
            z_copy(k, 3, at_mp(far)).wait_send()
        route(tok, t_v, ts, tr).wait_send()
        route(cot, c_v, cs, cr).wait_send()

    @pl.when(is_mid)
    def _():
        for k in range(count):
            cast_piece(k)
            for copy in own_copies(k):
                copy.start()
            if k == count - 1:
                pl.when(is_second)(lambda: route(cot, c_v, cs, cr).start())
            z_copy(k, 2, at_mp(other_mid)).start()
            keep_own(k)

        @pl.when(is_main)
        def _():
            mod_v[...] = mod_in[...]
            small_v[...] = small_in[...]

        @pl.when(is_second)
        def _():
            for copy in meta_copies():
                copy.wait_recv()

        column = counted((ROWS, 1), 0)
        line = counted((1, ROWS), 1)
        small = small_v[...]
        for layer in range(L):
            pos_c, clip_c, id_c, from_c = slot_meta(small, column, is_main, layer % 2 == 1)
            idc_o[layer] = id_c
            pos_s[layer] = pos_c
            pos_r, _, id_r, from_r = slot_meta(small, line, is_main, layer % 2 == 1)
            idr_o[layer] = id_r
            pos_o[layer] = pos_r
        lane = counted((ROWS, 4 * SLOTS), 1)
        lane_clip = lane - SLOTS * jnp.floor(lane / SLOTS)
        hot_o[...] = jnp.where((lane_clip == clip_c) & (lane < 3 * SLOTS), 1.0, 0.0).astype(bf16)
        for index in range(6 * L):
            tab_o[index] = split_table(mod_v[:, index * D : (index + 1) * D])
        pos_s[2] = from_c
        pos_o[2] = from_r
        collect(0)
        for span in chunks():
            x_v[0, span, :] = mm(one_hot(pos_s[0, span, :], counted((CHUNK, CAP), 1)), t_v[...], 1, 0)
        x_out(0).start()

        lifted(0, 0, 0)
        attn_unit(0, 0)
        serve_z(0, 1, 2, 3)
        serve_g(0, 1, 2)
        attn_unit(0, 1)
        serve_z(1, 1, 2)
        attn_unit(0, 2)
        serve_g(0, 3)
        serve_z(1, 3)
        attn_unit(0, 3)
        serve_g(1, 1, 2)
        add_branch(0, 2, 1)
        x_out(1).start()
        lifted(0, 3, 1)
        up_unit(0, 0)
        serve_z(2, 1, 2)
        up_unit(0, 1)
        up_unit(0, 2)
        serve_g(1, 3)
        serve_z(2, 3)
        up_unit(0, 3)
        down_unit(0, 0)
        serve_g(2, 1, 2)
        down_unit(0, 1)
        down_unit(0, 2)
        serve_z(3, 1, 2)
        serve_g(2, 3)
        down_unit(0, 3)
        serve_z(3, 3)
        x_out(0).wait()

        @pl.when(is_main)
        def _():
            for index in range(4):
                pass_on(t_v, ts, tr, index).wait_send()

        for span in chunks():
            value = branch_rows(0, 5, 2, span)
            high = value.astype(bf16)
            rest = value - high.astype(f32)
            middle = rest.astype(bf16)
            t_v[span, :] = high
            t_v[slice(ROWS + span.start, ROWS + span.stop), :] = middle
            u_s[span, :] = (rest - middle.astype(f32)).astype(bf16)
        for span in chunks():
            move = one_hot(pos_s[2, span, :], counted((CHUNK, ROWS), 1))
            x_v[0, span, :] = (
                mm(move, t_v[:ROWS, :], 1, 0) + mm(move, t_v[ROWS:, :], 1, 0) + mm(move, u_s[...], 1, 0)
            )
        x_out(2).start()
        lifted(1, 0, 2)
        qo_out(0, 2).wait()
        qo_out(0, 3).wait()
        attn_unit(1, 0)
        serve_g(3, 1, 2)
        serve_z(4, 1, 2)
        attn_unit(1, 1)
        serve_g(3, 3)
        attn_unit(1, 2)
        serve_z(4, 3)
        attn_unit(1, 3)
        serve_g(4, 1, 2)
        add_branch(1, 2, 3)
        x_out(3).start()
        lifted(1, 3, 3)
        serve_g(4, 3)
        up_unit(1, 2)
        collect(1)
        for span in chunks():
            grad = mm(one_hot(pos_s[1, span, :], counted((CHUNK, CAP), 1)), c_v[...], 1, 0)
            g_o[span, :] = grad
            d_t[:, span] = (row_mod(hot_o[span, :], tab_o, 1, 5) * grad).T.astype(bf16)
        early_unit(0)
        for copy in exchange(0):
            copy.start()
        serve_z(5, 1, 2)
        up_unit(1, 3)
        finish(0)
        early_unit(1)
        for copy in exchange(1):
            copy.start()
        up_unit(1, 1)
        serve_z(5, 3)
        finish(1)
        early_unit(2)
        for copy in exchange(2):
            copy.start()
        up_unit(1, 0)
        finish(2)
        down_unit(1, 0)
        serve_g(5, 1, 2)
        down_unit(1, 1)
        down_unit(1, 2)
        serve_g(5, 3)
        down_unit(1, 3)
        for span in chunks():
            u_s[span, :] = branch_rows(1, 5, 4, span).astype(bf16)

        @pl.when(is_main)
        def _():
            for index in range(4):
                pass_on(c_v, cs, cr, index).wait_send()

        for at in range(0, CAP, 256):
            place = one_hot(counted((256, ROWS), 0, at), pos_o[1])
            c_v[at : at + 256, :] = mm(place, u_s[...], 1, 0).astype(bf16)

        @pl.when(is_second)
        def _():
            rows_copy().start()

        @pl.when(is_main)
        def _():
            rows_copy().wait_recv()
            for at in range(0, CAP, 256):
                c_v[at : at + 256, :] = c_v[at : at + 256, :] + t_v[at : at + 256, :]
            rows_out().start()

        early_arrival(1).wait_recv()
        for turn in range(3):
            to_owner(turn).wait_send()
        x_out(2).wait()
        x_out(3).wait()
        for slot in (2, 3):
            qo_out(1, slot).wait()
        for slot in range(4):
            ad_out(1, slot).wait()
        for k in range(count):
            for copy in own_copies(k):
                copy.wait_send()
            for slot in range(4):
                w_out(k, slot).wait()
            for slot in (1, 2, 3):
                g_copy(k, slot).wait_send()
                for mine in (True, False):
                    for copy in d_copies(k, slot, mine):
                        copy.wait_send()
        for k in range(count):
            z_copy(k, 2, at_mp(other_mid)).wait_send()

    @pl.when(is_main)
    def _():
        for copy in meta_copies():
            copy.wait_send()
        rows_out().wait()

    @pl.when(is_second)
    def _():
        rows_copy().wait_send()
        route(tok, t_v, ts, tr).wait_send()
        route(cot, c_v, cs, cr).wait_send()


def run_forward(tok, cot, mod, small, par):
    sds = jax.ShapeDtypeStruct
    n_dp = lax.axis_size("dp")
    rows, cols = par.shape[1], par.shape[2]
    count = L * cols // PIECE
    peers = n_dp - 1
    return pl.pallas_call(
        partial(fwd_kernel, n_dp),
        out_shape=(
            sds((count, 4, D, PIECE), bf16), sds((2 * L, ROWS, D), f32), sds((L, 4, ROWS, D), bf16),
            sds((L, 4, 2, ROWS, FF // 4), bf16), sds((2, rows, PIECE), bf16), sds((CAP, D), bf16),
            sds((L, HEADS, 1, ROWS), f32), sds((ROWS, D), f32), sds((ROWS, 4 * SLOTS), bf16), sds((L, ROWS, 1), f32), sds((L, 1, ROWS), f32),
            sds((3, 1, ROWS), f32), sds((6 * L, 4 * SLOTS, D), bf16),
        ),
        in_specs=[any_spec(), any_spec(), vm_spec(), vm_spec(), any_spec()],
        out_specs=(any_spec(),) * 6 + (vm_spec(),) * 7,
        scratch_shapes=[
            VM((count, 4, D, PIECE), bf16), VM((count, rows, PIECE), bf16), VM((2, rows, PIECE), f32),
            VM((CAP, D), bf16), VM((CAP, D), bf16), VM((2, ROWS, D), f32), VM((ROWS, D), bf16),
            VM((ROWS, D), f32), VM((2, ROWS, D), bf16), VM((4, 2, ROWS, FF // 4), bf16), VM((8, 128), f32), VM(mod.shape, f32),
            VM((3, ROWS, 1), f32), VM((D, ROWS), bf16), VM((2, D, PIECE), bf16),
            VM((2, peers, rows, PIECE), bf16), VM((3, rows, PIECE), bf16),
            DMA((count, 3)), DMA((count, 3)), DMA((count, 3)), DMA((count, 3)),
            DMA((count, 3, 2, peers)), DMA((count, 3, 2, peers)), DMA((count, peers)), DMA((count, peers)),
            DMA((5,)), DMA((8,)), DMA((5,)), DMA((8,)), DMA((2,)), DMA((2,)), DMA((2,)),
            DMA((2,)), DMA((count, 4)), DMA((2 * L,)), DMA((2,)), DMA((4,)),
            DMA((3, peers)), DMA((3, peers)), DMA((3,)), DMA((2,)), DMA((1,)), DMA((1,)), DMA((1,)),
        ],
        compiler_params=pltpu.CompilerParams(
            collective_id=1, has_side_effects=True, vmem_limit_bytes=63 * MIB
        ),
    )(tok, cot, mod, small, par)


def share_rows(rows, n_grp):
    part = rows // n_grp
    return part if part * n_grp == rows and part % 16 == 0 else rows


def back_kernel(
    n_dp, n_grp,
    pos_r, g_in, hot, idc, idr, tables, lse, xs, qo, ad, early, rows_in,
    w_hbm, par, mom, var,
    recv, avg, mix_o, gin_o,
    g_s, x_b, w_b, a_b, q_b, u_t, d_s, d_t, dh, dq, do_s, dk_s, acc, out, inbox, stage,
    p_b, p_in, opt, gsum, diff, box, own_avg,
    xsem, wsem, asem, ce_s, ce_r, os_s, os_r, loc, pe_s, pe_r, ro_s, ro_r, rl, osem,
    as_s, as_r, bs_s, bs_r, bl, esem,
):
    grp, dp, mp = lax.axis_index("grp"), lax.axis_index("dp"), lax.axis_index("mp")
    rows, cols = par.shape[1], par.shape[2]
    quarter = mix_o.shape[0]
    share = share_rows(rows, n_grp)
    star = 1 + lax.rem(dp, 2)
    is_mid = jnp.logical_or(mp == 1, mp == 2)
    is_outer = jnp.logical_not(is_mid)
    is_main = mp == star
    is_second = jnp.logical_and(is_mid, mp != star)
    other_mid = 3 - mp
    near_outer = jnp.where(mp == 1, 0, 3)
    far_outer = 3 - near_outer
    heads = HEADS_DEV
    hw = HW
    mate = (grp, flip(dp, 1), mp)

    def at_mp(where):
        return (grp, dp, where)

    def at_grp(step):
        return (lax.rem(grp + step, n_grp), dp, mp)

    def at_dp(step):
        return (grp, lax.rem(dp + step, n_dp), mp)

    peers = [at_grp(step) for step in range(1, n_grp)]

    @pl.when(is_mid)
    def _():
        greet(
            [at_mp(0), at_mp(3), at_mp(other_mid)] + peers + [at_dp(step) for step in range(1, n_dp)]
        )

    @pl.when(is_outer)
    def _():
        greet([at_mp(1), at_mp(2)] + peers)

    def layer_of(sub):
        return 1 - sub // 2

    def slot_of(step):
        return 3 - step % 4

    units = []
    for sub in range(4):
        steps = range(4 * sub, 4 * sub + 4)
        if sub % 2:
            units += [(step, "attn") for step in steps]
        else:
            units += [(step, kind) for step in steps for kind in ("down", "up")]
    units = [unit for unit in units if unit not in ((0, "down"), (1, "down"), (2, "down"))]

    def piece_of(unit):
        step, kind = units[unit]
        return layer_of(step // 4), {"attn": 0, "up": PIECE, "down": 2 * PIECE}[kind]

    def index_of(piece):
        return piece[0] * (cols // PIECE) + piece[1] // PIECE

    def halves(piece):
        return [(0, 512), (512, PIECE)] if piece == (0, 0) else [(0, PIECE)]

    def weight_loads(step):
        sub, slot, place = step // 4, slot_of(step), step % 2
        first = layer_of(sub) * (cols // PIECE) + (1 if sub % 2 == 0 else 0)
        return [
            pltpu.make_async_copy(
                w_hbm.at[first + turn, slot], w_b.at[place, :, turn * D : turn * D + D], wsem.at[place, turn]
            )
            for turn in range(2 if sub % 2 == 0 else 1)
        ]

    def kept_load(step):
        sub, slot, place = step // 4, slot_of(step), step % 2
        layer = layer_of(sub)
        if sub % 2 == 0:
            return pltpu.make_async_copy(ad.at[layer, slot], a_b.at[place], asem.at[place])
        return pltpu.make_async_copy(qo.at[layer, slot], q_b.at[place], asem.at[place])

    def load(step):
        for copy in (kept_load(step), *weight_loads(step)):
            copy.start()

    def x_load(sub):
        source = xs.at[2 * layer_of(sub) + (1 if sub % 2 == 0 else 0)]
        return pltpu.make_async_copy(source, x_b.at[sub % 2], xsem.at[sub % 2])

    def exchange(unit):
        place = unit % 2
        result = []
        for hop in range(1, n_dp):
            target = lax.rem(dp + hop, n_dp)
            result.append(
                remote(
                    out.at[place, pl.ds(pl.multiple_of(target * rows, rows), rows)],
                    inbox.at[place, hop - 1],
                    ce_s.at[unit, hop - 1], ce_r.at[unit, hop - 1], at_dp(hop),
                )
            )
        return result

    def to_owner(unit, turns=(0, 1)):
        piece, slot = piece_of(unit), slot_of(units[unit][0])
        plane, index = (1 if slot >= 2 else 0), index_of(piece)
        result = []
        for turn, (low, high) in enumerate(halves(piece)):
            if turn not in turns:
                continue
            source = stage.at[unit, :, low:high]
            place = recv.at[plane, piece[0], :, piece[1] + low : piece[1] + high]
            if slot == 0:
                result.append(pltpu.make_async_copy(source, place, loc.at[index, turn]))
            else:
                device = at_mp((None, near_outer, other_mid, far_outer)[slot])
                result.append(
                    remote(source, place, os_s.at[unit, turn], os_r.at[index, plane, turn], device)
                )
        return result

    def owner_arrival(piece, plane, turn):
        low, high = halves(piece)[turn]
        place = recv.at[plane, piece[0], :, piece[1] + low : piece[1] + high]
        return remote(place, place, os_s.at[0, 0], os_r.at[index_of(piece), plane, turn], mate)

    early_piece = (L - 1, 2 * PIECE)

    def early_copy(plane):
        place = recv.at[plane, early_piece[0], :, early_piece[1] : early_piece[1] + PIECE]
        return pltpu.make_async_copy(early.at[plane], place, esem.at[plane])

    def finish(unit):
        place = unit % 2
        for copy in exchange(unit):
            copy.wait_recv()
        block = 96 if rows % 96 == 0 else rows
        for at in range(0, rows, block):
            mine = pl.ds(pl.multiple_of(dp * rows + at, 16), block)
            total = out[place, mine, :].astype(f32)
            for hop in range(1, n_dp):
                total = total + inbox[place, hop - 1, at : at + block, :].astype(f32)
            stage[unit, at : at + block, :] = total.astype(bf16)
        for copy in exchange(unit):
            copy.wait_send()
        for copy in to_owner(unit):
            copy.start()

    def put_rows(values):
        for at in range(0, CAP, 256):
            place = one_hot(counted((256, ROWS), 0, at), pos_r[0])
            p_b[at : at + 256, :] = mm(place, values, 1, 0).astype(bf16)

        @pl.when(is_second)
        def _():
            remote(p_b, p_in, pe_s.at[0], pe_r.at[0], mate).start()

    def quarter_of(index):
        return pl.ds(pl.multiple_of(index * quarter, quarter), quarter)

    def row_copies(which):
        source, dest = ((rows_in, mix_o), (p_b, gin_o))[which]
        return [
            remote(
                source.at[quarter_of(index)], dest, ro_s.at[which, turn], ro_r.at[which], at_mp(index)
            )
            for turn, index in enumerate((other_mid, 0, 3))
        ]

    def row_keep(which):
        source, dest = ((rows_in, mix_o), (p_b, gin_o))[which]
        return pltpu.make_async_copy(source.at[quarter_of(mp)], dest, rl.at[which])

    def send_rows(which):
        @pl.when(is_main)
        def _():
            if which == 1:
                remote(p_b, p_in, pe_s.at[0], pe_r.at[0], mate).wait_recv()
                for at in range(0, CAP, 256):
                    span = slice(at, at + 256)
                    p_b[span, :] = p_b[span, :] + p_in[span, :]
            for copy in row_copies(which):
                copy.start()
            row_keep(which).start()

    def end_rows():
        @pl.when(is_main)
        def _():
            for which in range(2):
                for copy in row_copies(which):
                    copy.wait_send()
                row_keep(which).wait()

        @pl.when(is_second)
        def _():
            remote(p_b, p_in, pe_s.at[0], pe_r.at[0], mate).wait_send()

    def rows_arrived(which, dest):
        @pl.when(jnp.logical_not(is_main))
        def _():
            remote(
                dest, dest, ro_s.at[which, 0], ro_r.at[which], at_mp(0)
            ).wait_recv()

    def diff_piece(piece, turn):
        layer, index = piece[0], index_of(piece)
        low, high = halves(piece)[turn]
        width = high - low
        span = slice(piece[1] + low, piece[1] + high)
        block = opt.shape[2]

        def opt_loads(lap):
            part, place = slice(lap * block, (lap + 1) * block), lap % 2
            return [
                pltpu.make_async_copy(
                    source.at[layer, part, span], opt.at[place, i, :, :width], osem.at[place, i]
                )
                for i, source in enumerate((par, mom, var))
            ] + [
                pltpu.make_async_copy(
                    recv.at[plane, layer, part, span], gsum.at[place, plane, :, :width],
                    osem.at[place, 3 + plane],
                )
                for plane in range(2)
            ]

        @pl.when(is_outer)
        def _():
            if piece == early_piece:
                early_copy(0).wait()
            else:
                owner_arrival(piece, 0, turn).wait_recv()

        @pl.when(is_mid)
        def _():
            own = [u for u in range(len(units)) if piece_of(u) == piece and slot_of(units[u][0]) == 0][0]
            to_owner(own, (turn,))[0].wait()

        if piece == early_piece:
            early_copy(1).wait()
        else:
            owner_arrival(piece, 1, turn).wait_recv()
        for copy in opt_loads(0):
            copy.start()
        for lap in range(rows // block):
            part, place = slice(lap * block, (lap + 1) * block), lap % 2
            if (lap + 1) * block < rows:
                for copy in opt_loads(lap + 1):
                    copy.start()
            for copy in opt_loads(lap):
                copy.wait()
            grad = gsum[place, 0, :, :width].astype(f32) + gsum[place, 1, :, :width].astype(f32)
            one = beta_one * opt[place, 1, :, :width] + (1 - beta_one) * grad
            two = beta_two * opt[place, 2, :, :width] + (1 - beta_two) * grad * grad
            step = one / (1 - beta_one**STEP) / (jnp.sqrt(two / (1 - beta_two**STEP)) + adam_eps)
            diff[index, part, low:high] = (
                inner_rate * (step + decay_rate * opt[place, 0, :, :width])
            ).astype(bf16)
        for copy in first_copies(piece, turn):
            copy.start()

    def rows_for(where):
        if share == rows:
            return slice(0, rows)
        return pl.ds(pl.multiple_of(where * share, share), share)

    def first_copies(piece, turn):
        index = index_of(piece)
        low, high = halves(piece)[turn]
        return [
            remote(
                diff.at[index, rows_for(lax.rem(grp + hop, n_grp)), low:high],
                box.at[index, hop - 1, :, low:high],
                as_s.at[index, turn, hop - 1], as_r.at[index, turn, hop - 1], at_grp(hop),
            )
            for hop in range(1, n_grp)
        ]

    def second_copies(piece, turn):
        index = index_of(piece)
        low, high = halves(piece)[turn]
        place = avg.at[piece[0], rows_for(grp), piece[1] + low : piece[1] + high]
        return [
            remote(
                own_avg.at[index, :, low:high], place,
                bs_s.at[index, turn, hop - 1], bs_r.at[index, turn, hop - 1], at_grp(hop),
            )
            for hop in range(1, n_grp)
        ]

    def second_arrivals(piece, turn):
        index = index_of(piece)
        low, high = halves(piece)[turn]
        result = []
        for hop in range(1, n_grp):
            source = lax.rem(grp + n_grp - hop, n_grp)
            place = avg.at[piece[0], rows_for(source), piece[1] + low : piece[1] + high]
            result.append(
                remote(
                    place, place, bs_s.at[index, turn, hop - 1], bs_r.at[index, turn, hop - 1], at_grp(hop)
                )
            )
        return result

    def own_copy(piece, turn):
        index = index_of(piece)
        low, high = halves(piece)[turn]
        place = avg.at[piece[0], rows_for(grp), piece[1] + low : piece[1] + high]
        return pltpu.make_async_copy(own_avg.at[index, :, low:high], place, bl.at[index, turn])

    def mean_piece(piece, turn):
        index = index_of(piece)
        low, high = halves(piece)[turn]
        for copy in first_copies(piece, turn):
            copy.wait_recv()
        total = diff[index, rows_for(grp), low:high].astype(f32)
        for hop in range(1, n_grp):
            total = total + box[index, hop - 1, :, low:high].astype(f32)
        own_avg[index, :, low:high] = (total / n_grp).astype(bf16)
        own_copy(piece, turn).start()
        if share != rows:
            for copy in second_copies(piece, turn):
                copy.start()

    def end_piece(piece, turn):
        for copy in first_copies(piece, turn):
            copy.wait_send()
        own_copy(piece, turn).wait()
        if share != rows:
            for copy in second_copies(piece, turn):
                copy.wait_send()
            for copy in second_arrivals(piece, turn):
                copy.wait_recv()

    def down_start(sub):
        layer = layer_of(sub)
        for part in chunks():
            down = row_mod(hot[part, :], tables, layer, 5) * g_s[part, :]
            d_s[part, :] = down.astype(bf16)
            d_t[:, part] = down.T.astype(bf16)

    def up_start(sub):
        layer, place = layer_of(sub), sub % 2
        x_load(sub).wait()
        for part in chunks():
            normed, _ = moments(x_b[place, part, :])
            shift = row_mod(hot[part, :], tables, layer, 3)
            scale = row_mod(hot[part, :], tables, layer, 4)
            u_t[:, part] = (normed * (1.0 + scale) + shift).T.astype(bf16)
        acc[...] = jnp.zeros_like(acc)

    def down_unit(step, turn):
        out[turn] = mm(d_t[...], a_b[step % 2, 0], 1, 0).astype(bf16)

    def up_unit(step, turn):
        place = step % 2
        for part in chunks():
            dact = mm(d_s[part, :], w_b[place, :, D:], 1, 0)
            dh[part, :] = (dact * a_b[place, 1, part, :].astype(f32)).astype(bf16)
        out[turn] = mm(u_t[...], dh[...], 1, 0).astype(bf16)
        acc[...] += mm(dh[...], w_b[place, :, :D], 1, 1)

    def attn_start(sub):
        layer, place = layer_of(sub), sub % 2
        x_load(sub).wait()
        for part in chunks():
            normed, _ = moments(x_b[place, part, :])
            shift = row_mod(hot[part, :], tables, layer, 0)
            scale = row_mod(hot[part, :], tables, layer, 1)
            u_t[:, part] = (normed * (1.0 + scale) + shift).T.astype(bf16)
            branch = row_mod(hot[part, :], tables, layer, 2) * g_s[part, :]
            d_s[part, :] = branch.astype(bf16)
            d_t[:, part] = branch.T.astype(bf16)
        acc[...] = jnp.zeros_like(acc)

    def attn_unit(step, turn):
        layer, place, slot = layer_of(step // 4), step % 2, slot_of(step)
        out[turn, :, 3 * hw : D] = mm(d_t[...], q_b[place, :, 3 * hw :], 1, 0).astype(bf16)
        do_s[...] = mm(d_s[...], w_b[place, :, 3 * hw : D], 1, 0).astype(bf16)
        for head in range(heads):
            base = head * HD
            dk_s[...] = jnp.zeros_like(dk_s)
            for span, near_by in bands(layer):
                query = q_b[place, span, base : base + HD]
                keys = q_b[place, near_by, hw + base : hw + base + HD]
                values = q_b[place, near_by, 2 * hw + base : 2 * hw + base + HD]
                grad = do_s[span, base : base + HD]
                scores = mm(keys, query * jnp.asarray(0.125, bf16), 1, 1)
                allowed = idc[layer, near_by, :] == idr[layer, :, span]
                probs = jnp.where(
                    allowed, jnp.exp(scores - lse[layer, slot * heads + head, :, span]), 0.0
                )
                dk_s[1, near_by, :] += mm(probs.astype(bf16), grad, 1, 0)
                weighted = probs * mm(values, grad, 1, 1)
                delta = jnp.sum(weighted, axis=0, keepdims=True)
                ds = (weighted - probs * delta).astype(bf16)
                dq[span, base : base + HD] = (mm(keys, ds, 0, 0).T * 0.125).astype(bf16)
                dk_s[0, near_by, :] += mm(ds, query, 1, 0)
            dq[:, hw + base : hw + base + HD] = (dk_s[0] * 0.125).astype(bf16)
            dq[:, 2 * hw + base : 2 * hw + base + HD] = dk_s[1].astype(bf16)
        out[turn, :, : 3 * hw] = mm(u_t[...], dq[...], 1, 0).astype(bf16)
        acc[...] += mm(dq[...], w_b[place, :, : 3 * hw], 1, 1)

    def sub_end(sub):
        layer, place = layer_of(sub), sub % 2
        row = 4 if sub % 2 == 0 else 1
        for part in chunks():
            normed, inv_std = moments(x_b[place, part, :])
            scale = row_mod(hot[part, :], tables, layer, row)
            g_s[part, :] = g_s[part, :] + norm_back(acc[part, :] * (1.0 + scale), normed, inv_std)

    def to_frame_order():
        for part in chunks():
            high = g_s[part, :].astype(bf16)
            dh[part, :] = high
            d_s[part, :] = (g_s[part, :] - high.astype(f32)).astype(bf16)
        for part in chunks():
            move = one_hot(counted((CHUNK, ROWS), 0, part.start), pos_r[2])
            g_s[part, :] = mm(move, dh[...], 1, 0) + mm(move, d_s[...], 1, 0)

    def chunk(sub, kind):
        return layer_of(sub), {"attn": 0, "up": PIECE, "down": 2 * PIECE}[kind]

    order = [chunk(0, "down"), chunk(0, "up"), chunk(1, "attn"), chunk(2, "down"), chunk(2, "up"), chunk(3, "attn")]
    served = {7: (diff_piece, 0), 9: (mean_piece, 0), 14: (diff_piece, 1), 17: (mean_piece, 1)}

    early_copy(1).start()
    pl.when(is_outer)(lambda: early_copy(0).start())

    @pl.when(is_mid)
    def _():
        x_load(0).start()
        send_rows(0)
        load(0)
        load(1)
        g_s[...] = g_in[...]
        for unit, (step, kind) in enumerate(units):
            sub = step // 4
            first_of_sub = unit == 0 or units[unit - 1][0] // 4 != sub
            last_of_step = unit + 1 == len(units) or step not in [s for s, _ in units[unit + 1 :]]
            last_of_sub = unit + 1 == len(units) or units[unit + 1][0] // 4 != sub
            if first_of_sub:
                if sub < 3:
                    x_load(sub + 1).start()
                (attn_start if kind == "attn" else down_start)(sub)
            if unit == 0 or units[unit - 1][0] != step:
                kept_load(step).wait()
            if kind != "down":
                if kind == "up" and step % 4 == 0:
                    up_start(sub)
                for copy in weight_loads(step):
                    copy.wait()
            {"attn": attn_unit, "up": up_unit, "down": down_unit}[kind](step, unit % 2)
            if unit > 0:
                finish(unit - 1)
            for copy in exchange(unit):
                copy.start()
            if last_of_step and step + 2 < 16:
                load(step + 2)
            if last_of_sub:
                sub_end(sub)
                if sub == 1:
                    to_frame_order()
            if unit in served:
                action, which = served[unit]
                action(order[which], 0)
        put_rows(g_s[...].astype(bf16))
        finish(len(units) - 1)
        send_rows(1)
        for piece in order[2:5]:
            diff_piece(piece, 0)
            mean_piece(piece, 0)
        for turn in range(2):
            diff_piece(order[5], turn)
        for turn in range(2):
            mean_piece(order[5], turn)
        for unit, (step, _) in enumerate(units):
            if slot_of(step) != 0:
                for copy in to_owner(unit):
                    copy.wait_send()
        end_rows()

    @pl.when(is_outer)
    def _():
        for piece in order[:5]:
            diff_piece(piece, 0)
            mean_piece(piece, 0)
        for turn in range(2):
            diff_piece(order[5], turn)
        for turn in range(2):
            mean_piece(order[5], turn)

    for which, dest in ((0, mix_o), (1, gin_o)):
        rows_arrived(which, dest)
    for piece in order:
        for turn in range(len(halves(piece))):
            end_piece(piece, turn)


def run_back(pos, g, hot, idc, idr, tables, lse, xs, qo, ad, early, rows_in, w, par, mom, var, quarter):
    sds = jax.ShapeDtypeStruct
    n_dp, n_grp = lax.axis_size("dp"), lax.axis_size("grp")
    rows, cols = par.shape[1], par.shape[2]
    share = share_rows(rows, n_grp)
    count = L * cols // PIECE
    far, peers = n_dp - 1, n_grp - 1
    block = 96 if rows % 96 == 0 else rows
    return pl.pallas_call(
        partial(back_kernel, n_dp, n_grp),
        out_shape=(
            sds((2, L, rows, cols), bf16), sds((L, rows, cols), bf16),
            sds((quarter, D), bf16), sds((quarter, D), bf16),
        ),
        in_specs=[vm_spec()] * 7 + [any_spec()] * 9,
        out_specs=(any_spec(),) * 4,
        scratch_shapes=[
            VM((ROWS, D), f32), VM((2, ROWS, D), f32), VM((2, D, 2 * D), bf16),
            VM((2, 2, ROWS, D), bf16), VM((2, ROWS, D), bf16),
            VM((D, ROWS), bf16), VM((ROWS, D), bf16), VM((D, ROWS), bf16), VM((ROWS, D), bf16),
            VM((ROWS, 9 * HD), bf16), VM((ROWS, 3 * HD), bf16), VM((2, ROWS, HD), f32), VM((ROWS, D), f32),
            VM((2, D, PIECE), bf16), VM((2, far, rows, PIECE), bf16), VM((4 * count, rows, PIECE), bf16),
            VM((CAP, D), bf16), VM((CAP, D), bf16),
            VM((2, 3, block, PIECE), f32), VM((2, 2, block, PIECE), bf16),
            VM((count, rows, PIECE), bf16), VM((count, peers, share, PIECE), bf16),
            VM((count, share, PIECE), bf16),
            DMA((2,)), DMA((2, 2)), DMA((2,)), DMA((4 * count, far)), DMA((4 * count, far)),
            DMA((4 * count, 2)), DMA((count, 2, 2)), DMA((count, 2)),
            DMA((2,)), DMA((2,)), DMA((2, 3)), DMA((2,)), DMA((2,)), DMA((2, 5)),
            DMA((count, 2, peers)), DMA((count, 2, peers)), DMA((count, 2, peers)), DMA((count, 2, peers)),
            DMA((count, 2)), DMA((2,)),
        ],
        compiler_params=pltpu.CompilerParams(
            collective_id=2, has_side_effects=True, vmem_limit_bytes=63 * MIB
        ),
    )(pos, g, hot, idc, idr, tables, lse, xs, qo, ad, early, rows_in, w, par, mom, var)


def last_kernel(
    par, mom, var, out_mom, ga, gb, avg, rows_m, rows_g, tok, frames, patches,
    new_m, new_v, out_a, out_m, out_w, out_l, mixed, grad_in,
):
    @pl.when(jnp.logical_and(pl.program_id(0) == 0, pl.program_id(1) == 0))
    def _():
        total = frames[:, 0:1] * patches[:, 0:1]
        for clip in range(1, SLOTS):
            total = total + frames[:, clip : clip + 1] * patches[:, clip : clip + 1]
        first = lax.axis_index("mp") * tok.shape[0]
        live = first + lax.broadcasted_iota(jnp.int32, (tok.shape[0], 1), 0) < total
        mixed[...] = jnp.where(live, rows_m[...].astype(f32), tok[...].astype(f32)).astype(bf16)
        grad_in[...] = jnp.where(live, rows_g[...].astype(f32), 0.0)

    grad = ga[...].astype(f32) + gb[...].astype(f32)
    new_m[...] = beta_one * mom[...] + (1 - beta_one) * grad
    new_v[...] = beta_two * var[...] + (1 - beta_two) * grad * grad
    average = avg[...].astype(f32)
    momentum = outer_mu * out_mom[...] + average
    updated = par[...] - outer_rate * (average + outer_mu * momentum)
    out_a[...] = average
    out_m[...] = momentum
    out_w[...] = updated
    out_l[...] = updated.astype(bf16)


def run_last(par, mom, var, out_mom, recv, avg, rows_m, rows_g, tok, frames, patches):
    rows, cols = par.shape[1], par.shape[2]
    block = 96 if rows % 96 == 0 else rows
    sds = jax.ShapeDtypeStruct
    full = pl.BlockSpec((None, block, cols), lambda i, j: (i, j, 0))

    def plane(which):
        return pl.BlockSpec((None, None, block, cols), lambda i, j: (which, i, j, 0))

    return pl.pallas_call(
        last_kernel,
        grid=(L, rows // block),
        out_shape=(sds(par.shape, f32),) * 5 + (sds(par.shape, bf16), sds(tok.shape, bf16), sds(tok.shape, f32)),
        in_specs=[full] * 4 + [plane(0), plane(1), full] + [vm_spec()] * 5,
        out_specs=(full,) * 6 + (vm_spec(),) * 2,
        compiler_params=pltpu.CompilerParams(vmem_limit_bytes=62 * MIB),
    )(par, mom, var, out_mom, recv, recv, avg, rows_m, rows_g, tok, frames, patches)


def body(
    tokens, cotangent, modulation, clip_frames, clip_patches, params, first_moment, second_moment,
    outer_momentum,
):
    quarter = tokens.shape[1]
    small = jnp.concatenate([clip_frames, clip_patches], axis=0).astype(f32)
    small = jnp.pad(small, ((0, 6), (0, 128 - SLOTS)))
    w, xs, qo, ad, early, rows_in, lse, gradient, hot, idc, idr, pos, tables = run_forward(
        tokens[0], cotangent[0], modulation[0], small, params
    )
    recv, avg, mixed_rows, grad_rows = run_back(
        pos, gradient, hot, idc, idr, tables, lse, xs, qo, ad, early, rows_in, w,
        params, first_moment[0], second_moment[0], quarter,
    )
    new_m, new_v, average, momentum, updated, low, mixed, input_grad = run_last(
        params, first_moment[0], second_moment[0], outer_momentum, recv, avg,
        mixed_rows, grad_rows, tokens[0], clip_frames, clip_patches,
    )
    return (
        mixed[None], input_grad[None], new_m[None], new_v[None], average, momentum, updated, low,
    )


def solution(mesh):
    in_specs = (
        P("grp", ("dp", "mp"), None),
        P("grp", ("dp", "mp"), None),
        P("grp", "dp", None),
        P("grp", "dp"),
        P("grp", "dp"),
        P(None, "dp", "mp"),
        P("grp", None, "dp", "mp"),
        P("grp", None, "dp", "mp"),
        P(None, "dp", "mp"),
    )
    out_specs = (
        P("grp", ("dp", "mp"), None),
        P("grp", ("dp", "mp"), None),
        P("grp", None, "dp", "mp"),
        P("grp", None, "dp", "mp"),
        P(None, "dp", "mp"),
        P(None, "dp", "mp"),
        P(None, "dp", "mp"),
        P(None, "dp", "mp"),
    )
    return jax.shard_map(body, mesh=mesh, in_specs=in_specs, out_specs=out_specs, check_vma=False)
```

```python
from functools import partial

import jax
import jax.numpy as jnp
from jax import lax
from jax.experimental import pallas as pl
from jax.experimental.pallas import tpu as pltpu
from jax.sharding import PartitionSpec as P

D = 768
HEADS = 12
HD = 64
FF = 3072
L = 2
STEP = 5
CAP = 1024
SLOTS = 4
LONGF = 64
ROWS = CAP // 2
CHUNK = 128
PIECE = 768
SIDE = PIECE // 2

ln_eps = 1e-06
neg_fill = -1e30
beta_one = 0.9
beta_two = 0.999
adam_eps = 1e-08
inner_rate = 0.04
decay_rate = 0.1
outer_rate = 0.7
outer_mu = 0.5

f32 = jnp.float32
bf16 = jnp.bfloat16
VM = pltpu.VMEM
DMA = pltpu.SemaphoreType.DMA
MESH_ID = pl.DeviceIdType.MESH
MIB = 2**20
HEADS_DEV = 3
HW = HEADS_DEV * HD


def mm(left, right, lc, rc):
    return lax.dot_general(left, right, (((lc,), (rc,)), ((), ())), preferred_element_type=f32)


def moments(values):
    centered = values - jnp.mean(values, axis=-1, keepdims=True)
    inv_std = lax.rsqrt(jnp.mean(centered * centered, axis=-1, keepdims=True) + ln_eps)
    return centered * inv_std, inv_std


def norm_back(grad_normed, normed, inv_std):
    inner = grad_normed - jnp.mean(grad_normed, axis=-1, keepdims=True)
    inner = inner - normed * jnp.mean(grad_normed * normed, axis=-1, keepdims=True)
    return inv_std * inner


def split_table(table):
    high = table.astype(bf16).astype(f32)
    rest = table - high
    middle = rest.astype(bf16).astype(f32)
    return jnp.concatenate([high, middle, rest - middle, jnp.zeros_like(table)], axis=0).astype(bf16)


def row_mod(hot, tables, layer, kind):
    return mm(hot, tables[layer * 6 + kind], 1, 0)


def chunks():
    return [slice(at, at + CHUNK) for at in range(0, ROWS, CHUNK)]


def any_spec():
    return pl.BlockSpec(memory_space=pl.ANY)


def vm_spec():
    return pl.BlockSpec(memory_space=VM)


def flip(index, bit):
    return index + bit - 2 * bit * lax.rem(index // bit, 2)


def slot_meta(small, index, long_core, by_patch):
    frames = [small[0:1, clip : clip + 1] for clip in range(SLOTS)]
    patches = [small[1:2, clip : clip + 1] for clip in range(SLOTS)]
    zero = jnp.zeros_like(frames[0])
    start, long_start, long_size = zero, zero, zero
    starts, ends = [], []
    for clip in range(SLOTS):
        size = frames[clip] * patches[clip]
        is_long = frames[clip] == float(LONGF)
        long_start = long_start + jnp.where(is_long, start, 0.0)
        long_size = long_size + jnp.where(is_long, size, 0.0)
        starts.append(start)
        start = start + size
        ends.append(start)
    pos_long = index + long_start
    pos_short = jnp.where(index < long_start, index, index + long_size)
    pos = jnp.where(long_core, pos_long, pos_short)
    clip_of = jnp.zeros_like(index)
    for clip in range(SLOTS):
        clip_of = clip_of + jnp.where(pos >= ends[clip], 1.0, 0.0)
    limit = jnp.where(long_core, long_start + long_size, start)
    live = pos < limit
    clip_of = jnp.where(live, clip_of, float(SLOTS))
    begin, many, wide = jnp.zeros_like(index), jnp.ones_like(index), jnp.ones_like(index)
    for clip in range(SLOTS):
        hit = clip_of == float(clip)
        begin = jnp.where(hit, starts[clip], begin)
        many = jnp.where(hit, frames[clip], many)
        wide = jnp.where(hit, patches[clip], wide)
    offset = pos - begin
    inner = many if by_patch else wide
    group = jnp.floor((offset + 0.5) / inner)
    within = offset - group * inner
    source = within * wide + group if by_patch else offset
    ident = jnp.where(live, clip_of * CAP + group, -1.0 - index)
    origin = jnp.where(live, index - offset + source, index)
    return jnp.where(live, begin + source, -1.0), clip_of, ident, origin


def one_hot(left, right):
    return jnp.where(left == right, 1.0, 0.0).astype(bf16)


def counted(shape, dim, first=0):
    return lax.broadcasted_iota(jnp.int32, shape, dim).astype(f32) + float(first)


def bands(layer):
    halo = 32 if layer % 2 == 0 else 64
    return [
        (slice(at, at + CHUNK), slice(max(at - halo, 0), min(at + CHUNK + halo, ROWS)))
        for at in range(0, ROWS, CHUNK)
    ]


def remote(src, dst, send, receive, device):
    return pltpu.make_async_remote_copy(
        src_ref=src, dst_ref=dst, send_sem=send, recv_sem=receive,
        device_id=device, device_id_type=MESH_ID,
    )


def greet(devices):
    barrier = pltpu.get_barrier_semaphore()
    for device in devices:
        pl.semaphore_signal(barrier, inc=1, device_id=device, device_id_type=MESH_ID)
    pl.semaphore_wait(barrier, len(devices))


def fwd_kernel(
    n_dp, tok, cot, mod_in, small_in, par,
    w_o, xs_o, qo_o, ad_o, early_o, rows_o, lse_o, g_o, hot_o, idc_o, idr_o, pos_o, tab_o,
    w_v, wb, par_f, t_v, c_v, x_v, u_s, acc, qo_v, ad_v, small_v, mod_v, pos_s, d_t, out, inbox, stage,
    zs, zr, gs, gr, ds, dr, os_s, os_r, ts, tr, cs, cr, tl, ms, mr, psem, wsem, xsem, qsem, asem, ce_s, ce_r, ow_s, ow_r, pe_s, pe_r, psend,
):
    grp, dp, mp = lax.axis_index("grp"), lax.axis_index("dp"), lax.axis_index("mp")
    rows, cols = par.shape[1], par.shape[2]
    quarter = tok.shape[0]
    pieces = [(layer, at) for layer in range(L) for at in range(0, cols, PIECE)]
    count = len(pieces)
    star = 1 + lax.rem(dp, 2)
    is_mid = jnp.logical_or(mp == 1, mp == 2)
    is_outer = jnp.logical_not(is_mid)
    is_main = mp == star
    is_second = jnp.logical_and(is_mid, mp != star)
    other_mid = 3 - mp
    near = jnp.where(mp == 0, 1, 2)
    far = 3 - near
    my_rows = pl.ds(pl.multiple_of(dp * rows, rows), rows)
    mate = (grp, flip(dp, 1), mp)
    hops = range(1, n_dp)

    def at_mp(where):
        return (grp, dp, where)

    def at_grp(bit):
        return (flip(grp, bit), dp, mp)

    def at_dp(step):
        return (grp, lax.rem(dp + step, n_dp), mp)

    @pl.when(is_mid)
    def _():
        greet(
            [at_mp(0), at_mp(3), at_mp(other_mid), at_grp(1), at_grp(2)] + [at_dp(hop) for hop in hops]
        )

    @pl.when(is_outer)
    def _():
        greet([at_mp(1), at_mp(2)])

    def bit_of(k, slot):
        return 1 + (k + slot) % 2

    def half(k, slot, mine):
        index = lax.rem(grp // bit_of(k, slot), 2)
        if not mine:
            index = 1 - index
        return pl.ds(pl.multiple_of(index * SIDE, 128), SIDE)

    def z_copy(k, slot, device):
        span = half(k, slot, True)
        return remote(
            wb.at[k, :, span], w_v.at[k, slot, my_rows, span], zs.at[k, slot - 1], zr.at[k, slot - 1], device
        )

    def g_copy(k, slot):
        place = w_v.at[k, slot, my_rows, half(k, slot, True)]
        return remote(place, place, gs.at[k, slot - 1], gr.at[k, slot - 1], at_grp(bit_of(k, slot)))

    def d_copies(k, slot, mine):
        place, turn = w_v.at[k, slot, my_rows, half(k, slot, mine)], 0 if mine else 1
        return [
            remote(
                place, place, ds.at[k, slot - 1, turn, hop - 1], dr.at[k, slot - 1, turn, hop - 1], at_dp(hop)
            )
            for hop in hops
        ]

    def rows_of(hop):
        source = lax.rem(dp + n_dp - hop, n_dp)
        return pl.ds(pl.multiple_of(source * rows, rows), rows)

    def d_arrivals(k, slot, mine):
        turn = 0 if mine else 1
        result = []
        for hop in hops:
            place = w_v.at[k, slot, rows_of(hop), half(k, slot, mine)]
            result.append(
                remote(
                    place, place, ds.at[k, slot - 1, turn, hop - 1], dr.at[k, slot - 1, turn, hop - 1],
                    at_dp(hop),
                )
            )
        return result

    def own_copies(k):
        return [
            remote(wb.at[k], w_v.at[k, 0, my_rows], os_s.at[k, hop - 1], os_r.at[k, hop - 1], at_dp(hop))
            for hop in hops
        ]

    def own_arrivals(k):
        return [
            remote(
                wb.at[k], w_v.at[k, 0, rows_of(hop)], os_s.at[k, hop - 1], os_r.at[k, hop - 1], at_dp(hop)
            )
            for hop in hops
        ]

    def part(ref, index):
        return ref.at[pl.ds(pl.multiple_of(index * quarter, quarter), quarter)]

    def route(src, out, send, receive):
        return remote(src, part(out, mp), send.at[0], receive.at[mp], at_mp(star))

    def pass_on(out, send, receive, index):
        return remote(part(out, index), part(out, index), send.at[1 + index], receive.at[4 + index], mate)

    def main_arrival(out, send, receive, index):
        return remote(part(out, index), part(out, index), send.at[0], receive.at[index], mate)

    def second_arrival(out, send, receive, index):
        return remote(part(out, index), part(out, index), send.at[0], receive.at[4 + index], mate)

    routes = ((tok, t_v, ts, tr), (cot, c_v, cs, cr))

    def keep(which):
        src, out = routes[which][:2]
        return pltpu.make_async_copy(src, part(out, mp), tl.at[which])

    def collect(which):
        out, send, receive = routes[which][1:]

        @pl.when(is_main)
        def _():
            keep(which).wait()
            pass_on(out, send, receive, mp).start()
            for index in (other_mid, 0, 3):
                main_arrival(out, send, receive, index).wait_recv()
                pass_on(out, send, receive, index).start()

        @pl.when(is_second)
        def _():
            for index in range(4):
                second_arrival(out, send, receive, index).wait_recv()

    def meta_copies():
        return [
            remote(mod_in, mod_v, ms.at[0], mr.at[0], mate),
            remote(small_in, small_v, ms.at[1], mr.at[1], mate),
        ]

    def par_load(k):
        layer, at = pieces[k]
        return pltpu.make_async_copy(par.at[layer, :, at : at + PIECE], par_f.at[k % 2], psem.at[k % 2])

    def cast_piece(k):
        if k == 0:
            par_load(0).start()
        if k + 1 < count:
            par_load(k + 1).start()
        par_load(k).wait()
        block = 96 if rows % 96 == 0 else rows
        for at in range(0, rows, block):
            wb[k, at : at + block, :] = par_f[k % 2, at : at + block, :].astype(bf16)

    def keep_own(k):
        block = 96 if rows % 96 == 0 else rows
        for at in range(0, rows, block):
            spot = pl.ds(pl.multiple_of(dp * rows + at, 16), block)
            w_v[k, 0, spot, :] = wb[k, at : at + block, :]

    def w_out(k, slot):
        return pltpu.make_async_copy(w_v.at[k, slot], w_o.at[k, slot], wsem.at[k, slot])

    def x_out(turn):
        return pltpu.make_async_copy(x_v.at[turn % 2], xs_o.at[turn], xsem.at[turn])

    def qo_out(layer, slot):
        return pltpu.make_async_copy(qo_v.at[slot % 2], qo_o.at[layer, slot], qsem.at[slot % 2])

    def ad_out(layer, slot):
        return pltpu.make_async_copy(ad_v.at[slot], ad_o.at[layer, slot], asem.at[slot])

    def serve_z(k, *slots):
        for slot in slots:
            z_copy(k, slot, at_mp(other_mid)).wait_recv()
            g_copy(k, slot).start()
            for copy in d_copies(k, slot, True):
                copy.start()

    def serve_g(k, *slots):
        for slot in slots:
            g_copy(k, slot).wait_recv()
            for copy in d_copies(k, slot, False):
                copy.start()

    def ready(k, slot):
        if slot == 0:
            for copy in own_arrivals(k):
                copy.wait_recv()
        else:
            for mine in (True, False):
                for copy in d_arrivals(k, slot, mine):
                    copy.wait_recv()
        w_out(k, slot).start()

    def lifted(layer, kind, turn):
        for span in chunks():
            normed, _ = moments(x_v[turn % 2, span, :])
            shift = row_mod(hot_o[span, :], tab_o, layer, kind)
            scale = row_mod(hot_o[span, :], tab_o, layer, kind + 1)
            u_s[span, :] = (normed * (1.0 + scale) + shift).astype(bf16)
        acc[...] = jnp.zeros_like(acc)

    def exchange(turn):
        result = []
        for hop in hops:
            target = lax.rem(dp + hop, n_dp)
            result.append(
                remote(
                    out.at[turn % 2, pl.ds(pl.multiple_of(target * rows, rows), rows)],
                    inbox.at[turn % 2, hop - 1],
                    ce_s.at[turn, hop - 1], ce_r.at[turn, hop - 1], at_dp(hop),
                )
            )
        return result

    def to_owner(turn):
        close = jnp.where(mp == 1, 0, 3)
        device = at_mp((3 - close, other_mid, close)[turn])
        plane = (1, 1, 0)[turn]
        return remote(stage.at[turn], early_o.at[plane], ow_s.at[turn], ow_r.at[plane], device)

    def early_arrival(plane):
        return remote(early_o.at[plane], early_o.at[plane], ow_s.at[0], ow_r.at[plane], mate)

    def finish(turn):
        for copy in exchange(turn):
            copy.wait_recv()
        block = 96 if rows % 96 == 0 else rows
        for at in range(0, rows, block):
            mine = pl.ds(pl.multiple_of(dp * rows + at, 16), block)
            total = out[turn % 2, mine, :].astype(f32)
            for hop in hops:
                total = total + inbox[turn % 2, hop - 1, at : at + block, :].astype(f32)
            stage[turn, at : at + block, :] = total.astype(bf16)
        for copy in exchange(turn):
            copy.wait_send()
        to_owner(turn).start()

    def early_unit(turn):
        out[turn % 2] = mm(d_t[...], ad_v[(3, 2, 1)[turn], 0], 1, 0).astype(bf16)

    def rows_copy():
        return remote(c_v, t_v, pe_s.at[0], pe_r.at[0], mate)

    def rows_out():
        return pltpu.make_async_copy(c_v, rows_o, psend.at[0])

    def branch_rows(layer, kind, turn, span):
        gate = row_mod(hot_o[span, :], tab_o, layer, kind)
        return x_v[1 - turn % 2, span, :] + gate * acc[span, :]

    def add_branch(layer, kind, turn):
        if turn >= 2:
            x_out(turn - 2).wait()
        for span in chunks():
            x_v[turn % 2, span, :] = branch_rows(layer, kind, turn, span)

    def attn_unit(layer, slot):
        k, place = layer * (cols // PIECE), slot % 2
        ready(k, slot)
        if slot >= 2:
            qo_out(layer, slot - 2).wait()
        qo = qo_v.at[place]
        qo[:, : 3 * HW] = mm(u_s[...], w_v[k, slot, :, : 3 * HW], 1, 0).astype(bf16)
        for head in range(HEADS_DEV):
            base = head * HD
            for span, near_by in bands(layer):
                query = qo[span, base : base + HD] * jnp.asarray(0.125, bf16)
                keys = qo[near_by, HW + base : HW + base + HD]
                values = qo[near_by, 2 * HW + base : 2 * HW + base + HD]
                scores = mm(keys, query, 1, 1)
                allowed = idc_o[layer, near_by, :] == idr_o[layer, :, span]
                scores = jnp.where(allowed, scores, neg_fill)
                top = jnp.max(scores, axis=0, keepdims=True)
                raw = jnp.exp(scores - top)
                total = jnp.sum(raw, axis=0, keepdims=True)
                probs = (raw * (1.0 / total)).astype(bf16)
                qo[span, 3 * HW + base : 3 * HW + base + HD] = mm(values, probs, 0, 0).T.astype(bf16)
                lse_o[layer, slot * HEADS_DEV + head, :, span] = top + jnp.log(total)
        acc[...] += mm(qo[:, 3 * HW :], w_v[k, slot, :, 3 * HW :], 1, 1)
        qo_out(layer, slot).start()

    def up_unit(layer, slot):
        k = layer * (cols // PIECE) + 1
        ready(k, slot)
        if layer > 0:
            ad_out(layer - 1, slot).wait()
        for span in chunks():
            hid = mm(u_s[span, :], w_v[k, slot], 1, 0)
            cdf = 0.5 * (1.0 + lax.erf(hid * 0.7071067811865476))
            pdf = jnp.exp(-0.5 * hid * hid) * 0.3989422804014327
            ad_v[slot, 0, span, :] = (hid * cdf).astype(bf16)
            ad_v[slot, 1, span, :] = (cdf + hid * pdf).astype(bf16)
        ad_out(layer, slot).start()

    def down_unit(layer, slot):
        k = layer * (cols // PIECE) + 2
        ready(k, slot)
        acc[...] += mm(ad_v[slot, 0], w_v[k, slot], 1, 1)

    @pl.when(jnp.logical_not(is_main))
    def _():
        route(tok, t_v, ts, tr).start()

    @pl.when(is_main)
    def _():
        keep(0).start()
        keep(1).start()
        for copy in meta_copies():
            copy.start()

    @pl.when(is_outer)
    def _():
        for k in range(count):
            cast_piece(k)
            if k == count - 1:
                route(cot, c_v, cs, cr).start()
            z_copy(k, 1, at_mp(near)).start()
            z_copy(k, 3, at_mp(far)).start()
        for plane in range(2):
            early_arrival(plane).wait_recv()
        for k in range(count):
            z_copy(k, 1, at_mp(near)).wait_send()
            z_copy(k, 3, at_mp(far)).wait_send()
        route(tok, t_v, ts, tr).wait_send()
        route(cot, c_v, cs, cr).wait_send()

    @pl.when(is_mid)
    def _():
        for k in range(count):
            cast_piece(k)
            for copy in own_copies(k):
                copy.start()
            if k == count - 1:
                pl.when(is_second)(lambda: route(cot, c_v, cs, cr).start())
            z_copy(k, 2, at_mp(other_mid)).start()
            keep_own(k)

        @pl.when(is_main)
        def _():
            mod_v[...] = mod_in[...]
            small_v[...] = small_in[...]

        @pl.when(is_second)
        def _():
            for copy in meta_copies():
                copy.wait_recv()

        column = counted((ROWS, 1), 0)
        line = counted((1, ROWS), 1)
        small = small_v[...]
        for layer in range(L):
            pos_c, clip_c, id_c, from_c = slot_meta(small, column, is_main, layer % 2 == 1)
            idc_o[layer] = id_c
            pos_s[layer] = pos_c
            pos_r, _, id_r, from_r = slot_meta(small, line, is_main, layer % 2 == 1)
            idr_o[layer] = id_r
            pos_o[layer] = pos_r
        lane = counted((ROWS, 4 * SLOTS), 1)
        lane_clip = lane - SLOTS * jnp.floor(lane / SLOTS)
        hot_o[...] = jnp.where((lane_clip == clip_c) & (lane < 3 * SLOTS), 1.0, 0.0).astype(bf16)
        for index in range(6 * L):
            tab_o[index] = split_table(mod_v[:, index * D : (index + 1) * D])
        pos_s[2] = from_c
        pos_o[2] = from_r
        collect(0)
        for span in chunks():
            x_v[0, span, :] = mm(one_hot(pos_s[0, span, :], counted((CHUNK, CAP), 1)), t_v[...], 1, 0)
        x_out(0).start()

        lifted(0, 0, 0)
        attn_unit(0, 0)
        serve_z(0, 1, 2, 3)
        serve_g(0, 1, 2)
        attn_unit(0, 1)
        serve_z(1, 1, 2)
        attn_unit(0, 2)
        serve_g(0, 3)
        serve_z(1, 3)
        attn_unit(0, 3)
        serve_g(1, 1, 2)
        add_branch(0, 2, 1)
        x_out(1).start()
        lifted(0, 3, 1)
        up_unit(0, 0)
        serve_z(2, 1, 2)
        up_unit(0, 1)
        up_unit(0, 2)
        serve_g(1, 3)
        serve_z(2, 3)
        up_unit(0, 3)
        down_unit(0, 0)
        serve_g(2, 1, 2)
        down_unit(0, 1)
        down_unit(0, 2)
        serve_z(3, 1, 2)
        serve_g(2, 3)
        down_unit(0, 3)
        serve_z(3, 3)
        x_out(0).wait()

        @pl.when(is_main)
        def _():
            for index in range(4):
                pass_on(t_v, ts, tr, index).wait_send()

        for span in chunks():
            value = branch_rows(0, 5, 2, span)
            high = value.astype(bf16)
            rest = value - high.astype(f32)
            middle = rest.astype(bf16)
            t_v[span, :] = high
            t_v[slice(ROWS + span.start, ROWS + span.stop), :] = middle
            u_s[span, :] = (rest - middle.astype(f32)).astype(bf16)
        for span in chunks():
            move = one_hot(pos_s[2, span, :], counted((CHUNK, ROWS), 1))
            x_v[0, span, :] = (
                mm(move, t_v[:ROWS, :], 1, 0) + mm(move, t_v[ROWS:, :], 1, 0) + mm(move, u_s[...], 1, 0)
            )
        x_out(2).start()
        lifted(1, 0, 2)
        qo_out(0, 2).wait()
        qo_out(0, 3).wait()
        attn_unit(1, 0)
        serve_g(3, 1, 2)
        serve_z(4, 1, 2)
        attn_unit(1, 1)
        serve_g(3, 3)
        attn_unit(1, 2)
        serve_z(4, 3)
        attn_unit(1, 3)
        serve_g(4, 1, 2)
        add_branch(1, 2, 3)
        x_out(3).start()
        lifted(1, 3, 3)
        serve_g(4, 3)
        up_unit(1, 3)
        collect(1)
        for span in chunks():
            grad = mm(one_hot(pos_s[1, span, :], counted((CHUNK, CAP), 1)), c_v[...], 1, 0)
            g_o[span, :] = grad
            d_t[:, span] = (row_mod(hot_o[span, :], tab_o, 1, 5) * grad).T.astype(bf16)
        early_unit(0)
        for copy in exchange(0):
            copy.start()
        serve_z(5, 1, 2)
        up_unit(1, 2)
        finish(0)
        early_unit(1)
        for copy in exchange(1):
            copy.start()
        up_unit(1, 1)
        serve_z(5, 3)
        finish(1)
        early_unit(2)
        for copy in exchange(2):
            copy.start()
        up_unit(1, 0)
        finish(2)
        down_unit(1, 0)
        serve_g(5, 1, 2)
        down_unit(1, 1)
        down_unit(1, 2)
        serve_g(5, 3)
        down_unit(1, 3)
        for span in chunks():
            u_s[span, :] = branch_rows(1, 5, 4, span).astype(bf16)

        @pl.when(is_main)
        def _():
            for index in range(4):
                pass_on(c_v, cs, cr, index).wait_send()

        for at in range(0, CAP, 256):
            place = one_hot(counted((256, ROWS), 0, at), pos_o[1])
            c_v[at : at + 256, :] = mm(place, u_s[...], 1, 0).astype(bf16)

        @pl.when(is_second)
        def _():
            rows_copy().start()

        @pl.when(is_main)
        def _():
            rows_copy().wait_recv()
            for at in range(0, CAP, 256):
                c_v[at : at + 256, :] = c_v[at : at + 256, :] + t_v[at : at + 256, :]
            rows_out().start()

        early_arrival(1).wait_recv()
        for turn in range(3):
            to_owner(turn).wait_send()
        x_out(2).wait()
        x_out(3).wait()
        for slot in (2, 3):
            qo_out(1, slot).wait()
        for slot in range(4):
            ad_out(1, slot).wait()
        for k in range(count):
            for copy in own_copies(k):
                copy.wait_send()
            for slot in range(4):
                w_out(k, slot).wait()
            for slot in (1, 2, 3):
                g_copy(k, slot).wait_send()
                for mine in (True, False):
                    for copy in d_copies(k, slot, mine):
                        copy.wait_send()
        for k in range(count):
            z_copy(k, 2, at_mp(other_mid)).wait_send()

    @pl.when(is_main)
    def _():
        for copy in meta_copies():
            copy.wait_send()
        rows_out().wait()

    @pl.when(is_second)
    def _():
        rows_copy().wait_send()
        route(tok, t_v, ts, tr).wait_send()
        route(cot, c_v, cs, cr).wait_send()


def run_forward(tok, cot, mod, small, par):
    sds = jax.ShapeDtypeStruct
    n_dp = lax.axis_size("dp")
    rows, cols = par.shape[1], par.shape[2]
    count = L * cols // PIECE
    peers = n_dp - 1
    return pl.pallas_call(
        partial(fwd_kernel, n_dp),
        out_shape=(
            sds((count, 4, D, PIECE), bf16), sds((2 * L, ROWS, D), f32), sds((L, 4, ROWS, D), bf16),
            sds((L, 4, 2, ROWS, FF // 4), bf16), sds((2, rows, PIECE), bf16), sds((CAP, D), bf16),
            sds((L, HEADS, 1, ROWS), f32), sds((ROWS, D), f32), sds((ROWS, 4 * SLOTS), bf16), sds((L, ROWS, 1), f32), sds((L, 1, ROWS), f32),
            sds((3, 1, ROWS), f32), sds((6 * L, 4 * SLOTS, D), bf16),
        ),
        in_specs=[any_spec(), any_spec(), vm_spec(), vm_spec(), any_spec()],
        out_specs=(any_spec(),) * 6 + (vm_spec(),) * 7,
        scratch_shapes=[
            VM((count, 4, D, PIECE), bf16), VM((count, rows, PIECE), bf16), VM((2, rows, PIECE), f32),
            VM((CAP, D), bf16), VM((CAP, D), bf16), VM((2, ROWS, D), f32), VM((ROWS, D), bf16),
            VM((ROWS, D), f32), VM((2, ROWS, D), bf16), VM((4, 2, ROWS, FF // 4), bf16), VM((8, 128), f32), VM(mod.shape, f32),
            VM((3, ROWS, 1), f32), VM((D, ROWS), bf16), VM((2, D, PIECE), bf16),
            VM((2, peers, rows, PIECE), bf16), VM((3, rows, PIECE), bf16),
            DMA((count, 3)), DMA((count, 3)), DMA((count, 3)), DMA((count, 3)),
            DMA((count, 3, 2, peers)), DMA((count, 3, 2, peers)), DMA((count, peers)), DMA((count, peers)),
            DMA((5,)), DMA((8,)), DMA((5,)), DMA((8,)), DMA((2,)), DMA((2,)), DMA((2,)),
            DMA((2,)), DMA((count, 4)), DMA((2 * L,)), DMA((2,)), DMA((4,)),
            DMA((3, peers)), DMA((3, peers)), DMA((3,)), DMA((2,)), DMA((1,)), DMA((1,)), DMA((1,)),
        ],
        compiler_params=pltpu.CompilerParams(
            collective_id=1, has_side_effects=True, vmem_limit_bytes=63 * MIB
        ),
    )(tok, cot, mod, small, par)


def share_rows(rows, n_grp):
    part = rows // n_grp
    return part if part * n_grp == rows and part % 16 == 0 else rows


def back_kernel(
    n_dp, n_grp,
    pos_r, g_in, hot, idc, idr, tables, lse, xs, qo, ad, early, rows_in,
    w_hbm, par, mom, var,
    recv, avg, mix_o, gin_o,
    g_s, x_b, w_b, a_b, q_b, u_t, d_s, d_t, dh, dq, do_s, dk_s, acc, out, inbox, stage,
    p_b, p_in, opt, gsum, diff, box, own_avg,
    xsem, wsem, asem, ce_s, ce_r, os_s, os_r, loc, pe_s, pe_r, ro_s, ro_r, rl, osem,
    as_s, as_r, bs_s, bs_r, bl, esem,
):
    grp, dp, mp = lax.axis_index("grp"), lax.axis_index("dp"), lax.axis_index("mp")
    rows, cols = par.shape[1], par.shape[2]
    quarter = mix_o.shape[0]
    share = share_rows(rows, n_grp)
    star = 1 + lax.rem(dp, 2)
    is_mid = jnp.logical_or(mp == 1, mp == 2)
    is_outer = jnp.logical_not(is_mid)
    is_main = mp == star
    is_second = jnp.logical_and(is_mid, mp != star)
    other_mid = 3 - mp
    near_outer = jnp.where(mp == 1, 0, 3)
    far_outer = 3 - near_outer
    heads = HEADS_DEV
    hw = HW
    mate = (grp, flip(dp, 1), mp)

    def at_mp(where):
        return (grp, dp, where)

    def at_grp(step):
        return (lax.rem(grp + step, n_grp), dp, mp)

    def at_dp(step):
        return (grp, lax.rem(dp + step, n_dp), mp)

    peers = [at_grp(step) for step in range(1, n_grp)]

    @pl.when(is_mid)
    def _():
        greet(
            [at_mp(0), at_mp(3), at_mp(other_mid)] + peers + [at_dp(step) for step in range(1, n_dp)]
        )

    @pl.when(is_outer)
    def _():
        greet([at_mp(1), at_mp(2)] + peers)

    def layer_of(sub):
        return 1 - sub // 2

    def slot_of(step):
        return 3 - step % 4

    units = []
    for sub in range(4):
        steps = range(4 * sub, 4 * sub + 4)
        if sub % 2:
            units += [(step, "attn") for step in steps]
        else:
            units += [(step, kind) for step in steps for kind in ("down", "up")]
    units = [unit for unit in units if unit not in ((0, "down"), (1, "down"), (2, "down"))]

    def piece_of(unit):
        step, kind = units[unit]
        return layer_of(step // 4), {"attn": 0, "up": PIECE, "down": 2 * PIECE}[kind]

    def index_of(piece):
        return piece[0] * (cols // PIECE) + piece[1] // PIECE

    def halves(piece):
        return [(0, 512), (512, PIECE)] if piece == (0, 0) else [(0, PIECE)]

    def weight_loads(step):
        sub, slot, place = step // 4, slot_of(step), step % 2
        first = layer_of(sub) * (cols // PIECE) + (1 if sub % 2 == 0 else 0)
        return [
            pltpu.make_async_copy(
                w_hbm.at[first + turn, slot], w_b.at[place, :, turn * D : turn * D + D], wsem.at[place, turn]
            )
            for turn in range(2 if sub % 2 == 0 else 1)
        ]

    def kept_load(step):
        sub, slot, place = step // 4, slot_of(step), step % 2
        layer = layer_of(sub)
        if sub % 2 == 0:
            return pltpu.make_async_copy(ad.at[layer, slot], a_b.at[place], asem.at[place])
        return pltpu.make_async_copy(qo.at[layer, slot], q_b.at[place], asem.at[place])

    def load(step):
        for copy in (kept_load(step), *weight_loads(step)):
            copy.start()

    def x_load(sub):
        source = xs.at[2 * layer_of(sub) + (1 if sub % 2 == 0 else 0)]
        return pltpu.make_async_copy(source, x_b.at[sub % 2], xsem.at[sub % 2])

    def exchange(unit):
        place = unit % 2
        result = []
        for hop in range(1, n_dp):
            target = lax.rem(dp + hop, n_dp)
            result.append(
                remote(
                    out.at[place, pl.ds(pl.multiple_of(target * rows, rows), rows)],
                    inbox.at[place, hop - 1],
                    ce_s.at[unit, hop - 1], ce_r.at[unit, hop - 1], at_dp(hop),
                )
            )
        return result

    def to_owner(unit, turns=(0, 1)):
        piece, slot = piece_of(unit), slot_of(units[unit][0])
        plane, index = (1 if slot >= 2 else 0), index_of(piece)
        result = []
        for turn, (low, high) in enumerate(halves(piece)):
            if turn not in turns:
                continue
            source = stage.at[unit, :, low:high]
            place = recv.at[plane, piece[0], :, piece[1] + low : piece[1] + high]
            if slot == 0:
                result.append(pltpu.make_async_copy(source, place, loc.at[index, turn]))
            else:
                device = at_mp((None, near_outer, other_mid, far_outer)[slot])
                result.append(
                    remote(source, place, os_s.at[unit, turn], os_r.at[index, plane, turn], device)
                )
        return result

    def owner_arrival(piece, plane, turn):
        low, high = halves(piece)[turn]
        place = recv.at[plane, piece[0], :, piece[1] + low : piece[1] + high]
        return remote(place, place, os_s.at[0, 0], os_r.at[index_of(piece), plane, turn], mate)

    early_piece = (L - 1, 2 * PIECE)

    def early_copy(plane):
        place = recv.at[plane, early_piece[0], :, early_piece[1] : early_piece[1] + PIECE]
        return pltpu.make_async_copy(early.at[plane], place, esem.at[plane])

    def finish(unit):
        place = unit % 2
        for copy in exchange(unit):
            copy.wait_recv()
        block = 96 if rows % 96 == 0 else rows
        for at in range(0, rows, block):
            mine = pl.ds(pl.multiple_of(dp * rows + at, 16), block)
            total = out[place, mine, :].astype(f32)
            for hop in range(1, n_dp):
                total = total + inbox[place, hop - 1, at : at + block, :].astype(f32)
            stage[unit, at : at + block, :] = total.astype(bf16)
        for copy in exchange(unit):
            copy.wait_send()
        for copy in to_owner(unit):
            copy.start()

    def put_rows(values):
        for at in range(0, CAP, 256):
            place = one_hot(counted((256, ROWS), 0, at), pos_r[0])
            p_b[at : at + 256, :] = mm(place, values, 1, 0).astype(bf16)

        @pl.when(is_second)
        def _():
            remote(p_b, p_in, pe_s.at[0], pe_r.at[0], mate).start()

    def quarter_of(index):
        return pl.ds(pl.multiple_of(index * quarter, quarter), quarter)

    def row_copies(which):
        source, dest = ((rows_in, mix_o), (p_b, gin_o))[which]
        return [
            remote(
                source.at[quarter_of(index)], dest, ro_s.at[which, turn], ro_r.at[which], at_mp(index)
            )
            for turn, index in enumerate((other_mid, 0, 3))
        ]

    def row_keep(which):
        source, dest = ((rows_in, mix_o), (p_b, gin_o))[which]
        return pltpu.make_async_copy(source.at[quarter_of(mp)], dest, rl.at[which])

    def send_rows(which):
        @pl.when(is_main)
        def _():
            if which == 1:
                remote(p_b, p_in, pe_s.at[0], pe_r.at[0], mate).wait_recv()
                for at in range(0, CAP, 256):
                    span = slice(at, at + 256)
                    p_b[span, :] = p_b[span, :] + p_in[span, :]
            for copy in row_copies(which):
                copy.start()
            row_keep(which).start()

    def end_rows():
        @pl.when(is_main)
        def _():
            for which in range(2):
                for copy in row_copies(which):
                    copy.wait_send()
                row_keep(which).wait()

        @pl.when(is_second)
        def _():
            remote(p_b, p_in, pe_s.at[0], pe_r.at[0], mate).wait_send()

    def rows_arrived(which, dest):
        @pl.when(jnp.logical_not(is_main))
        def _():
            remote(
                dest, dest, ro_s.at[which, 0], ro_r.at[which], at_mp(0)
            ).wait_recv()

    def diff_piece(piece, turn):
        layer, index = piece[0], index_of(piece)
        low, high = halves(piece)[turn]
        width = high - low
        span = slice(piece[1] + low, piece[1] + high)
        block = opt.shape[2]

        def opt_loads(lap):
            part, place = slice(lap * block, (lap + 1) * block), lap % 2
            return [
                pltpu.make_async_copy(
                    source.at[layer, part, span], opt.at[place, i, :, :width], osem.at[place, i]
                )
                for i, source in enumerate((par, mom, var))
            ] + [
                pltpu.make_async_copy(
                    recv.at[plane, layer, part, span], gsum.at[place, plane, :, :width],
                    osem.at[place, 3 + plane],
                )
                for plane in range(2)
            ]

        @pl.when(is_outer)
        def _():
            if piece == early_piece:
                early_copy(0).wait()
            else:
                owner_arrival(piece, 0, turn).wait_recv()

        @pl.when(is_mid)
        def _():
            own = [u for u in range(len(units)) if piece_of(u) == piece and slot_of(units[u][0]) == 0][0]
            to_owner(own, (turn,))[0].wait()

        if piece == early_piece:
            early_copy(1).wait()
        else:
            owner_arrival(piece, 1, turn).wait_recv()
        for copy in opt_loads(0):
            copy.start()
        for lap in range(rows // block):
            part, place = slice(lap * block, (lap + 1) * block), lap % 2
            if (lap + 1) * block < rows:
                for copy in opt_loads(lap + 1):
                    copy.start()
            for copy in opt_loads(lap):
                copy.wait()
            grad = gsum[place, 0, :, :width].astype(f32) + gsum[place, 1, :, :width].astype(f32)
            one = beta_one * opt[place, 1, :, :width] + (1 - beta_one) * grad
            two = beta_two * opt[place, 2, :, :width] + (1 - beta_two) * grad * grad
            step = one / (1 - beta_one**STEP) / (jnp.sqrt(two / (1 - beta_two**STEP)) + adam_eps)
            diff[index, part, low:high] = (
                inner_rate * (step + decay_rate * opt[place, 0, :, :width])
            ).astype(bf16)
        for copy in first_copies(piece, turn):
            copy.start()

    def rows_for(where):
        if share == rows:
            return slice(0, rows)
        return pl.ds(pl.multiple_of(where * share, share), share)

    def first_copies(piece, turn):
        index = index_of(piece)
        low, high = halves(piece)[turn]
        return [
            remote(
                diff.at[index, rows_for(lax.rem(grp + hop, n_grp)), low:high],
                box.at[index, hop - 1, :, low:high],
                as_s.at[index, turn, hop - 1], as_r.at[index, turn, hop - 1], at_grp(hop),
            )
            for hop in range(1, n_grp)
        ]

    def second_copies(piece, turn):
        index = index_of(piece)
        low, high = halves(piece)[turn]
        place = avg.at[piece[0], rows_for(grp), piece[1] + low : piece[1] + high]
        return [
            remote(
                own_avg.at[index, :, low:high], place,
                bs_s.at[index, turn, hop - 1], bs_r.at[index, turn, hop - 1], at_grp(hop),
            )
            for hop in range(1, n_grp)
        ]

    def second_arrivals(piece, turn):
        index = index_of(piece)
        low, high = halves(piece)[turn]
        result = []
        for hop in range(1, n_grp):
            source = lax.rem(grp + n_grp - hop, n_grp)
            place = avg.at[piece[0], rows_for(source), piece[1] + low : piece[1] + high]
            result.append(
                remote(
                    place, place, bs_s.at[index, turn, hop - 1], bs_r.at[index, turn, hop - 1], at_grp(hop)
                )
            )
        return result

    def own_copy(piece, turn):
        index = index_of(piece)
        low, high = halves(piece)[turn]
        place = avg.at[piece[0], rows_for(grp), piece[1] + low : piece[1] + high]
        return pltpu.make_async_copy(own_avg.at[index, :, low:high], place, bl.at[index, turn])

    def mean_piece(piece, turn):
        index = index_of(piece)
        low, high = halves(piece)[turn]
        for copy in first_copies(piece, turn):
            copy.wait_recv()
        total = diff[index, rows_for(grp), low:high].astype(f32)
        for hop in range(1, n_grp):
            total = total + box[index, hop - 1, :, low:high].astype(f32)
        own_avg[index, :, low:high] = (total / n_grp).astype(bf16)
        own_copy(piece, turn).start()
        if share != rows:
            for copy in second_copies(piece, turn):
                copy.start()

    def end_piece(piece, turn):
        for copy in first_copies(piece, turn):
            copy.wait_send()
        own_copy(piece, turn).wait()
        if share != rows:
            for copy in second_copies(piece, turn):
                copy.wait_send()
            for copy in second_arrivals(piece, turn):
                copy.wait_recv()

    def down_start(sub):
        layer = layer_of(sub)
        for part in chunks():
            down = row_mod(hot[part, :], tables, layer, 5) * g_s[part, :]
            d_s[part, :] = down.astype(bf16)
            d_t[:, part] = down.T.astype(bf16)

    def up_start(sub):
        layer, place = layer_of(sub), sub % 2
        x_load(sub).wait()
        for part in chunks():
            normed, _ = moments(x_b[place, part, :])
            shift = row_mod(hot[part, :], tables, layer, 3)
            scale = row_mod(hot[part, :], tables, layer, 4)
            u_t[:, part] = (normed * (1.0 + scale) + shift).T.astype(bf16)
        acc[...] = jnp.zeros_like(acc)

    def down_unit(step, turn):
        out[turn] = mm(d_t[...], a_b[step % 2, 0], 1, 0).astype(bf16)

    def up_unit(step, turn):
        place = step % 2
        for part in chunks():
            dact = mm(d_s[part, :], w_b[place, :, D:], 1, 0)
            dh[part, :] = (dact * a_b[place, 1, part, :].astype(f32)).astype(bf16)
        out[turn] = mm(u_t[...], dh[...], 1, 0).astype(bf16)
        acc[...] += mm(dh[...], w_b[place, :, :D], 1, 1)

    def attn_start(sub):
        layer, place = layer_of(sub), sub % 2
        x_load(sub).wait()
        for part in chunks():
            normed, _ = moments(x_b[place, part, :])
            shift = row_mod(hot[part, :], tables, layer, 0)
            scale = row_mod(hot[part, :], tables, layer, 1)
            u_t[:, part] = (normed * (1.0 + scale) + shift).T.astype(bf16)
            branch = row_mod(hot[part, :], tables, layer, 2) * g_s[part, :]
            d_s[part, :] = branch.astype(bf16)
            d_t[:, part] = branch.T.astype(bf16)
        acc[...] = jnp.zeros_like(acc)

    def attn_unit(step, turn):
        layer, place, slot = layer_of(step // 4), step % 2, slot_of(step)
        out[turn, :, 3 * hw : D] = mm(d_t[...], q_b[place, :, 3 * hw :], 1, 0).astype(bf16)
        do_s[...] = mm(d_s[...], w_b[place, :, 3 * hw : D], 1, 0).astype(bf16)
        for head in range(heads):
            base = head * HD
            dk_s[...] = jnp.zeros_like(dk_s)
            for span, near_by in bands(layer):
                query = q_b[place, span, base : base + HD]
                keys = q_b[place, near_by, hw + base : hw + base + HD]
                values = q_b[place, near_by, 2 * hw + base : 2 * hw + base + HD]
                grad = do_s[span, base : base + HD]
                scores = mm(keys, query * jnp.asarray(0.125, bf16), 1, 1)
                allowed = idc[layer, near_by, :] == idr[layer, :, span]
                probs = jnp.where(
                    allowed, jnp.exp(scores - lse[layer, slot * heads + head, :, span]), 0.0
                )
                dk_s[1, near_by, :] += mm(probs.astype(bf16), grad, 1, 0)
                weighted = probs * mm(values, grad, 1, 1)
                delta = jnp.sum(weighted, axis=0, keepdims=True)
                ds = (weighted - probs * delta).astype(bf16)
                dq[span, base : base + HD] = (mm(keys, ds, 0, 0).T * 0.125).astype(bf16)
                dk_s[0, near_by, :] += mm(ds, query, 1, 0)
            dq[:, hw + base : hw + base + HD] = (dk_s[0] * 0.125).astype(bf16)
            dq[:, 2 * hw + base : 2 * hw + base + HD] = dk_s[1].astype(bf16)
        out[turn, :, : 3 * hw] = mm(u_t[...], dq[...], 1, 0).astype(bf16)
        acc[...] += mm(dq[...], w_b[place, :, : 3 * hw], 1, 1)

    def sub_end(sub):
        layer, place = layer_of(sub), sub % 2
        row = 4 if sub % 2 == 0 else 1
        for part in chunks():
            normed, inv_std = moments(x_b[place, part, :])
            scale = row_mod(hot[part, :], tables, layer, row)
            g_s[part, :] = g_s[part, :] + norm_back(acc[part, :] * (1.0 + scale), normed, inv_std)

    def to_frame_order():
        for part in chunks():
            high = g_s[part, :].astype(bf16)
            dh[part, :] = high
            d_s[part, :] = (g_s[part, :] - high.astype(f32)).astype(bf16)
        for part in chunks():
            move = one_hot(counted((CHUNK, ROWS), 0, part.start), pos_r[2])
            g_s[part, :] = mm(move, dh[...], 1, 0) + mm(move, d_s[...], 1, 0)

    def chunk(sub, kind):
        return layer_of(sub), {"attn": 0, "up": PIECE, "down": 2 * PIECE}[kind]

    order = [chunk(0, "down"), chunk(0, "up"), chunk(1, "attn"), chunk(2, "down"), chunk(2, "up"), chunk(3, "attn")]
    served = {7: (diff_piece, 0), 9: (mean_piece, 0), 14: (diff_piece, 1), 17: (mean_piece, 1)}

    early_copy(1).start()
    pl.when(is_outer)(lambda: early_copy(0).start())

    @pl.when(is_mid)
    def _():
        x_load(0).start()
        send_rows(0)
        load(0)
        load(1)
        g_s[...] = g_in[...]
        for unit, (step, kind) in enumerate(units):
            sub = step // 4
            first_of_sub = unit == 0 or units[unit - 1][0] // 4 != sub
            last_of_step = unit + 1 == len(units) or step not in [s for s, _ in units[unit + 1 :]]
            last_of_sub = unit + 1 == len(units) or units[unit + 1][0] // 4 != sub
            if first_of_sub:
                if sub < 3:
                    x_load(sub + 1).start()
                (attn_start if kind == "attn" else down_start)(sub)
            if unit == 0 or units[unit - 1][0] != step:
                kept_load(step).wait()
            if kind != "down":
                if kind == "up" and step % 4 == 0:
                    up_start(sub)
                for copy in weight_loads(step):
                    copy.wait()
            {"attn": attn_unit, "up": up_unit, "down": down_unit}[kind](step, unit % 2)
            if unit > 0:
                finish(unit - 1)
            for copy in exchange(unit):
                copy.start()
            if last_of_step and step + 2 < 16:
                load(step + 2)
            if last_of_sub:
                sub_end(sub)
                if sub == 1:
                    to_frame_order()
            if unit in served:
                action, which = served[unit]
                action(order[which], 0)
        put_rows(g_s[...].astype(bf16))
        finish(len(units) - 1)
        send_rows(1)
        for piece in order[2:5]:
            diff_piece(piece, 0)
            mean_piece(piece, 0)
        for turn in range(2):
            diff_piece(order[5], turn)
        for turn in range(2):
            mean_piece(order[5], turn)
        for unit, (step, _) in enumerate(units):
            if slot_of(step) != 0:
                for copy in to_owner(unit):
                    copy.wait_send()
        end_rows()

    @pl.when(is_outer)
    def _():
        for piece in order[:5]:
            diff_piece(piece, 0)
            mean_piece(piece, 0)
        for turn in range(2):
            diff_piece(order[5], turn)
        for turn in range(2):
            mean_piece(order[5], turn)

    for which, dest in ((0, mix_o), (1, gin_o)):
        rows_arrived(which, dest)
    for piece in order:
        for turn in range(len(halves(piece))):
            end_piece(piece, turn)


def run_back(pos, g, hot, idc, idr, tables, lse, xs, qo, ad, early, rows_in, w, par, mom, var, quarter):
    sds = jax.ShapeDtypeStruct
    n_dp, n_grp = lax.axis_size("dp"), lax.axis_size("grp")
    rows, cols = par.shape[1], par.shape[2]
    share = share_rows(rows, n_grp)
    count = L * cols // PIECE
    far, peers = n_dp - 1, n_grp - 1
    block = 96 if rows % 96 == 0 else rows
    return pl.pallas_call(
        partial(back_kernel, n_dp, n_grp),
        out_shape=(
            sds((2, L, rows, cols), bf16), sds((L, rows, cols), bf16),
            sds((quarter, D), bf16), sds((quarter, D), bf16),
        ),
        in_specs=[vm_spec()] * 7 + [any_spec()] * 9,
        out_specs=(any_spec(),) * 4,
        scratch_shapes=[
            VM((ROWS, D), f32), VM((2, ROWS, D), f32), VM((2, D, 2 * D), bf16),
            VM((2, 2, ROWS, D), bf16), VM((2, ROWS, D), bf16),
            VM((D, ROWS), bf16), VM((ROWS, D), bf16), VM((D, ROWS), bf16), VM((ROWS, D), bf16),
            VM((ROWS, 9 * HD), bf16), VM((ROWS, 3 * HD), bf16), VM((2, ROWS, HD), f32), VM((ROWS, D), f32),
            VM((2, D, PIECE), bf16), VM((2, far, rows, PIECE), bf16), VM((4 * count, rows, PIECE), bf16),
            VM((CAP, D), bf16), VM((CAP, D), bf16),
            VM((2, 3, block, PIECE), f32), VM((2, 2, block, PIECE), bf16),
            VM((count, rows, PIECE), bf16), VM((count, peers, share, PIECE), bf16),
            VM((count, share, PIECE), bf16),
            DMA((2,)), DMA((2, 2)), DMA((2,)), DMA((4 * count, far)), DMA((4 * count, far)),
            DMA((4 * count, 2)), DMA((count, 2, 2)), DMA((count, 2)),
            DMA((2,)), DMA((2,)), DMA((2, 3)), DMA((2,)), DMA((2,)), DMA((2, 5)),
            DMA((count, 2, peers)), DMA((count, 2, peers)), DMA((count, 2, peers)), DMA((count, 2, peers)),
            DMA((count, 2)), DMA((2,)),
        ],
        compiler_params=pltpu.CompilerParams(
            collective_id=2, has_side_effects=True, vmem_limit_bytes=63 * MIB
        ),
    )(pos, g, hot, idc, idr, tables, lse, xs, qo, ad, early, rows_in, w, par, mom, var)


def last_kernel(
    par, mom, var, out_mom, ga, gb, avg, rows_m, rows_g, tok, frames, patches,
    new_m, new_v, out_a, out_m, out_w, out_l, mixed, grad_in,
):
    @pl.when(jnp.logical_and(pl.program_id(0) == 0, pl.program_id(1) == 0))
    def _():
        total = frames[:, 0:1] * patches[:, 0:1]
        for clip in range(1, SLOTS):
            total = total + frames[:, clip : clip + 1] * patches[:, clip : clip + 1]
        first = lax.axis_index("mp") * tok.shape[0]
        live = first + lax.broadcasted_iota(jnp.int32, (tok.shape[0], 1), 0) < total
        mixed[...] = jnp.where(live, rows_m[...].astype(f32), tok[...].astype(f32)).astype(bf16)
        grad_in[...] = jnp.where(live, rows_g[...].astype(f32), 0.0)

    grad = ga[...].astype(f32) + gb[...].astype(f32)
    new_m[...] = beta_one * mom[...] + (1 - beta_one) * grad
    new_v[...] = beta_two * var[...] + (1 - beta_two) * grad * grad
    average = avg[...].astype(f32)
    momentum = outer_mu * out_mom[...] + average
    updated = par[...] - outer_rate * (average + outer_mu * momentum)
    out_a[...] = average
    out_m[...] = momentum
    out_w[...] = updated
    out_l[...] = updated.astype(bf16)


def run_last(par, mom, var, out_mom, recv, avg, rows_m, rows_g, tok, frames, patches):
    rows, cols = par.shape[1], par.shape[2]
    block = 96 if rows % 96 == 0 else rows
    sds = jax.ShapeDtypeStruct
    full = pl.BlockSpec((None, block, cols), lambda i, j: (i, j, 0))

    def plane(which):
        return pl.BlockSpec((None, None, block, cols), lambda i, j: (which, i, j, 0))

    return pl.pallas_call(
        last_kernel,
        grid=(L, rows // block),
        out_shape=(sds(par.shape, f32),) * 5 + (sds(par.shape, bf16), sds(tok.shape, bf16), sds(tok.shape, f32)),
        in_specs=[full] * 4 + [plane(0), plane(1), full] + [vm_spec()] * 5,
        out_specs=(full,) * 6 + (vm_spec(),) * 2,
        compiler_params=pltpu.CompilerParams(vmem_limit_bytes=62 * MIB),
    )(par, mom, var, out_mom, recv, recv, avg, rows_m, rows_g, tok, frames, patches)


def body(
    tokens, cotangent, modulation, clip_frames, clip_patches, params, first_moment, second_moment,
    outer_momentum,
):
    quarter = tokens.shape[1]
    small = jnp.concatenate([clip_frames, clip_patches], axis=0).astype(f32)
    small = jnp.pad(small, ((0, 6), (0, 128 - SLOTS)))
    w, xs, qo, ad, early, rows_in, lse, gradient, hot, idc, idr, pos, tables = run_forward(
        tokens[0], cotangent[0], modulation[0], small, params
    )
    recv, avg, mixed_rows, grad_rows = run_back(
        pos, gradient, hot, idc, idr, tables, lse, xs, qo, ad, early, rows_in, w,
        params, first_moment[0], second_moment[0], quarter,
    )
    new_m, new_v, average, momentum, updated, low, mixed, input_grad = run_last(
        params, first_moment[0], second_moment[0], outer_momentum, recv, avg,
        mixed_rows, grad_rows, tokens[0], clip_frames, clip_patches,
    )
    return (
        mixed[None], input_grad[None], new_m[None], new_v[None], average, momentum, updated, low,
    )


def solution(mesh):
    in_specs = (
        P("grp", ("dp", "mp"), None),
        P("grp", ("dp", "mp"), None),
        P("grp", "dp", None),
        P("grp", "dp"),
        P("grp", "dp"),
        P(None, "dp", "mp"),
        P("grp", None, "dp", "mp"),
        P("grp", None, "dp", "mp"),
        P(None, "dp", "mp"),
    )
    out_specs = (
        P("grp", ("dp", "mp"), None),
        P("grp", ("dp", "mp"), None),
        P("grp", None, "dp", "mp"),
        P("grp", None, "dp", "mp"),
        P(None, "dp", "mp"),
        P(None, "dp", "mp"),
        P(None, "dp", "mp"),
        P(None, "dp", "mp"),
    )
    return jax.shard_map(body, mesh=mesh, in_specs=in_specs, out_specs=out_specs, check_vma=False)
```

```python
from functools import partial

import jax
import jax.numpy as jnp
from jax import lax
from jax.experimental import pallas as pl
from jax.experimental.pallas import tpu as pltpu
from jax.sharding import PartitionSpec as P

D = 768
HEADS = 12
HD = 64
FF = 3072
L = 2
STEP = 5
CAP = 1024
SLOTS = 4
LONGF = 64
ROWS = CAP // 2
CHUNK = 128
PIECE = 768
SIDE = PIECE // 2

ln_eps = 1e-06
neg_fill = -1e30
beta_one = 0.9
beta_two = 0.999
adam_eps = 1e-08
inner_rate = 0.04
decay_rate = 0.1
outer_rate = 0.7
outer_mu = 0.5

f32 = jnp.float32
bf16 = jnp.bfloat16
VM = pltpu.VMEM
DMA = pltpu.SemaphoreType.DMA
MESH_ID = pl.DeviceIdType.MESH
MIB = 2**20
HEADS_DEV = 3
HW = HEADS_DEV * HD


def mm(left, right, lc, rc):
    return lax.dot_general(left, right, (((lc,), (rc,)), ((), ())), preferred_element_type=f32)


def moments(values):
    centered = values - jnp.mean(values, axis=-1, keepdims=True)
    inv_std = lax.rsqrt(jnp.mean(centered * centered, axis=-1, keepdims=True) + ln_eps)
    return centered * inv_std, inv_std


def norm_back(grad_normed, normed, inv_std):
    inner = grad_normed - jnp.mean(grad_normed, axis=-1, keepdims=True)
    inner = inner - normed * jnp.mean(grad_normed * normed, axis=-1, keepdims=True)
    return inv_std * inner


def split_table(table):
    high = table.astype(bf16).astype(f32)
    rest = table - high
    middle = rest.astype(bf16).astype(f32)
    return jnp.concatenate([high, middle, rest - middle, jnp.zeros_like(table)], axis=0).astype(bf16)


def row_mod(hot, tables, layer, kind):
    return mm(hot, tables[layer * 6 + kind], 1, 0)


def chunks():
    return [slice(at, at + CHUNK) for at in range(0, ROWS, CHUNK)]


def any_spec():
    return pl.BlockSpec(memory_space=pl.ANY)


def vm_spec():
    return pl.BlockSpec(memory_space=VM)


def flip(index, bit):
    return index + bit - 2 * bit * lax.rem(index // bit, 2)


def slot_meta(small, index, long_core, by_patch):
    frames = [small[0:1, clip : clip + 1] for clip in range(SLOTS)]
    patches = [small[1:2, clip : clip + 1] for clip in range(SLOTS)]
    zero = jnp.zeros_like(frames[0])
    start, long_start, long_size = zero, zero, zero
    starts, ends = [], []
    for clip in range(SLOTS):
        size = frames[clip] * patches[clip]
        is_long = frames[clip] == float(LONGF)
        long_start = long_start + jnp.where(is_long, start, 0.0)
        long_size = long_size + jnp.where(is_long, size, 0.0)
        starts.append(start)
        start = start + size
        ends.append(start)
    pos_long = index + long_start
    pos_short = jnp.where(index < long_start, index, index + long_size)
    pos = jnp.where(long_core, pos_long, pos_short)
    clip_of = jnp.zeros_like(index)
    for clip in range(SLOTS):
        clip_of = clip_of + jnp.where(pos >= ends[clip], 1.0, 0.0)
    limit = jnp.where(long_core, long_start + long_size, start)
    live = pos < limit
    clip_of = jnp.where(live, clip_of, float(SLOTS))
    begin, many, wide = jnp.zeros_like(index), jnp.ones_like(index), jnp.ones_like(index)
    for clip in range(SLOTS):
        hit = clip_of == float(clip)
        begin = jnp.where(hit, starts[clip], begin)
        many = jnp.where(hit, frames[clip], many)
        wide = jnp.where(hit, patches[clip], wide)
    offset = pos - begin
    inner = many if by_patch else wide
    group = jnp.floor((offset + 0.5) / inner)
    within = offset - group * inner
    source = within * wide + group if by_patch else offset
    ident = jnp.where(live, clip_of * CAP + group, -1.0 - index)
    origin = jnp.where(live, index - offset + source, index)
    return jnp.where(live, begin + source, -1.0), clip_of, ident, origin


def one_hot(left, right):
    return jnp.where(left == right, 1.0, 0.0).astype(bf16)


def counted(shape, dim, first=0):
    return lax.broadcasted_iota(jnp.int32, shape, dim).astype(f32) + float(first)


def bands(layer):
    halo = 32 if layer % 2 == 0 else 64
    return [
        (slice(at, at + CHUNK), slice(max(at - halo, 0), min(at + CHUNK + halo, ROWS)))
        for at in range(0, ROWS, CHUNK)
    ]


def remote(src, dst, send, receive, device):
    return pltpu.make_async_remote_copy(
        src_ref=src, dst_ref=dst, send_sem=send, recv_sem=receive,
        device_id=device, device_id_type=MESH_ID,
    )


def greet(devices):
    barrier = pltpu.get_barrier_semaphore()
    for device in devices:
        pl.semaphore_signal(barrier, inc=1, device_id=device, device_id_type=MESH_ID)
    pl.semaphore_wait(barrier, len(devices))


def fwd_kernel(
    n_dp, tok, cot, mod_in, small_in, par,
    w_o, xs_o, qo_o, ad_o, early_o, rows_o, lse_o, g_o, hot_o, idc_o, idr_o, pos_o, tab_o,
    w_v, wb, par_f, t_v, c_v, x_v, u_s, acc, qo_v, ad_v, small_v, mod_v, pos_s, d_t, out, inbox, stage,
    zs, zr, gs, gr, ds, dr, os_s, os_r, ts, tr, cs, cr, tl, ms, mr, psem, wsem, xsem, qsem, asem, ce_s, ce_r, ow_s, ow_r, pe_s, pe_r, psend,
):
    grp, dp, mp = lax.axis_index("grp"), lax.axis_index("dp"), lax.axis_index("mp")
    rows, cols = par.shape[1], par.shape[2]
    quarter = tok.shape[0]
    pieces = [(layer, at) for layer in range(L) for at in range(0, cols, PIECE)]
    count = len(pieces)
    star = 1 + lax.rem(dp, 2)
    is_mid = jnp.logical_or(mp == 1, mp == 2)
    is_outer = jnp.logical_not(is_mid)
    is_main = mp == star
    is_second = jnp.logical_and(is_mid, mp != star)
    other_mid = 3 - mp
    near = jnp.where(mp == 0, 1, 2)
    far = 3 - near
    my_rows = pl.ds(pl.multiple_of(dp * rows, rows), rows)
    mate = (grp, flip(dp, 1), mp)
    hops = range(1, n_dp)

    def at_mp(where):
        return (grp, dp, where)

    def at_grp(bit):
        return (flip(grp, bit), dp, mp)

    def at_dp(step):
        return (grp, lax.rem(dp + step, n_dp), mp)

    @pl.when(is_mid)
    def _():
        greet(
            [at_mp(0), at_mp(3), at_mp(other_mid), at_grp(1), at_grp(2)] + [at_dp(hop) for hop in hops]
        )

    @pl.when(is_outer)
    def _():
        greet([at_mp(1), at_mp(2)])

    def bit_of(k, slot):
        return 1 + (k + slot) % 2

    def half(k, slot, mine):
        index = lax.rem(grp // bit_of(k, slot), 2)
        if not mine:
            index = 1 - index
        return pl.ds(pl.multiple_of(index * SIDE, 128), SIDE)

    def z_copy(k, slot, device):
        span = half(k, slot, True)
        return remote(
            wb.at[k, :, span], w_v.at[k, slot, my_rows, span], zs.at[k, slot - 1], zr.at[k, slot - 1], device
        )

    def g_copy(k, slot):
        place = w_v.at[k, slot, my_rows, half(k, slot, True)]
        return remote(place, place, gs.at[k, slot - 1], gr.at[k, slot - 1], at_grp(bit_of(k, slot)))

    def d_copies(k, slot, mine):
        place, turn = w_v.at[k, slot, my_rows, half(k, slot, mine)], 0 if mine else 1
        return [
            remote(
                place, place, ds.at[k, slot - 1, turn, hop - 1], dr.at[k, slot - 1, turn, hop - 1], at_dp(hop)
            )
            for hop in hops
        ]

    def rows_of(hop):
        source = lax.rem(dp + n_dp - hop, n_dp)
        return pl.ds(pl.multiple_of(source * rows, rows), rows)

    def d_arrivals(k, slot, mine):
        turn = 0 if mine else 1
        result = []
        for hop in hops:
            place = w_v.at[k, slot, rows_of(hop), half(k, slot, mine)]
            result.append(
                remote(
                    place, place, ds.at[k, slot - 1, turn, hop - 1], dr.at[k, slot - 1, turn, hop - 1],
                    at_dp(hop),
                )
            )
        return result

    def own_copies(k):
        return [
            remote(wb.at[k], w_v.at[k, 0, my_rows], os_s.at[k, hop - 1], os_r.at[k, hop - 1], at_dp(hop))
            for hop in hops
        ]

    def own_arrivals(k):
        return [
            remote(
                wb.at[k], w_v.at[k, 0, rows_of(hop)], os_s.at[k, hop - 1], os_r.at[k, hop - 1], at_dp(hop)
            )
            for hop in hops
        ]

    def part(ref, index):
        return ref.at[pl.ds(pl.multiple_of(index * quarter, quarter), quarter)]

    def route(src, out, send, receive):
        return remote(src, part(out, mp), send.at[0], receive.at[mp], at_mp(star))

    def pass_on(out, send, receive, index):
        return remote(part(out, index), part(out, index), send.at[1 + index], receive.at[4 + index], mate)

    def main_arrival(out, send, receive, index):
        return remote(part(out, index), part(out, index), send.at[0], receive.at[index], mate)

    def second_arrival(out, send, receive, index):
        return remote(part(out, index), part(out, index), send.at[0], receive.at[4 + index], mate)

    routes = ((tok, t_v, ts, tr), (cot, c_v, cs, cr))

    def keep(which):
        src, out = routes[which][:2]
        return pltpu.make_async_copy(src, part(out, mp), tl.at[which])

    def collect(which):
        out, send, receive = routes[which][1:]

        @pl.when(is_main)
        def _():
            keep(which).wait()
            pass_on(out, send, receive, mp).start()
            for index in (other_mid, 0, 3):
                main_arrival(out, send, receive, index).wait_recv()
                pass_on(out, send, receive, index).start()

        @pl.when(is_second)
        def _():
            for index in range(4):
                second_arrival(out, send, receive, index).wait_recv()

    def meta_copies():
        return [
            remote(mod_in, mod_v, ms.at[0], mr.at[0], mate),
            remote(small_in, small_v, ms.at[1], mr.at[1], mate),
        ]

    def par_load(k):
        layer, at = pieces[k]
        return pltpu.make_async_copy(par.at[layer, :, at : at + PIECE], par_f.at[k % 2], psem.at[k % 2])

    def cast_piece(k):
        if k == 0:
            par_load(0).start()
        if k + 1 < count:
            par_load(k + 1).start()
        par_load(k).wait()
        block = 96 if rows % 96 == 0 else rows
        for at in range(0, rows, block):
            wb[k, at : at + block, :] = par_f[k % 2, at : at + block, :].astype(bf16)

    def keep_own(k):
        block = 96 if rows % 96 == 0 else rows
        for at in range(0, rows, block):
            spot = pl.ds(pl.multiple_of(dp * rows + at, 16), block)
            w_v[k, 0, spot, :] = wb[k, at : at + block, :]

    def w_out(k, slot):
        return pltpu.make_async_copy(w_v.at[k, slot], w_o.at[k, slot], wsem.at[k, slot])

    def x_out(turn):
        return pltpu.make_async_copy(x_v.at[turn % 2], xs_o.at[turn], xsem.at[turn])

    def qo_out(layer, slot):
        return pltpu.make_async_copy(qo_v.at[slot % 2], qo_o.at[layer, slot], qsem.at[slot % 2])

    def ad_out(layer, slot):
        return pltpu.make_async_copy(ad_v.at[slot], ad_o.at[layer, slot], asem.at[slot])

    def serve_z(k, *slots):
        for slot in slots:
            z_copy(k, slot, at_mp(other_mid)).wait_recv()
            g_copy(k, slot).start()
            for copy in d_copies(k, slot, True):
                copy.start()

    def serve_g(k, *slots):
        for slot in slots:
            g_copy(k, slot).wait_recv()
            for copy in d_copies(k, slot, False):
                copy.start()

    def ready(k, slot):
        if slot == 0:
            for copy in own_arrivals(k):
                copy.wait_recv()
        else:
            for mine in (True, False):
                for copy in d_arrivals(k, slot, mine):
                    copy.wait_recv()
        w_out(k, slot).start()

    def lifted(layer, kind, turn):
        for span in chunks():
            normed, _ = moments(x_v[turn % 2, span, :])
            shift = row_mod(hot_o[span, :], tab_o, layer, kind)
            scale = row_mod(hot_o[span, :], tab_o, layer, kind + 1)
            u_s[span, :] = (normed * (1.0 + scale) + shift).astype(bf16)
        acc[...] = jnp.zeros_like(acc)

    def exchange(turn):
        result = []
        for hop in hops:
            target = lax.rem(dp + hop, n_dp)
            result.append(
                remote(
                    out.at[turn % 2, pl.ds(pl.multiple_of(target * rows, rows), rows)],
                    inbox.at[turn % 2, hop - 1],
                    ce_s.at[turn, hop - 1], ce_r.at[turn, hop - 1], at_dp(hop),
                )
            )
        return result

    def to_owner(turn):
        close = jnp.where(mp == 1, 0, 3)
        device = at_mp((3 - close, other_mid, close)[turn])
        plane = (1, 1, 0)[turn]
        return remote(stage.at[turn], early_o.at[plane], ow_s.at[turn], ow_r.at[plane], device)

    def early_arrival(plane):
        return remote(early_o.at[plane], early_o.at[plane], ow_s.at[0], ow_r.at[plane], mate)

    def finish(turn):
        for copy in exchange(turn):
            copy.wait_recv()
        block = 96 if rows % 96 == 0 else rows
        for at in range(0, rows, block):
            mine = pl.ds(pl.multiple_of(dp * rows + at, 16), block)
            total = out[turn % 2, mine, :].astype(f32)
            for hop in hops:
                total = total + inbox[turn % 2, hop - 1, at : at + block, :].astype(f32)
            stage[turn, at : at + block, :] = total.astype(bf16)
        for copy in exchange(turn):
            copy.wait_send()
        to_owner(turn).start()

    def early_unit(turn):
        out[turn % 2] = mm(d_t[...], ad_v[(3, 2, 1)[turn], 0], 1, 0).astype(bf16)

    def rows_copy():
        return remote(c_v, t_v, pe_s.at[0], pe_r.at[0], mate)

    def rows_out():
        return pltpu.make_async_copy(c_v, rows_o, psend.at[0])

    def branch_rows(layer, kind, turn, span):
        gate = row_mod(hot_o[span, :], tab_o, layer, kind)
        return x_v[1 - turn % 2, span, :] + gate * acc[span, :]

    def add_branch(layer, kind, turn):
        if turn >= 2:
            x_out(turn - 2).wait()
        for span in chunks():
            x_v[turn % 2, span, :] = branch_rows(layer, kind, turn, span)

    def attn_unit(layer, slot):
        k, place = layer * (cols // PIECE), slot % 2
        ready(k, slot)
        if slot >= 2:
            qo_out(layer, slot - 2).wait()
        qo = qo_v.at[place]
        qo[:, : 3 * HW] = mm(u_s[...], w_v[k, slot, :, : 3 * HW], 1, 0).astype(bf16)
        for head in range(HEADS_DEV):
            base = head * HD
            for span, near_by in bands(layer):
                query = qo[span, base : base + HD] * jnp.asarray(0.125, bf16)
                keys = qo[near_by, HW + base : HW + base + HD]
                values = qo[near_by, 2 * HW + base : 2 * HW + base + HD]
                scores = mm(keys, query, 1, 1)
                allowed = idc_o[layer, near_by, :] == idr_o[layer, :, span]
                scores = jnp.where(allowed, scores, neg_fill)
                top = jnp.max(scores, axis=0, keepdims=True)
                raw = jnp.exp(scores - top)
                total = jnp.sum(raw, axis=0, keepdims=True)
                probs = (raw * (1.0 / total)).astype(bf16)
                qo[span, 3 * HW + base : 3 * HW + base + HD] = mm(values, probs, 0, 0).T.astype(bf16)
                lse_o[layer, slot * HEADS_DEV + head, :, span] = top + jnp.log(total)
        acc[...] += mm(qo[:, 3 * HW :], w_v[k, slot, :, 3 * HW :], 1, 1)
        qo_out(layer, slot).start()

    def up_unit(layer, slot):
        k = layer * (cols // PIECE) + 1
        ready(k, slot)
        if layer > 0:
            ad_out(layer - 1, slot).wait()
        for span in chunks():
            hid = mm(u_s[span, :], w_v[k, slot], 1, 0)
            cdf = 0.5 * (1.0 + lax.erf(hid * 0.7071067811865476))
            pdf = jnp.exp(-0.5 * hid * hid) * 0.3989422804014327
            ad_v[slot, 0, span, :] = (hid * cdf).astype(bf16)
            ad_v[slot, 1, span, :] = (cdf + hid * pdf).astype(bf16)
        ad_out(layer, slot).start()

    def down_unit(layer, slot):
        k = layer * (cols // PIECE) + 2
        ready(k, slot)
        acc[...] += mm(ad_v[slot, 0], w_v[k, slot], 1, 1)

    @pl.when(jnp.logical_not(is_main))
    def _():
        route(tok, t_v, ts, tr).start()

    @pl.when(is_main)
    def _():
        keep(0).start()
        keep(1).start()
        for copy in meta_copies():
            copy.start()

    @pl.when(is_outer)
    def _():
        for k in range(count):
            cast_piece(k)
            if k == count - 1:
                route(cot, c_v, cs, cr).start()
            z_copy(k, 1, at_mp(near)).start()
            z_copy(k, 3, at_mp(far)).start()
        for plane in range(2):
            early_arrival(plane).wait_recv()
        for k in range(count):
            z_copy(k, 1, at_mp(near)).wait_send()
            z_copy(k, 3, at_mp(far)).wait_send()
        route(tok, t_v, ts, tr).wait_send()
        route(cot, c_v, cs, cr).wait_send()

    @pl.when(is_mid)
    def _():
        for k in range(count):
            cast_piece(k)
            for copy in own_copies(k):
                copy.start()
            if k == count - 1:
                pl.when(is_second)(lambda: route(cot, c_v, cs, cr).start())
            z_copy(k, 2, at_mp(other_mid)).start()
            keep_own(k)

        @pl.when(is_main)
        def _():
            mod_v[...] = mod_in[...]
            small_v[...] = small_in[...]

        @pl.when(is_second)
        def _():
            for copy in meta_copies():
                copy.wait_recv()

        column = counted((ROWS, 1), 0)
        line = counted((1, ROWS), 1)
        small = small_v[...]
        for layer in range(L):
            pos_c, clip_c, id_c, from_c = slot_meta(small, column, is_main, layer % 2 == 1)
            idc_o[layer] = id_c
            pos_s[layer] = pos_c
            pos_r, _, id_r, from_r = slot_meta(small, line, is_main, layer % 2 == 1)
            idr_o[layer] = id_r
            pos_o[layer] = pos_r
        lane = counted((ROWS, 4 * SLOTS), 1)
        lane_clip = lane - SLOTS * jnp.floor(lane / SLOTS)
        hot_o[...] = jnp.where((lane_clip == clip_c) & (lane < 3 * SLOTS), 1.0, 0.0).astype(bf16)
        for index in range(6 * L):
            tab_o[index] = split_table(mod_v[:, index * D : (index + 1) * D])
        pos_s[2] = from_c
        pos_o[2] = from_r
        collect(0)
        for span in chunks():
            x_v[0, span, :] = mm(one_hot(pos_s[0, span, :], counted((CHUNK, CAP), 1)), t_v[...], 1, 0)
        x_out(0).start()

        lifted(0, 0, 0)
        attn_unit(0, 0)
        serve_z(0, 1, 2, 3)
        serve_g(0, 1, 2)
        attn_unit(0, 1)
        serve_z(1, 1, 2)
        attn_unit(0, 2)
        serve_g(0, 3)
        serve_z(1, 3)
        attn_unit(0, 3)
        serve_g(1, 1, 2)
        add_branch(0, 2, 1)
        x_out(1).start()
        lifted(0, 3, 1)
        up_unit(0, 0)
        serve_z(2, 1, 2)
        up_unit(0, 1)
        up_unit(0, 2)
        serve_g(1, 3)
        serve_z(2, 3)
        up_unit(0, 3)
        down_unit(0, 0)
        serve_g(2, 1, 2)
        down_unit(0, 1)
        down_unit(0, 2)
        serve_z(3, 1, 2)
        serve_g(2, 3)
        down_unit(0, 3)
        serve_z(3, 3)
        x_out(0).wait()

        @pl.when(is_main)
        def _():
            for index in range(4):
                pass_on(t_v, ts, tr, index).wait_send()

        for span in chunks():
            value = branch_rows(0, 5, 2, span)
            high = value.astype(bf16)
            rest = value - high.astype(f32)
            middle = rest.astype(bf16)
            t_v[span, :] = high
            t_v[slice(ROWS + span.start, ROWS + span.stop), :] = middle
            u_s[span, :] = (rest - middle.astype(f32)).astype(bf16)
        for span in chunks():
            move = one_hot(pos_s[2, span, :], counted((CHUNK, ROWS), 1))
            x_v[0, span, :] = (
                mm(move, t_v[:ROWS, :], 1, 0) + mm(move, t_v[ROWS:, :], 1, 0) + mm(move, u_s[...], 1, 0)
            )
        x_out(2).start()
        lifted(1, 0, 2)
        qo_out(0, 2).wait()
        qo_out(0, 3).wait()
        attn_unit(1, 0)
        serve_g(3, 1, 2)
        serve_z(4, 1, 2)
        attn_unit(1, 1)
        serve_g(3, 3)
        attn_unit(1, 2)
        serve_z(4, 3)
        attn_unit(1, 3)
        serve_g(4, 1, 2)
        add_branch(1, 2, 3)
        x_out(3).start()
        lifted(1, 3, 3)
        serve_g(4, 3)
        up_unit(1, 3)
        collect(1)
        for span in chunks():
            grad = mm(one_hot(pos_s[1, span, :], counted((CHUNK, CAP), 1)), c_v[...], 1, 0)
            g_o[span, :] = grad
            d_t[:, span] = (row_mod(hot_o[span, :], tab_o, 1, 5) * grad).T.astype(bf16)
        early_unit(0)
        for copy in exchange(0):
            copy.start()
        serve_z(5, 1, 2)
        up_unit(1, 2)
        finish(0)
        early_unit(1)
        for copy in exchange(1):
            copy.start()
        up_unit(1, 1)
        serve_z(5, 3)
        finish(1)
        early_unit(2)
        for copy in exchange(2):
            copy.start()
        up_unit(1, 0)
        finish(2)
        down_unit(1, 0)
        serve_g(5, 1, 2)
        down_unit(1, 1)
        down_unit(1, 2)
        serve_g(5, 3)
        down_unit(1, 3)
        for span in chunks():
            u_s[span, :] = branch_rows(1, 5, 4, span).astype(bf16)

        @pl.when(is_main)
        def _():
            for index in range(4):
                pass_on(c_v, cs, cr, index).wait_send()

        for at in range(0, CAP, 256):
            place = one_hot(counted((256, ROWS), 0, at), pos_o[1])
            c_v[at : at + 256, :] = mm(place, u_s[...], 1, 0).astype(bf16)

        @pl.when(is_second)
        def _():
            rows_copy().start()

        @pl.when(is_main)
        def _():
            rows_copy().wait_recv()
            for at in range(0, CAP, 256):
                c_v[at : at + 256, :] = c_v[at : at + 256, :] + t_v[at : at + 256, :]
            rows_out().start()

        early_arrival(1).wait_recv()
        for turn in range(3):
            to_owner(turn).wait_send()
        x_out(2).wait()
        x_out(3).wait()
        for slot in (2, 3):
            qo_out(1, slot).wait()
        for slot in range(4):
            ad_out(1, slot).wait()
        for k in range(count):
            for copy in own_copies(k):
                copy.wait_send()
            for slot in range(4):
                w_out(k, slot).wait()
            for slot in (1, 2, 3):
                g_copy(k, slot).wait_send()
                for mine in (True, False):
                    for copy in d_copies(k, slot, mine):
                        copy.wait_send()
        for k in range(count):
            z_copy(k, 2, at_mp(other_mid)).wait_send()

    @pl.when(is_main)
    def _():
        for copy in meta_copies():
            copy.wait_send()
        rows_out().wait()

    @pl.when(is_second)
    def _():
        rows_copy().wait_send()
        route(tok, t_v, ts, tr).wait_send()
        route(cot, c_v, cs, cr).wait_send()


def run_forward(tok, cot, mod, small, par):
    sds = jax.ShapeDtypeStruct
    n_dp = lax.axis_size("dp")
    rows, cols = par.shape[1], par.shape[2]
    count = L * cols // PIECE
    peers = n_dp - 1
    return pl.pallas_call(
        partial(fwd_kernel, n_dp),
        out_shape=(
            sds((count, 4, D, PIECE), bf16), sds((2 * L, ROWS, D), f32), sds((L, 4, ROWS, D), bf16),
            sds((L, 4, 2, ROWS, FF // 4), bf16), sds((2, rows, PIECE), bf16), sds((CAP, D), bf16),
            sds((L, HEADS, 1, ROWS), f32), sds((ROWS, D), f32), sds((ROWS, 4 * SLOTS), bf16), sds((L, ROWS, 1), f32), sds((L, 1, ROWS), f32),
            sds((3, 1, ROWS), f32), sds((6 * L, 4 * SLOTS, D), bf16),
        ),
        in_specs=[any_spec(), any_spec(), vm_spec(), vm_spec(), any_spec()],
        out_specs=(any_spec(),) * 6 + (vm_spec(),) * 7,
        scratch_shapes=[
            VM((count, 4, D, PIECE), bf16), VM((count, rows, PIECE), bf16), VM((2, rows, PIECE), f32),
            VM((CAP, D), bf16), VM((CAP, D), bf16), VM((2, ROWS, D), f32), VM((ROWS, D), bf16),
            VM((ROWS, D), f32), VM((2, ROWS, D), bf16), VM((4, 2, ROWS, FF // 4), bf16), VM((8, 128), f32), VM(mod.shape, f32),
            VM((3, ROWS, 1), f32), VM((D, ROWS), bf16), VM((2, D, PIECE), bf16),
            VM((2, peers, rows, PIECE), bf16), VM((3, rows, PIECE), bf16),
            DMA((count, 3)), DMA((count, 3)), DMA((count, 3)), DMA((count, 3)),
            DMA((count, 3, 2, peers)), DMA((count, 3, 2, peers)), DMA((count, peers)), DMA((count, peers)),
            DMA((5,)), DMA((8,)), DMA((5,)), DMA((8,)), DMA((2,)), DMA((2,)), DMA((2,)),
            DMA((2,)), DMA((count, 4)), DMA((2 * L,)), DMA((2,)), DMA((4,)),
            DMA((3, peers)), DMA((3, peers)), DMA((3,)), DMA((2,)), DMA((1,)), DMA((1,)), DMA((1,)),
        ],
        compiler_params=pltpu.CompilerParams(
            collective_id=1, has_side_effects=True, vmem_limit_bytes=63 * MIB
        ),
    )(tok, cot, mod, small, par)


def share_rows(rows, n_grp):
    part = rows // n_grp
    return part if part * n_grp == rows and part % 16 == 0 else rows


def back_kernel(
    n_dp, n_grp,
    pos_r, g_in, hot, idc, idr, tables, lse, xs, qo, ad, early, rows_in,
    w_hbm, par, mom, var,
    recv, avg, mix_o, gin_o,
    g_s, x_b, w_b, a_b, q_b, u_t, d_s, d_t, dh, dq, do_s, dk_s, acc, out, inbox, stage,
    p_b, p_in, opt, gsum, diff, box, own_avg,
    xsem, wsem, asem, ce_s, ce_r, os_s, os_r, loc, pe_s, pe_r, ro_s, ro_r, rl, osem,
    as_s, as_r, bs_s, bs_r, bl, esem,
):
    grp, dp, mp = lax.axis_index("grp"), lax.axis_index("dp"), lax.axis_index("mp")
    rows, cols = par.shape[1], par.shape[2]
    quarter = mix_o.shape[0]
    share = share_rows(rows, n_grp)
    star = 1 + lax.rem(dp, 2)
    is_mid = jnp.logical_or(mp == 1, mp == 2)
    is_outer = jnp.logical_not(is_mid)
    is_main = mp == star
    is_second = jnp.logical_and(is_mid, mp != star)
    other_mid = 3 - mp
    near_outer = jnp.where(mp == 1, 0, 3)
    far_outer = 3 - near_outer
    heads = HEADS_DEV
    hw = HW
    mate = (grp, flip(dp, 1), mp)

    def at_mp(where):
        return (grp, dp, where)

    def at_grp(step):
        return (lax.rem(grp + step, n_grp), dp, mp)

    def at_dp(step):
        return (grp, lax.rem(dp + step, n_dp), mp)

    peers = [at_grp(step) for step in range(1, n_grp)]

    @pl.when(is_mid)
    def _():
        greet(
            [at_mp(0), at_mp(3), at_mp(other_mid)] + peers + [at_dp(step) for step in range(1, n_dp)]
        )

    @pl.when(is_outer)
    def _():
        greet([at_mp(1), at_mp(2)] + peers)

    def layer_of(sub):
        return 1 - sub // 2

    def slot_of(step):
        return 3 - step % 4

    units = []
    for sub in range(4):
        steps = range(4 * sub, 4 * sub + 4)
        if sub % 2:
            units += [(step, "attn") for step in steps]
        else:
            units += [(step, kind) for step in steps for kind in ("down", "up")]
    units = [unit for unit in units if unit not in ((0, "down"), (1, "down"), (2, "down"))]

    def piece_of(unit):
        step, kind = units[unit]
        return layer_of(step // 4), {"attn": 0, "up": PIECE, "down": 2 * PIECE}[kind]

    def index_of(piece):
        return piece[0] * (cols // PIECE) + piece[1] // PIECE

    def halves(piece):
        return [(0, 384), (384, 640), (640, PIECE)] if piece == (0, 0) else [(0, PIECE)]

    def weight_loads(step):
        sub, slot, place = step // 4, slot_of(step), step % 2
        first = layer_of(sub) * (cols // PIECE) + (1 if sub % 2 == 0 else 0)
        return [
            pltpu.make_async_copy(
                w_hbm.at[first + turn, slot], w_b.at[place, :, turn * D : turn * D + D], wsem.at[place, turn]
            )
            for turn in range(2 if sub % 2 == 0 else 1)
        ]

    def kept_load(step):
        sub, slot, place = step // 4, slot_of(step), step % 2
        layer = layer_of(sub)
        if sub % 2 == 0:
            return pltpu.make_async_copy(ad.at[layer, slot], a_b.at[place], asem.at[place])
        return pltpu.make_async_copy(qo.at[layer, slot], q_b.at[place], asem.at[place])

    def load(step):
        for copy in (kept_load(step), *weight_loads(step)):
            copy.start()

    def x_load(sub):
        source = xs.at[2 * layer_of(sub) + (1 if sub % 2 == 0 else 0)]
        return pltpu.make_async_copy(source, x_b.at[sub % 2], xsem.at[sub % 2])

    def exchange(unit):
        place = unit % 2
        result = []
        for hop in range(1, n_dp):
            target = lax.rem(dp + hop, n_dp)
            result.append(
                remote(
                    out.at[place, pl.ds(pl.multiple_of(target * rows, rows), rows)],
                    inbox.at[place, hop - 1],
                    ce_s.at[unit, hop - 1], ce_r.at[unit, hop - 1], at_dp(hop),
                )
            )
        return result

    def to_owner(unit, turns=(0, 1, 2)):
        piece, slot = piece_of(unit), slot_of(units[unit][0])
        plane, index = (1 if slot >= 2 else 0), index_of(piece)
        result = []
        for turn, (low, high) in enumerate(halves(piece)):
            if turn not in turns:
                continue
            source = stage.at[unit, :, low:high]
            place = recv.at[plane, piece[0], :, piece[1] + low : piece[1] + high]
            if slot == 0:
                result.append(pltpu.make_async_copy(source, place, loc.at[index, turn]))
            else:
                device = at_mp((None, near_outer, other_mid, far_outer)[slot])
                result.append(
                    remote(source, place, os_s.at[unit, turn], os_r.at[index, plane, turn], device)
                )
        return result

    def owner_arrival(piece, plane, turn):
        low, high = halves(piece)[turn]
        place = recv.at[plane, piece[0], :, piece[1] + low : piece[1] + high]
        return remote(place, place, os_s.at[0, 0], os_r.at[index_of(piece), plane, turn], mate)

    early_piece = (L - 1, 2 * PIECE)

    def early_copy(plane):
        place = recv.at[plane, early_piece[0], :, early_piece[1] : early_piece[1] + PIECE]
        return pltpu.make_async_copy(early.at[plane], place, esem.at[plane])

    def finish(unit):
        place = unit % 2
        for copy in exchange(unit):
            copy.wait_recv()
        block = 96 if rows % 96 == 0 else rows
        for at in range(0, rows, block):
            mine = pl.ds(pl.multiple_of(dp * rows + at, 16), block)
            total = out[place, mine, :].astype(f32)
            for hop in range(1, n_dp):
                total = total + inbox[place, hop - 1, at : at + block, :].astype(f32)
            stage[unit, at : at + block, :] = total.astype(bf16)
        for copy in exchange(unit):
            copy.wait_send()
        for copy in to_owner(unit):
            copy.start()

    def put_rows(values):
        for at in range(0, CAP, 256):
            place = one_hot(counted((256, ROWS), 0, at), pos_r[0])
            p_b[at : at + 256, :] = mm(place, values, 1, 0).astype(bf16)

        @pl.when(is_second)
        def _():
            remote(p_b, p_in, pe_s.at[0], pe_r.at[0], mate).start()

    def quarter_of(index):
        return pl.ds(pl.multiple_of(index * quarter, quarter), quarter)

    def row_copies(which):
        source, dest = ((rows_in, mix_o), (p_b, gin_o))[which]
        return [
            remote(
                source.at[quarter_of(index)], dest, ro_s.at[which, turn], ro_r.at[which], at_mp(index)
            )
            for turn, index in enumerate((other_mid, 0, 3))
        ]

    def row_keep(which):
        source, dest = ((rows_in, mix_o), (p_b, gin_o))[which]
        return pltpu.make_async_copy(source.at[quarter_of(mp)], dest, rl.at[which])

    def send_rows(which):
        @pl.when(is_main)
        def _():
            if which == 1:
                remote(p_b, p_in, pe_s.at[0], pe_r.at[0], mate).wait_recv()
                for at in range(0, CAP, 256):
                    span = slice(at, at + 256)
                    p_b[span, :] = p_b[span, :] + p_in[span, :]
            for copy in row_copies(which):
                copy.start()
            row_keep(which).start()

    def end_rows():
        @pl.when(is_main)
        def _():
            for which in range(2):
                for copy in row_copies(which):
                    copy.wait_send()
                row_keep(which).wait()

        @pl.when(is_second)
        def _():
            remote(p_b, p_in, pe_s.at[0], pe_r.at[0], mate).wait_send()

    def rows_arrived(which, dest):
        @pl.when(jnp.logical_not(is_main))
        def _():
            remote(
                dest, dest, ro_s.at[which, 0], ro_r.at[which], at_mp(0)
            ).wait_recv()

    def diff_piece(piece, turn):
        layer, index = piece[0], index_of(piece)
        low, high = halves(piece)[turn]
        width = high - low
        span = slice(piece[1] + low, piece[1] + high)
        block = opt.shape[2]

        def opt_loads(lap):
            part, place = slice(lap * block, (lap + 1) * block), lap % 2
            return [
                pltpu.make_async_copy(
                    source.at[layer, part, span], opt.at[place, i, :, :width], osem.at[place, i]
                )
                for i, source in enumerate((par, mom, var))
            ] + [
                pltpu.make_async_copy(
                    recv.at[plane, layer, part, span], gsum.at[place, plane, :, :width],
                    osem.at[place, 3 + plane],
                )
                for plane in range(2)
            ]

        @pl.when(is_outer)
        def _():
            if piece == early_piece:
                early_copy(0).wait()
            else:
                owner_arrival(piece, 0, turn).wait_recv()

        @pl.when(is_mid)
        def _():
            own = [u for u in range(len(units)) if piece_of(u) == piece and slot_of(units[u][0]) == 0][0]
            to_owner(own, (turn,))[0].wait()

        if piece == early_piece:
            early_copy(1).wait()
        else:
            owner_arrival(piece, 1, turn).wait_recv()
        for copy in opt_loads(0):
            copy.start()
        for lap in range(rows // block):
            part, place = slice(lap * block, (lap + 1) * block), lap % 2
            if (lap + 1) * block < rows:
                for copy in opt_loads(lap + 1):
                    copy.start()
            for copy in opt_loads(lap):
                copy.wait()
            grad = gsum[place, 0, :, :width].astype(f32) + gsum[place, 1, :, :width].astype(f32)
            one = beta_one * opt[place, 1, :, :width] + (1 - beta_one) * grad
            two = beta_two * opt[place, 2, :, :width] + (1 - beta_two) * grad * grad
            step = one / (1 - beta_one**STEP) / (jnp.sqrt(two / (1 - beta_two**STEP)) + adam_eps)
            diff[index, part, low:high] = (
                inner_rate * (step + decay_rate * opt[place, 0, :, :width])
            ).astype(bf16)
        for copy in first_copies(piece, turn):
            copy.start()

    def rows_for(where):
        if share == rows:
            return slice(0, rows)
        return pl.ds(pl.multiple_of(where * share, share), share)

    def first_copies(piece, turn):
        index = index_of(piece)
        low, high = halves(piece)[turn]
        return [
            remote(
                diff.at[index, rows_for(lax.rem(grp + hop, n_grp)), low:high],
                box.at[index, hop - 1, :, low:high],
                as_s.at[index, turn, hop - 1], as_r.at[index, turn, hop - 1], at_grp(hop),
            )
            for hop in range(1, n_grp)
        ]

    def second_copies(piece, turn):
        index = index_of(piece)
        low, high = halves(piece)[turn]
        place = avg.at[piece[0], rows_for(grp), piece[1] + low : piece[1] + high]
        return [
            remote(
                own_avg.at[index, :, low:high], place,
                bs_s.at[index, turn, hop - 1], bs_r.at[index, turn, hop - 1], at_grp(hop),
            )
            for hop in range(1, n_grp)
        ]

    def second_arrivals(piece, turn):
        index = index_of(piece)
        low, high = halves(piece)[turn]
        result = []
        for hop in range(1, n_grp):
            source = lax.rem(grp + n_grp - hop, n_grp)
            place = avg.at[piece[0], rows_for(source), piece[1] + low : piece[1] + high]
            result.append(
                remote(
                    place, place, bs_s.at[index, turn, hop - 1], bs_r.at[index, turn, hop - 1], at_grp(hop)
                )
            )
        return result

    def own_copy(piece, turn):
        index = index_of(piece)
        low, high = halves(piece)[turn]
        place = avg.at[piece[0], rows_for(grp), piece[1] + low : piece[1] + high]
        return pltpu.make_async_copy(own_avg.at[index, :, low:high], place, bl.at[index, turn])

    def mean_piece(piece, turn):
        index = index_of(piece)
        low, high = halves(piece)[turn]
        for copy in first_copies(piece, turn):
            copy.wait_recv()
        total = diff[index, rows_for(grp), low:high].astype(f32)
        for hop in range(1, n_grp):
            total = total + box[index, hop - 1, :, low:high].astype(f32)
        own_avg[index, :, low:high] = (total / n_grp).astype(bf16)
        own_copy(piece, turn).start()
        if share != rows:
            for copy in second_copies(piece, turn):
                copy.start()

    def end_piece(piece, turn):
        for copy in first_copies(piece, turn):
            copy.wait_send()
        own_copy(piece, turn).wait()
        if share != rows:
            for copy in second_copies(piece, turn):
                copy.wait_send()
            for copy in second_arrivals(piece, turn):
                copy.wait_recv()

    def down_start(sub):
        layer = layer_of(sub)
        for part in chunks():
            down = row_mod(hot[part, :], tables, layer, 5) * g_s[part, :]
            d_s[part, :] = down.astype(bf16)
            d_t[:, part] = down.T.astype(bf16)

    def up_start(sub):
        layer, place = layer_of(sub), sub % 2
        x_load(sub).wait()
        for part in chunks():
            normed, _ = moments(x_b[place, part, :])
            shift = row_mod(hot[part, :], tables, layer, 3)
            scale = row_mod(hot[part, :], tables, layer, 4)
            u_t[:, part] = (normed * (1.0 + scale) + shift).T.astype(bf16)
        acc[...] = jnp.zeros_like(acc)

    def down_unit(step, turn):
        out[turn] = mm(d_t[...], a_b[step % 2, 0], 1, 0).astype(bf16)

    def up_unit(step, turn):
        place = step % 2
        for part in chunks():
            dact = mm(d_s[part, :], w_b[place, :, D:], 1, 0)
            dh[part, :] = (dact * a_b[place, 1, part, :].astype(f32)).astype(bf16)
        out[turn] = mm(u_t[...], dh[...], 1, 0).astype(bf16)
        acc[...] += mm(dh[...], w_b[place, :, :D], 1, 1)

    def attn_start(sub):
        layer, place = layer_of(sub), sub % 2
        x_load(sub).wait()
        for part in chunks():
            normed, _ = moments(x_b[place, part, :])
            shift = row_mod(hot[part, :], tables, layer, 0)
            scale = row_mod(hot[part, :], tables, layer, 1)
            u_t[:, part] = (normed * (1.0 + scale) + shift).T.astype(bf16)
            branch = row_mod(hot[part, :], tables, layer, 2) * g_s[part, :]
            d_s[part, :] = branch.astype(bf16)
            d_t[:, part] = branch.T.astype(bf16)
        acc[...] = jnp.zeros_like(acc)

    def attn_unit(step, turn):
        layer, place, slot = layer_of(step // 4), step % 2, slot_of(step)
        out[turn, :, 3 * hw : D] = mm(d_t[...], q_b[place, :, 3 * hw :], 1, 0).astype(bf16)
        do_s[...] = mm(d_s[...], w_b[place, :, 3 * hw : D], 1, 0).astype(bf16)
        for head in range(heads):
            base = head * HD
            dk_s[...] = jnp.zeros_like(dk_s)
            for span, near_by in bands(layer):
                query = q_b[place, span, base : base + HD]
                keys = q_b[place, near_by, hw + base : hw + base + HD]
                values = q_b[place, near_by, 2 * hw + base : 2 * hw + base + HD]
                grad = do_s[span, base : base + HD]
                scores = mm(keys, query * jnp.asarray(0.125, bf16), 1, 1)
                allowed = idc[layer, near_by, :] == idr[layer, :, span]
                probs = jnp.where(
                    allowed, jnp.exp(scores - lse[layer, slot * heads + head, :, span]), 0.0
                )
                dk_s[1, near_by, :] += mm(probs.astype(bf16), grad, 1, 0)
                weighted = probs * mm(values, grad, 1, 1)
                delta = jnp.sum(weighted, axis=0, keepdims=True)
                ds = (weighted - probs * delta).astype(bf16)
                dq[span, base : base + HD] = (mm(keys, ds, 0, 0).T * 0.125).astype(bf16)
                dk_s[0, near_by, :] += mm(ds, query, 1, 0)
            dq[:, hw + base : hw + base + HD] = (dk_s[0] * 0.125).astype(bf16)
            dq[:, 2 * hw + base : 2 * hw + base + HD] = dk_s[1].astype(bf16)
        out[turn, :, : 3 * hw] = mm(u_t[...], dq[...], 1, 0).astype(bf16)
        acc[...] += mm(dq[...], w_b[place, :, : 3 * hw], 1, 1)

    def sub_end(sub):
        layer, place = layer_of(sub), sub % 2
        row = 4 if sub % 2 == 0 else 1
        for part in chunks():
            normed, inv_std = moments(x_b[place, part, :])
            scale = row_mod(hot[part, :], tables, layer, row)
            g_s[part, :] = g_s[part, :] + norm_back(acc[part, :] * (1.0 + scale), normed, inv_std)

    def to_frame_order():
        for part in chunks():
            high = g_s[part, :].astype(bf16)
            dh[part, :] = high
            d_s[part, :] = (g_s[part, :] - high.astype(f32)).astype(bf16)
        for part in chunks():
            move = one_hot(counted((CHUNK, ROWS), 0, part.start), pos_r[2])
            g_s[part, :] = mm(move, dh[...], 1, 0) + mm(move, d_s[...], 1, 0)

    def chunk(sub, kind):
        return layer_of(sub), {"attn": 0, "up": PIECE, "down": 2 * PIECE}[kind]

    order = [chunk(0, "down"), chunk(0, "up"), chunk(1, "attn"), chunk(2, "down"), chunk(2, "up"), chunk(3, "attn")]
    served = {7: (diff_piece, 0), 9: (mean_piece, 0), 14: (diff_piece, 1), 17: (mean_piece, 1)}

    early_copy(1).start()
    pl.when(is_outer)(lambda: early_copy(0).start())

    @pl.when(is_mid)
    def _():
        x_load(0).start()
        send_rows(0)
        load(0)
        load(1)
        g_s[...] = g_in[...]
        for unit, (step, kind) in enumerate(units):
            sub = step // 4
            first_of_sub = unit == 0 or units[unit - 1][0] // 4 != sub
            last_of_step = unit + 1 == len(units) or step not in [s for s, _ in units[unit + 1 :]]
            last_of_sub = unit + 1 == len(units) or units[unit + 1][0] // 4 != sub
            if first_of_sub:
                if sub < 3:
                    x_load(sub + 1).start()
                (attn_start if kind == "attn" else down_start)(sub)
            if unit == 0 or units[unit - 1][0] != step:
                kept_load(step).wait()
            if kind != "down":
                if kind == "up" and step % 4 == 0:
                    up_start(sub)
                for copy in weight_loads(step):
                    copy.wait()
            {"attn": attn_unit, "up": up_unit, "down": down_unit}[kind](step, unit % 2)
            if unit > 0:
                finish(unit - 1)
            for copy in exchange(unit):
                copy.start()
            if last_of_step and step + 2 < 16:
                load(step + 2)
            if last_of_sub:
                sub_end(sub)
                if sub == 1:
                    to_frame_order()
            if unit in served:
                action, which = served[unit]
                action(order[which], 0)
        put_rows(g_s[...].astype(bf16))
        finish(len(units) - 1)
        send_rows(1)
        for piece in order[2:5]:
            diff_piece(piece, 0)
            mean_piece(piece, 0)
        for turn in range(3):
            diff_piece(order[5], turn)
            if turn > 0:
                mean_piece(order[5], turn - 1)
        mean_piece(order[5], 2)
        for unit, (step, _) in enumerate(units):
            if slot_of(step) != 0:
                for copy in to_owner(unit):
                    copy.wait_send()
        end_rows()

    @pl.when(is_outer)
    def _():
        for piece in order[:5]:
            diff_piece(piece, 0)
            mean_piece(piece, 0)
        for turn in range(3):
            diff_piece(order[5], turn)
            if turn > 0:
                mean_piece(order[5], turn - 1)
        mean_piece(order[5], 2)

    for which, dest in ((0, mix_o), (1, gin_o)):
        rows_arrived(which, dest)
    for piece in order:
        for turn in range(len(halves(piece))):
            end_piece(piece, turn)


def run_back(pos, g, hot, idc, idr, tables, lse, xs, qo, ad, early, rows_in, w, par, mom, var, quarter):
    sds = jax.ShapeDtypeStruct
    n_dp, n_grp = lax.axis_size("dp"), lax.axis_size("grp")
    rows, cols = par.shape[1], par.shape[2]
    share = share_rows(rows, n_grp)
    count = L * cols // PIECE
    far, peers = n_dp - 1, n_grp - 1
    block = 96 if rows % 96 == 0 else rows
    return pl.pallas_call(
        partial(back_kernel, n_dp, n_grp),
        out_shape=(
            sds((2, L, rows, cols), bf16), sds((L, rows, cols), bf16),
            sds((quarter, D), bf16), sds((quarter, D), bf16),
        ),
        in_specs=[vm_spec()] * 7 + [any_spec()] * 9,
        out_specs=(any_spec(),) * 4,
        scratch_shapes=[
            VM((ROWS, D), f32), VM((2, ROWS, D), f32), VM((2, D, 2 * D), bf16),
            VM((2, 2, ROWS, D), bf16), VM((2, ROWS, D), bf16),
            VM((D, ROWS), bf16), VM((ROWS, D), bf16), VM((D, ROWS), bf16), VM((ROWS, D), bf16),
            VM((ROWS, 9 * HD), bf16), VM((ROWS, 3 * HD), bf16), VM((2, ROWS, HD), f32), VM((ROWS, D), f32),
            VM((2, D, PIECE), bf16), VM((2, far, rows, PIECE), bf16), VM((4 * count, rows, PIECE), bf16),
            VM((CAP, D), bf16), VM((CAP, D), bf16),
            VM((2, 3, block, PIECE), f32), VM((2, 2, block, PIECE), bf16),
            VM((count, rows, PIECE), bf16), VM((count, peers, share, PIECE), bf16),
            VM((count, share, PIECE), bf16),
            DMA((2,)), DMA((2, 2)), DMA((2,)), DMA((4 * count, far)), DMA((4 * count, far)),
            DMA((4 * count, 3)), DMA((count, 2, 3)), DMA((count, 3)),
            DMA((2,)), DMA((2,)), DMA((2, 3)), DMA((2,)), DMA((2,)), DMA((2, 5)),
            DMA((count, 3, peers)), DMA((count, 3, peers)), DMA((count, 3, peers)), DMA((count, 3, peers)),
            DMA((count, 3)), DMA((2,)),
        ],
        compiler_params=pltpu.CompilerParams(
            collective_id=2, has_side_effects=True, vmem_limit_bytes=63 * MIB
        ),
    )(pos, g, hot, idc, idr, tables, lse, xs, qo, ad, early, rows_in, w, par, mom, var)


def last_kernel(
    par, mom, var, out_mom, ga, gb, avg, rows_m, rows_g, tok, frames, patches,
    new_m, new_v, out_a, out_m, out_w, out_l, mixed, grad_in,
):
    @pl.when(jnp.logical_and(pl.program_id(0) == 0, pl.program_id(1) == 0))
    def _():
        total = frames[:, 0:1] * patches[:, 0:1]
        for clip in range(1, SLOTS):
            total = total + frames[:, clip : clip + 1] * patches[:, clip : clip + 1]
        first = lax.axis_index("mp") * tok.shape[0]
        live = first + lax.broadcasted_iota(jnp.int32, (tok.shape[0], 1), 0) < total
        mixed[...] = jnp.where(live, rows_m[...].astype(f32), tok[...].astype(f32)).astype(bf16)
        grad_in[...] = jnp.where(live, rows_g[...].astype(f32), 0.0)

    grad = ga[...].astype(f32) + gb[...].astype(f32)
    new_m[...] = beta_one * mom[...] + (1 - beta_one) * grad
    new_v[...] = beta_two * var[...] + (1 - beta_two) * grad * grad
    average = avg[...].astype(f32)
    momentum = outer_mu * out_mom[...] + average
    updated = par[...] - outer_rate * (average + outer_mu * momentum)
    out_a[...] = average
    out_m[...] = momentum
    out_w[...] = updated
    out_l[...] = updated.astype(bf16)


def run_last(par, mom, var, out_mom, recv, avg, rows_m, rows_g, tok, frames, patches):
    rows, cols = par.shape[1], par.shape[2]
    block = 96 if rows % 96 == 0 else rows
    sds = jax.ShapeDtypeStruct
    full = pl.BlockSpec((None, block, cols), lambda i, j: (i, j, 0))

    def plane(which):
        return pl.BlockSpec((None, None, block, cols), lambda i, j: (which, i, j, 0))

    return pl.pallas_call(
        last_kernel,
        grid=(L, rows // block),
        out_shape=(sds(par.shape, f32),) * 5 + (sds(par.shape, bf16), sds(tok.shape, bf16), sds(tok.shape, f32)),
        in_specs=[full] * 4 + [plane(0), plane(1), full] + [vm_spec()] * 5,
        out_specs=(full,) * 6 + (vm_spec(),) * 2,
        compiler_params=pltpu.CompilerParams(vmem_limit_bytes=62 * MIB),
    )(par, mom, var, out_mom, recv, recv, avg, rows_m, rows_g, tok, frames, patches)


def body(
    tokens, cotangent, modulation, clip_frames, clip_patches, params, first_moment, second_moment,
    outer_momentum,
):
    quarter = tokens.shape[1]
    small = jnp.concatenate([clip_frames, clip_patches], axis=0).astype(f32)
    small = jnp.pad(small, ((0, 6), (0, 128 - SLOTS)))
    w, xs, qo, ad, early, rows_in, lse, gradient, hot, idc, idr, pos, tables = run_forward(
        tokens[0], cotangent[0], modulation[0], small, params
    )
    recv, avg, mixed_rows, grad_rows = run_back(
        pos, gradient, hot, idc, idr, tables, lse, xs, qo, ad, early, rows_in, w,
        params, first_moment[0], second_moment[0], quarter,
    )
    new_m, new_v, average, momentum, updated, low, mixed, input_grad = run_last(
        params, first_moment[0], second_moment[0], outer_momentum, recv, avg,
        mixed_rows, grad_rows, tokens[0], clip_frames, clip_patches,
    )
    return (
        mixed[None], input_grad[None], new_m[None], new_v[None], average, momentum, updated, low,
    )


def solution(mesh):
    in_specs = (
        P("grp", ("dp", "mp"), None),
        P("grp", ("dp", "mp"), None),
        P("grp", "dp", None),
        P("grp", "dp"),
        P("grp", "dp"),
        P(None, "dp", "mp"),
        P("grp", None, "dp", "mp"),
        P("grp", None, "dp", "mp"),
        P(None, "dp", "mp"),
    )
    out_specs = (
        P("grp", ("dp", "mp"), None),
        P("grp", ("dp", "mp"), None),
        P("grp", None, "dp", "mp"),
        P("grp", None, "dp", "mp"),
        P(None, "dp", "mp"),
        P(None, "dp", "mp"),
        P(None, "dp", "mp"),
        P(None, "dp", "mp"),
    )
    return jax.shard_map(body, mesh=mesh, in_specs=in_specs, out_specs=out_specs, check_vma=False)
```
